32 devices in a mesh: wide: 4 (over y, core), narrow: 8 (over z, x).
Axes of the slice: x: 2, y: 2, z: 4, core: 2. Of those that a mesh axis runs over, the one named last changes fastest.
Arguments:
- tokens: bfloat16 [16384, 1280], P(('wide', 'narrow')), may hold values from -6 to 6
- lengths: int32 [8, 4], P('wide'), may hold values from 1 to 1280, 1920 in all within a row
- qkv_weight: bfloat16 [3, 1280, 1280], P(None, 'wide', 'narrow'), may hold values from -0.15625 to 0.15625
- out_weight: bfloat16 [1280, 1280], P('narrow', 'wide'), may hold values from -0.625 to 0.625
- up_weight: bfloat16 [1280, 1280], P('wide', 'narrow'), may hold values from -0.15625 to 0.15625
- up_bias: bfloat16 [1280], P('narrow'), may hold values from -3 to 3
- down_weight: bfloat16 [1280, 1280], P('narrow', 'wide'), may hold values from -0.15625 to 0.15625
- down_bias: bfloat16 [1280], replicated, may hold values from -3 to 3
- attn_gain: float32 [1280], replicated, may hold values from 0.5 to 1.5
- mlp_gain: float32 [1280], replicated, may hold values from 0.5 to 1.5
- query_scale: float32 [80], replicated, may hold values from 0 to 1.5
- cotangent: bfloat16 [16384, 1280], P(('wide', 'narrow')), may hold values from -6 to 6
Outputs:
- result: bfloat16 [16384, 1280], P(('wide', 'narrow'))
- tokens_grad: float32 [16384, 1280], P(('wide', 'narrow'))
- qkv_grad: float32 [3, 1280, 1280], P(None, 'wide', 'narrow')
- out_grad: float32 [1280, 1280], P('narrow', 'wide')
- up_grad: float32 [1280, 1280], P('wide', 'narrow')
- up_bias_grad: float32 [1280], P('narrow')
- down_grad: float32 [1280, 1280], P('narrow', 'wide')
- down_bias_grad: float32 [1280], replicated
- attn_gain_grad: float32 [1280], replicated
- mlp_gain_grad: float32 [1280], replicated
- query_scale_grad: float32 [80], replicated
The draws below stay inside these ranges and needn't reach their ends.
Inputs may be any that keep to these rules, and one draw needn't show every extreme that they name: Each row holds 4 document lengths that sum to 1920; the longest is exactly 1280; the last 128 tokens of every sequence are padding.
All inputs are finite; a program needn't handle non-finite values.
Results may differ from the reference program's by a relative error of at most 0.012.
The reference program's roundings to bfloat16 on the way count: a program that leaves them out, or rounds other values in their place, can miss the bound.
Values may be sent and summed in bfloat16 or wider, within the bound.
A program may use at most 320 MiB of HBM per device.

```python
import math
import jax
import jax.numpy as jnp
import numpy as np
from jax import lax

D = 1280
FF = 1280
HEADS = 16
HEAD_DIM = 80
LEN = 2048
WINDOW = 1024
BLOCK = 512
NDOC = 4
PAD = 128
MOST = 1280
SEQS = 8
TOKENS = 16384


def block_scale(own_key, extent, cuts, smallest, top_value):
    def one(position, parts):
        draws = jax.random.uniform(jax.random.fold_in(jax.random.fold_in(own_key, 6), position), (parts,), jnp.float32, smallest / len(cuts), top_value / len(cuts))
        return jnp.repeat(jnp.exp(draws), extent[position] // parts).reshape((-1,) + (1,) * (len(extent) - position - 1))

    loudness = one(*cuts[0])
    for cut in cuts[1:]:
        loudness = loudness * one(*cut)
    return loudness


def profile(count, total, limit, skew):
    portions = [(1 << 20) // math.isqrt(standing ** skew) + 1 for standing in range(2, count + 1)]
    spare, counts = total - limit - (count - 1), [1] * (count - 1)
    while spare > 0:
        candidates = [i for i in range(count - 1) if counts[i] < limit]
        mass, budget = sum([portions[i] for i in candidates]), spare
        for i in candidates:
            more = min(limit - counts[i], max(1, budget * portions[i] // mass), spare)
            counts[i] = counts[i] + more
            spare = spare - more
    return np.array([limit] + counts)


def ragged(key, amount, total, reach, skew):
    if amount == 2:
        one = jax.random.randint(key, (), max(1, total - reach), min(reach, total - 1) + 1)
        return jnp.stack([one, total - one])
    sizes = jnp.asarray(profile(amount, total, reach, skew), jnp.int32)
    pairs = (amount - 1) // 2
    giver, taker = sizes[1:1 + 2 * pairs:2], sizes[2:2 + 2 * pairs:2]
    room = jnp.minimum(giver - 1, reach - taker)
    moved = jax.random.randint(jax.random.fold_in(key, 1), (pairs,), 0, 1 << 20) % (room + 1)
    sizes = sizes.at[1:1 + 2 * pairs:2].set(giver - moved).at[2:2 + 2 * pairs:2].set(taker + moved)
    return sizes[jax.random.permutation(jax.random.fold_in(key, 2), amount)]


def normal_values(own_key, shape, spread, bound, pieces=(), held_as=jnp.bfloat16):
    result = spread * jax.random.normal(own_key, shape, jnp.float32)
    if pieces:
        result = result * block_scale(own_key, shape, pieces, -0.22, 0.18)
    return jnp.clip(result, -bound, bound).astype(held_as)


def setup_inputs(seed: int = 0) -> dict:
    keys = jax.random.split(jax.random.key(seed), 13)
    return {
        "tokens": normal_values(keys[0], (TOKENS, D), 1.0, 6.0, ((0, 32),)),
        "lengths": jax.vmap(lambda own: ragged(own, NDOC, LEN - PAD, MOST, 2))(jax.random.split(keys[1], SEQS)).reshape((SEQS, NDOC)).astype(jnp.int32),
        "qkv_weight": normal_values(keys[2], (3, D, D), D ** -0.5, 0.15625, ((1, 4), (2, 8))),
        "out_weight": normal_values(keys[3], (D, D), (D // 16) ** -0.5, 0.625, ((0, 8), (1, 4))),
        "up_weight": normal_values(keys[4], (D, FF), D ** -0.5, 0.15625, ((0, 4), (1, 8))),
        "up_bias": normal_values(keys[5], (FF,), 0.5, 3.0, ((0, 8),)),
        "down_weight": normal_values(keys[6], (FF, D), FF ** -0.5, 0.15625, ((0, 8), (1, 4))),
        "down_bias": normal_values(keys[7], (D,), 0.5, 3.0),
        "attn_gain": jnp.clip(1.0 + 0.1 * jax.random.normal(keys[8], (D,), jnp.float32), 0.5, 1.5),
        "mlp_gain": jnp.clip(1.0 + 0.1 * jax.random.normal(keys[9], (D,), jnp.float32), 0.5, 1.5),
        "query_scale": jnp.clip(jax.random.uniform(keys[10], (HEAD_DIM,), jnp.float32, 0.0, 1.5), 0.0, 1.5),
        "cotangent": normal_values(keys[11], (TOKENS, D), 1.0, 6.0, ((0, 32),)),
    }


LOG_TWO_E = 1.4426950408889634
EPSILON = 1e-06
NEG_FILL = -1e+30

@jax.custom_vjp
def low(v):
    return lax.optimization_barrier(v.astype(jnp.bfloat16)).astype(jnp.float32)

@jax.custom_vjp
def low_back(v):
    return v

def low_keep(v):
    return (low(v), None)

def low_pass(kept, grad):
    return (grad,)

def back_keep(v):
    return (v, None)

def back_low(kept, grad):
    return (low(grad),)
low.defvjp(low_keep, low_pass)
low_back.defvjp(back_keep, back_low)

def matmul(left, right):
    return jnp.dot(left, right, precision=lax.Precision.HIGHEST)

def rms_scale(values):
    return values * lax.rsqrt(lax.optimization_barrier(jnp.mean(values * values, axis=-1, keepdims=True)) + EPSILON)

def segment_ids(lengths_row):
    positions = jnp.arange(LEN, dtype=jnp.int32)
    ends = jnp.cumsum(lengths_row).astype(jnp.int32)
    return lax.optimization_barrier(jnp.sum((positions[:, None] >= ends[None, :]).astype(jnp.int32), axis=1)).astype(jnp.int32)

def block_mask(segments, padded_seg, offset):
    query_pos = (offset + jnp.arange(BLOCK, dtype=jnp.int32)).astype(jnp.int32)
    key_pos = (offset - WINDOW + jnp.arange(WINDOW + BLOCK, dtype=jnp.int32)).astype(jnp.int32)
    query_seg = lax.dynamic_slice_in_dim(segments, offset, BLOCK)
    key_seg = lax.dynamic_slice_in_dim(padded_seg, offset, WINDOW + BLOCK)
    spacing = query_pos[:, None] - key_pos[None, :]
    same_doc = query_seg[:, None] == key_seg[None, :]
    inside = (spacing >= 0) & (spacing < WINDOW)
    real_doc = (query_seg[:, None] < NDOC) | (spacing == 0)
    return same_doc & inside & real_doc

def attend_sequence(queries, keys_in, values_in, segments):
    pad_rows = jnp.zeros((WINDOW, HEADS, HEAD_DIM), jnp.float32)
    keys_pad = jnp.concatenate([pad_rows.astype(keys_in.dtype), keys_in], axis=0)
    values_pad = jnp.concatenate([pad_rows.astype(values_in.dtype), values_in], axis=0)
    padded_seg = jnp.concatenate([jnp.full((WINDOW,), -2, jnp.int32), segments.astype(jnp.int32)])

    @jax.checkpoint
    def one_block(block_index):
        offset = (block_index * BLOCK).astype(jnp.int32)
        query_block = lax.dynamic_slice_in_dim(queries, offset, BLOCK)
        key_block = lax.dynamic_slice_in_dim(keys_pad, offset, WINDOW + BLOCK)
        value_block = lax.dynamic_slice_in_dim(values_pad, offset, WINDOW + BLOCK)
        allowed = block_mask(segments, padded_seg, offset)
        scores = low_back(jnp.einsum('ihd,jhd->hij', query_block, key_block, precision=lax.Precision.HIGHEST))
        masked = jnp.where(allowed[None], scores, NEG_FILL)
        maxima = lax.optimization_barrier(jnp.max(masked, axis=2, keepdims=True))
        exponent = jnp.exp(masked - maxima)
        soft_probs = exponent / lax.optimization_barrier(jnp.sum(exponent, axis=2, keepdims=True))
        return jnp.einsum('hij,jhd->ihd', low(soft_probs), value_block, precision=lax.Precision.HIGHEST)
    blocks = lax.map(one_block, jnp.arange(LEN // BLOCK, dtype=jnp.int32))
    return blocks.reshape(LEN, HEADS, HEAD_DIM)

def layer(tokens, qkv_weight, out_weight, up_weight, up_bias, down_weight, down_bias, attn_gain, mlp_gain, query_scale, segments):
    normal_one = low(rms_scale(tokens) * attn_gain)
    query_heads = low_back(matmul(normal_one, qkv_weight[0]))
    key_low = low_back(low(matmul(normal_one, qkv_weight[1])))
    value_low = low_back(low(matmul(normal_one, qkv_weight[2])))
    scale_dim = LOG_TWO_E / math.sqrt(HEAD_DIM) * jax.nn.softplus(query_scale)
    query_low = low(query_heads.reshape(SEQS, LEN, HEADS, HEAD_DIM) * scale_dim)
    key_seq = key_low.reshape(SEQS, LEN, HEADS, HEAD_DIM)
    value_seq = value_low.reshape(SEQS, LEN, HEADS, HEAD_DIM)

    def per_sequence(packed):
        return attend_sequence(packed[0], packed[1], packed[2], packed[3])
    attended = lax.map(per_sequence, (query_low, key_seq, value_seq, segments))
    attended_rows = low_back(low(attended.reshape(TOKENS, D)))
    middle = tokens + low_back(matmul(attended_rows, out_weight))
    normal_two = low(rms_scale(middle) * mlp_gain)
    hidden_pre = low_back(matmul(normal_two, up_weight) + up_bias)
    hidden_low = low(jax.nn.silu(hidden_pre))
    return middle + low_back(matmul(hidden_low, down_weight) + down_bias)

def reference(tokens, lengths, qkv_weight, out_weight, up_weight, up_bias, down_weight, down_bias, attn_gain, mlp_gain, query_scale, cotangent):
    segments = jax.vmap(segment_ids)(lengths)
    floats = [item.astype(jnp.float32) for item in (tokens, qkv_weight, out_weight, up_weight, up_bias, down_weight, down_bias, attn_gain, mlp_gain, query_scale)]

    def forward(*params):
        return layer(*params, segments)
    output, pullback = jax.vjp(forward, *floats)
    grads = pullback(cotangent.astype(jnp.float32))
    return (output.astype(jnp.bfloat16), grads[0], grads[1], grads[2], grads[3], grads[4], grads[5], grads[6], grads[7], grads[8], grads[9])
```

```python
import functools
import math

import jax
import jax.numpy as jnp
from jax import lax
from jax.experimental import pallas as pl
from jax.experimental.pallas import tpu as pltpu
from jax.sharding import PartitionSpec as P

HEAD_DIM = 80
LEN = 2048
WINDOW = 1024
BLOCK = 512
NDOC = 4
TILE = 256

LOG_TWO_E = 1.4426950408889634
EPSILON = 1e-06
NEG_FILL = -1e30

F32 = jnp.float32
LOW = jnp.bfloat16
MESH = pl.DeviceIdType.MESH
VMEM_LIMIT = 62 * 2**20


def group_rows(values):
    return lax.all_gather(values, "narrow", axis=0, tiled=True)


def group_parts(values):
    return lax.psum_scatter(values, "narrow", scatter_dimension=0, tiled=True)


def contract_last(left, right):
    return lax.dot_general(
        left, right, (((1,), (1,)), ((), ())), preferred_element_type=jnp.float32
    )


def contract_first(left, right):
    return lax.dot_general(
        left, right, (((0,), (0,)), ((), ())), preferred_element_type=jnp.float32
    )


def norm_share(inputs, norm_gain):
    inverse = lax.rsqrt(jnp.mean(inputs * inputs, axis=1) + EPSILON)
    normed = inputs * inverse[:, None]
    return (inverse, normed, (normed * norm_gain).astype(jnp.bfloat16))


def norm_back(grad_normal, norm_gain, inverse, normed):
    scaled = grad_normal * norm_gain
    inner_dots = jnp.mean(scaled * normed, axis=1)
    grad_inputs = inverse[:, None] * (scaled - normed * inner_dots[:, None])
    return (grad_inputs, jnp.sum(grad_normal * normed, axis=0))


def segment_ids(lengths_row):
    positions = jnp.arange(LEN, dtype=jnp.int32)
    ends = jnp.cumsum(lengths_row)
    return jnp.sum((positions[:, None] >= ends[None, :]).astype(jnp.int32), axis=1)


def block_mask(segments, padded_seg, offset):
    query_pos = offset + jnp.arange(BLOCK, dtype=jnp.int32)
    key_pos = offset - WINDOW + jnp.arange(WINDOW + BLOCK, dtype=jnp.int32)
    query_seg = segments[offset : offset + BLOCK]
    key_seg = padded_seg[offset : offset + WINDOW + BLOCK]
    spacing = query_pos[:, None] - key_pos[None, :]
    same_doc = query_seg[:, None] == key_seg[None, :]
    inside = (spacing >= 0) & (spacing < WINDOW)
    real_doc = (query_seg[:, None] < NDOC) | (spacing == 0)
    return same_doc & inside & real_doc


def padded_inputs(keys_in, values_in, segments):
    pad_rows = jnp.zeros((WINDOW,) + keys_in.shape[1:], keys_in.dtype)
    keys_pad = jnp.concatenate([pad_rows, keys_in], axis=0)
    values_pad = jnp.concatenate([pad_rows, values_in], axis=0)
    padded_seg = jnp.concatenate([jnp.full((WINDOW,), -2, jnp.int32), segments])
    return (keys_pad, values_pad, padded_seg)


def attend_forward(queries, keys_in, values_in, segments):
    keys_pad, values_pad, padded_seg = padded_inputs(keys_in, values_in, segments)
    outputs = []
    logsums = []
    for block_index in range(LEN // BLOCK):
        offset = block_index * BLOCK
        query_block = queries[offset : offset + BLOCK]
        key_block = keys_pad[offset : offset + WINDOW + BLOCK]
        value_block = values_pad[offset : offset + WINDOW + BLOCK]
        allowed = block_mask(segments, padded_seg, offset)
        scores = jnp.einsum(
            "ihd,jhd->hij", query_block, key_block, preferred_element_type=jnp.float32
        )
        masked = jnp.where(allowed[None], scores, NEG_FILL)
        maxima = jnp.max(masked, axis=2)
        exponent = jnp.exp(masked - maxima[:, :, None])
        totals = jnp.sum(exponent, axis=2)
        probs_low = (exponent / totals[:, :, None]).astype(jnp.bfloat16)
        block_out = jnp.einsum(
            "hij,jhd->ihd", probs_low, value_block, preferred_element_type=jnp.float32
        )
        outputs.append(block_out.astype(jnp.bfloat16))
        logsums.append(maxima + jnp.log(totals))
    return (jnp.concatenate(outputs, axis=0), jnp.concatenate(logsums, axis=1))


def attend_backward(queries, keys_in, values_in, segments, logsum, grad_out):
    keys_pad, values_pad, padded_seg = padded_inputs(keys_in, values_in, segments)
    grad_keys = jnp.zeros(keys_pad.shape, jnp.float32)
    grad_values = jnp.zeros(values_pad.shape, jnp.float32)
    grad_queries = []
    for block_index in range(LEN // BLOCK):
        offset = block_index * BLOCK
        query_block = queries[offset : offset + BLOCK]
        key_block = keys_pad[offset : offset + WINDOW + BLOCK]
        value_block = values_pad[offset : offset + WINDOW + BLOCK]
        grad_block = grad_out[offset : offset + BLOCK]
        allowed = block_mask(segments, padded_seg, offset)
        scores = jnp.einsum(
            "ihd,jhd->hij", query_block, key_block, preferred_element_type=jnp.float32
        )
        masked = jnp.where(allowed[None], scores, NEG_FILL)
        soft_probs = jnp.exp(masked - logsum[:, offset : offset + BLOCK, None])
        probs_low = soft_probs.astype(jnp.bfloat16)
        grad_probs = jnp.einsum(
            "ihd,jhd->hij", grad_block, value_block, preferred_element_type=jnp.float32
        )
        inner_sums = jnp.sum(soft_probs * grad_probs, axis=2)
        grad_scores = (soft_probs * (grad_probs - inner_sums[:, :, None])).astype(jnp.bfloat16)
        grad_queries.append(
            jnp.einsum("hij,jhd->ihd", grad_scores, key_block, preferred_element_type=jnp.float32)
        )
        key_terms = jnp.einsum(
            "hij,ihd->jhd", grad_scores, query_block, preferred_element_type=jnp.float32
        )
        value_terms = jnp.einsum(
            "hij,ihd->jhd", probs_low, grad_block, preferred_element_type=jnp.float32
        )
        grad_keys = grad_keys.at[offset : offset + WINDOW + BLOCK].add(key_terms)
        grad_values = grad_values.at[offset : offset + WINDOW + BLOCK].add(value_terms)
    return (jnp.concatenate(grad_queries, axis=0), grad_keys[WINDOW:], grad_values[WINDOW:])


def silu_slope(hidden_pre):
    sigmoid_pre = jax.nn.sigmoid(hidden_pre)
    return sigmoid_pre * (1.0 + hidden_pre * (1.0 - sigmoid_pre))


def general_device(
    tokens,
    lengths,
    qkv_weight,
    out_weight,
    up_weight,
    up_bias,
    down_weight,
    down_bias,
    attn_gain,
    mlp_gain,
    query_scale,
    cotangent,
):
    head_count = qkv_weight.shape[2] // HEAD_DIM
    seq_count = lengths.shape[0]
    row_count = seq_count * LEN

    def by_sequence(values):
        return values.reshape((seq_count, LEN) + values.shape[1:])

    qkv_full, out_full, up_full, down_full = (
        lax.all_gather(qkv_weight, "wide", axis=1, tiled=True),
        lax.all_gather(out_weight, "wide", axis=1, tiled=True),
        lax.all_gather(up_weight, "wide", axis=0, tiled=True),
        lax.all_gather(down_weight, "wide", axis=1, tiled=True),
    )
    segments = jax.vmap(segment_ids)(lengths)
    inputs = tokens.astype(jnp.float32)
    inverse_one, normed_one, normal_one = norm_share(inputs, attn_gain)
    rows_one = group_rows(normal_one)
    projected = jnp.einsum("td,cdn->ctn", rows_one, qkv_full, preferred_element_type=jnp.float32)
    scale_dim = LOG_TWO_E / math.sqrt(HEAD_DIM) * jax.nn.softplus(query_scale)
    query_heads = projected[0].reshape(row_count, head_count, HEAD_DIM)
    query_low = (query_heads * scale_dim).astype(jnp.bfloat16)
    key_low = projected[1].astype(jnp.bfloat16).reshape(row_count, head_count, HEAD_DIM)
    value_low = projected[2].astype(jnp.bfloat16).reshape(row_count, head_count, HEAD_DIM)
    attended, logsum = jax.vmap(attend_forward)(
        by_sequence(query_low), by_sequence(key_low), by_sequence(value_low), segments
    )
    attended_rows = attended.reshape(row_count, head_count * HEAD_DIM)
    middle = inputs + group_parts(
        jnp.dot(attended_rows, out_full, preferred_element_type=jnp.float32)
    )
    inverse_two, normed_two, normal_two = norm_share(middle, mlp_gain)
    grad_down_bias = jnp.sum(cotangent.astype(jnp.float32), axis=0)
    rows_two = group_rows(normal_two)
    hidden_pre = jnp.dot(rows_two, up_full, preferred_element_type=jnp.float32) + up_bias
    hidden_low = jax.nn.silu(hidden_pre).astype(jnp.bfloat16)
    branch_two = (
        group_parts(jnp.dot(hidden_low, down_full, preferred_element_type=jnp.float32)) + down_bias
    )
    result = middle + branch_two
    grad_rows = group_rows(cotangent)
    grad_hidden = contract_last(grad_rows, down_full)
    grad_pre = (grad_hidden * silu_slope(hidden_pre)).astype(jnp.bfloat16)
    grad_up = contract_first(rows_two, grad_pre)
    grad_down = contract_first(hidden_low, grad_rows)
    grad_up_bias = jnp.sum(grad_pre.astype(jnp.float32), axis=0)
    grad_normal_two = group_parts(contract_last(grad_pre, up_full))
    grad_middle_norm, grad_mlp_gain = norm_back(grad_normal_two, mlp_gain, inverse_two, normed_two)
    grad_middle = cotangent.astype(jnp.float32) + grad_middle_norm
    grad_branch = group_rows(grad_middle.astype(jnp.bfloat16))
    grad_attended = contract_last(grad_branch, out_full).astype(jnp.bfloat16)
    grad_out = contract_first(attended_rows, grad_branch)
    grad_scaled, grad_key, grad_value = jax.vmap(attend_backward)(
        by_sequence(query_low),
        by_sequence(key_low),
        by_sequence(value_low),
        segments,
        logsum,
        by_sequence(grad_attended.reshape(row_count, head_count, HEAD_DIM)),
    )
    grad_scaled = grad_scaled.reshape(row_count, head_count, HEAD_DIM)
    grad_scale_part = (
        jnp.sum(grad_scaled * query_heads, axis=(0, 1))
        * (LOG_TWO_E / math.sqrt(HEAD_DIM))
        * jax.nn.sigmoid(query_scale)
    )
    grad_projected = jnp.stack(
        [
            (grad_scaled * scale_dim).reshape(row_count, head_count * HEAD_DIM),
            grad_key.reshape(row_count, head_count * HEAD_DIM),
            grad_value.reshape(row_count, head_count * HEAD_DIM),
        ]
    ).astype(jnp.bfloat16)
    grad_qkv = jnp.einsum(
        "td,ctn->cdn", rows_one, grad_projected, preferred_element_type=jnp.float32
    )
    grad_normal_one = group_parts(
        jnp.einsum("ctn,cdn->td", grad_projected, qkv_full, preferred_element_type=jnp.float32)
    )
    grad_input_norm, grad_attn_gain = norm_back(grad_normal_one, attn_gain, inverse_one, normed_one)
    grad_tokens = grad_middle + grad_input_norm
    grad_qkv, grad_out, grad_up, grad_down = (
        lax.psum_scatter(grad_qkv, "wide", scatter_dimension=1, tiled=True),
        lax.psum_scatter(grad_out, "wide", scatter_dimension=1, tiled=True),
        lax.psum_scatter(grad_up, "wide", scatter_dimension=0, tiled=True),
        lax.psum_scatter(grad_down, "wide", scatter_dimension=1, tiled=True),
    )
    grad_attn_gain, grad_mlp_gain, grad_down_bias, grad_scale = lax.psum(
        (grad_attn_gain, grad_mlp_gain, grad_down_bias, grad_scale_part), ("wide", "narrow")
    )
    grad_up_bias = lax.psum(grad_up_bias, "wide")
    return (
        result.astype(jnp.bfloat16),
        grad_tokens,
        grad_qkv,
        grad_out,
        grad_up,
        grad_up_bias,
        grad_down,
        grad_down_bias,
        grad_attn_gain,
        grad_mlp_gain,
        grad_scale,
    )


def product(left, right, left_dim=1, right_dim=0):
    return lax.dot_general(
        left, right, (((left_dim,), (right_dim,)), ((), ())), preferred_element_type=F32
    )


def flip(value, mask):
    bit = 1
    while bit <= mask:
        if mask & bit:
            value = value + bit * (1 - 2 * lax.rem(lax.div(value, bit), 2))
        bit *= 2
    return value


def part(start, size):
    return pl.ds(pl.multiple_of(start * size, size), size)


def chunks(total, size, body):
    def step(index, carry):
        body(part(index, size))
        return carry

    lax.fori_loop(0, total // size, step, 0)


def add_rows(target, source, size):
    def body(span):
        target[span, :] = (target[span, :].astype(F32) + source[span, :].astype(F32)).astype(LOW)

    chunks(source.shape[0], size, body)


class Place:
    def __init__(self, group):
        self.wide = lax.axis_index("wide")
        self.narrow = lax.axis_index("narrow")
        self.core = lax.rem(self.wide, 2)
        self.y = lax.div(self.wide, 2)
        self.quarter = lax.rem(self.narrow, group)
        self.half = lax.div(self.narrow, group)

    def along_wide(self, mask):
        return (flip(self.wide, mask), self.narrow)

    def along_narrow(self, mask):
        return (self.wide, flip(self.narrow, mask))


def greet(place, narrow_masks, wide_masks):
    barrier = pltpu.get_barrier_semaphore()
    peers = [place.along_narrow(m) for m in narrow_masks]
    peers += [place.along_wide(m) for m in wide_masks]
    for peer in peers:
        pl.semaphore_signal(barrier, inc=1, device_id=peer, device_id_type=MESH)
    pl.semaphore_wait(barrier, len(peers))


def document_ends(lengths, row):
    ends, total = [], 0
    for index in range(NDOC):
        total = total + lengths[row, index]
        ends.append(total)
    return ends


def first_key(ends, offset):
    position = offset + lax.broadcasted_iota(jnp.int32, (1, TILE), 1)
    start = jnp.zeros_like(position)
    for end in ends:
        start = jnp.where(position >= end, end, start)
    start = jnp.maximum(start, position - (WINDOW - 1))
    return jnp.where(position >= ends[-1], position, start), position


def allowed_scores(scores, key_start, offset, first, position):
    key = key_start + lax.broadcasted_iota(jnp.int32, scores.shape, 0)
    allowed = key >= first
    if key_start + scores.shape[0] > offset:
        allowed = allowed & (key <= position)
    return jnp.where(allowed, scores, NEG_FILL)


def tile_keys(tile):
    offset = tile * TILE
    return offset, range(max(0, offset - WINDOW), offset + TILE, TILE)


def pipelined(count, first_half, second_half):
    waiting = None
    for tile in range(count):
        current = (tile, first_half(tile))
        if waiting is not None:
            second_half(*waiting)
        waiting = current
    second_half(*waiting)


def attend_head(head, ends, queries, keys, values_t, attended, logsum):
    def first_half(tile):
        offset, starts = tile_keys(tile)
        first, position = first_key(ends, offset)
        query = queries[head, :, offset : offset + TILE]
        blocks, maxima = [], None
        for start in starts:
            scores = product(keys[head, start : start + TILE, :], query)
            scores = allowed_scores(scores, start, offset, first, position)
            top = jnp.max(scores, axis=0, keepdims=True)
            maxima = top if maxima is None else jnp.maximum(maxima, top)
            blocks.append(scores)
        return blocks, maxima

    def second_half(tile, held):
        blocks, maxima = held
        offset, starts = tile_keys(tile)
        total, output = None, None
        for scores, start in zip(blocks, starts):
            exponent = jnp.exp(scores - maxima)
            share = jnp.sum(exponent, axis=0, keepdims=True)
            term = product(values_t[head, :, start : start + TILE], exponent.astype(LOW))
            total, output = (
                (share, term) if total is None else (total + share, output + term)
            )
        attended[head, :, offset : offset + TILE] = (output * (1.0 / total)).astype(LOW)
        logsum[head, :, offset : offset + TILE] = maxima + jnp.log(total)

    pipelined(LEN // TILE, first_half, second_half)


def norm_rows(inputs):
    return lax.rsqrt(jnp.mean(inputs * inputs, axis=1, keepdims=True) + EPSILON)


def forward_kernel(
    group,
    lengths,
    tokens,
    shards,
    gain,
    scale,
    bias,
    x_out,
    qf_out,
    q_out,
    kt_out,
    kn_out,
    vn_out,
    wq_out,
    lse_out,
    att_out,
    wm_out,
    bias_out,
    x_all,
    w_qkv,
    w_mlp,
    w_pair,
    w_half,
    bias_all,
    query_full,
    query_t,
    key_t,
    value_t,
    key_n,
    value_n,
    logsum,
    attended,
    att_all,
    send_sem,
    recv_sem,
    local_sem,
):
    place = Place(group)
    core, y, quarter, half, narrow = (
        place.core,
        place.y,
        place.quarter,
        place.half,
        place.narrow,
    )
    rows = tokens.shape[0]
    mid = rows // 2
    slab = shards.shape[1] // 2
    pair_cols = 2 * shards.shape[2]
    cols_y = part(y, pair_cols)
    cols_other = part(1 - y, pair_cols)
    x_dev, z_dev, far_dev = (
        place.along_narrow(1),
        place.along_narrow(2),
        place.along_narrow(group),
    )
    core_dev, y_dev = place.along_wide(1), place.along_wide(2)
    ids = iter(range(send_sem.shape[0]))
    sent = []

    def copy(source, target, device, index=None):
        index = next(ids) if index is None else index
        return pltpu.make_async_remote_copy(
            src_ref=source,
            dst_ref=target,
            send_sem=send_sem.at[index],
            recv_sem=recv_sem.at[index],
            device_id=device,
            device_id_type=MESH,
        )

    def exchange(source, target, incoming, device):
        index = next(ids)
        out = copy(source, target, device, index)
        out.start()
        sent.append(out)
        return copy(incoming, incoming, device, index)

    greet(place, range(1, 2 * group), (1, 2))

    halves = (slice(0, mid), slice(mid, rows))

    def x_part(mask, which):
        return x_all.at[flip(quarter, mask), halves[which]]

    w_arrived = exchange(shards.at[:, part(1 - core, slab), :], w_half, w_half, core_dev)
    x_from = {}
    for key, device, mask, which in (
        ("x0", x_dev, 1, 0),
        ("z1", z_dev, 2, 1),
        ("x1", x_dev, 1, 1),
        ("z0", z_dev, 2, 0),
    ):
        x_from[key] = exchange(
            tokens.at[halves[which]], x_part(0, which), x_part(mask, which), device
        )
    bias_from = [
        exchange(bias, bias_all.at[narrow], bias_all.at[flip(narrow, mask)], place.along_narrow(mask))
        for mask in range(1, 2 * group)
    ]
    bias_all[narrow] = bias[...]
    x_all[quarter] = tokens[...]

    w_arrived.wait_recv()
    own = shards[:, part(core, slab), :]
    other = w_half[...]
    w_pair[:, :, : pair_cols // 2] = jnp.where(core == 0, own, other)
    w_pair[:, :, pair_cols // 2 :] = jnp.where(core == 0, other, own)
    for m in range(3):
        w_qkv[m, core, half, :, cols_y] = w_pair[m]
        w_mlp[m, core, part(narrow, slab), cols_y] = w_pair[3 + m]

    def q_block(which, columns):
        return w_qkv.at[:, core, which, :, columns]

    def m_block(m, mask):
        return w_mlp.at[m, core, part(flip(narrow, mask), slab), cols_y]

    q_far = exchange(q_block(half, cols_y), q_block(half, cols_y), q_block(1 - half, cols_y), far_dev)
    m_far = [
        exchange(m_block(m, 0), m_block(m, 0), m_block(m, group), far_dev) for m in range(3)
    ]
    q_far.wait_recv()
    q_y = exchange(
        w_qkv.at[:, core, :, :, cols_y],
        w_qkv.at[:, core, :, :, cols_y],
        w_qkv.at[:, core, :, :, cols_other],
        y_dev,
    )

    def z_step(m):
        m_far[m].wait_recv()
        return [
            exchange(m_block(m, o), m_block(m, o), m_block(m, o ^ 2), z_dev) for o in (0, group)
        ]

    def x_step(m, arrived):
        for one in arrived:
            one.wait_recv()
        return [
            exchange(m_block(m, o), m_block(m, o), m_block(m, o ^ 1), x_dev)
            for o in (0, 2, group, group + 2)
        ]

    m_z = [z_step(0)]
    x_from["x0"].wait_recv()
    x_from["d0"] = exchange(x_part(1, 0), x_part(1, 0), x_part(3, 0), z_dev)
    x_from["z1"].wait_recv()
    x_from["d1"] = exchange(x_part(2, 1), x_part(2, 1), x_part(3, 1), x_dev)
    q_y.wait_recv()
    q_core = exchange(w_qkv.at[:, core], w_qkv.at[:, core], w_qkv.at[:, 1 - core], core_dev)
    m_z += [z_step(1), z_step(2)]
    m_x = [x_step(0, m_z[0])]
    q_core.wait_recv()

    def project(mask):
        where = flip(quarter, mask)
        span = part(where, rows)
        inputs = x_all[where].astype(F32)
        normal = (inputs * norm_rows(inputs) * gain[...]).astype(LOW)
        weight = w_qkv[...].reshape(-1, normal.shape[1])
        result = product(weight, normal, 1, 1)
        size = result.shape[0] // 3
        heads = size // HEAD_DIM
        query_full[:, span] = result[:size]
        query_t[:, :, span] = (
            (result[:size] * scale[...]).astype(LOW).reshape(heads, HEAD_DIM, rows)
        )
        key = result[size : 2 * size].astype(LOW).reshape(heads, HEAD_DIM, rows)
        value = result[2 * size :].astype(LOW).reshape(heads, HEAD_DIM, rows)
        key_t[:, :, span] = key
        value_t[:, :, span] = value
        for head in range(heads):
            key_n[head, span, :] = key[head].T
            value_n[head, span, :] = value[head].T

    project(0)
    x_from["x1"].wait_recv()
    project(1)
    x_from["z0"].wait_recv()
    project(2)
    x_from["d0"].wait_recv()
    x_from["d1"].wait_recv()
    project(3)
    m_x += [x_step(1, m_z[1]), x_step(2, m_z[2])]

    stores = []

    def store(source, target):
        one = pltpu.make_async_copy(source, target, local_sem.at[len(stores)])
        one.start()
        stores.append(one)

    store(x_all, x_out)
    store(query_full, qf_out)
    store(query_t, q_out)
    store(key_t, kt_out)
    store(key_n, kn_out)
    store(value_n, vn_out)
    store(w_qkv, wq_out)

    ends = document_ends(lengths, half)
    heads = query_t.shape[0]
    first_id = next(ids)
    for _ in range(3 * heads - 1):
        next(ids)

    def att_copy(head, mask, incoming):
        peer = flip(quarter, mask)
        index = first_id + 3 * head + mask - 1
        slot = (lax.div(head, 2), lax.rem(head, 2))
        if incoming:
            there = att_all.at[slot[0], slot[1], peer]
            return copy(there, there, place.along_narrow(mask), index)
        return copy(
            attended.at[head, :, part(peer, rows)],
            att_all.at[slot[0], slot[1], quarter],
            place.along_narrow(mask),
            index,
        )

    def y_step(m):
        for one in m_x[m]:
            one.wait_recv()
        return exchange(
            w_mlp.at[m, core, :, cols_y],
            w_mlp.at[m, core, :, cols_y],
            w_mlp.at[m, core, :, cols_other],
            y_dev,
        )

    def core_step(m, arrived):
        arrived.wait_recv()
        return exchange(w_mlp.at[m, core], w_mlp.at[m, core], w_mlp.at[m, 1 - core], core_dev)

    m_y = [y_step(0)]

    def one_head(head, carry):
        attend_head(head, ends, query_t, key_n, value_t, attended, logsum)
        for mask in (3, 1, 2):
            att_copy(head, mask, False).start()
        att_all[lax.div(head, 2), lax.rem(head, 2), quarter] = attended[head, :, part(quarter, rows)]
        return carry

    lax.fori_loop(0, heads // 2, one_head, 0)
    m_y.append(y_step(1))
    lax.fori_loop(heads // 2, heads, one_head, 0)
    m_y.append(y_step(2))
    m_core = [core_step(0, m_y[0]), core_step(1, m_y[1])]
    store(logsum, lse_out)

    def finish_head(head, carry):
        for mask in (1, 2, 3):
            att_copy(head, mask, True).wait_recv()
        return carry

    lax.fori_loop(0, heads, finish_head, 0)
    store(att_all, att_out)
    for one in bias_from:
        one.wait_recv()
    store(bias_all, bias_out)
    m_core.append(core_step(2, m_y[2]))
    for m in range(3):
        m_core[m].wait_recv()
        store(w_mlp.at[m], wm_out.at[m])

    def finish_send(head, carry):
        for mask in (1, 2, 3):
            att_copy(head, mask, False).wait_send()
        return carry

    lax.fori_loop(0, heads, finish_send, 0)
    for one in sent:
        one.wait_send()
    for one in stores:
        one.wait()


def mlp_kernel(
    tokens,
    attended,
    weights,
    up_bias,
    down_bias,
    gain,
    cotangent,
    result,
    grad_middle,
    grad_attended,
    grads,
    sums,
):
    att = attended[...].reshape(-1, attended.shape[-1])
    size = att.shape[0]
    wide_shape = (2, size // 2, weights.shape[-1])

    def weight(m):
        return weights[m].reshape(size, -1)

    middle = tokens[...].astype(F32) + product(att, weight(0), 0, 0)
    inverse = norm_rows(middle)
    normed = middle * inverse
    normal = (normed * gain[...]).astype(LOW)
    pre = product(normal, weight(1), 1, 1) + up_bias[...]
    gate = 1.0 / (1.0 + jnp.exp(-pre))
    hidden = (pre * gate).astype(LOW)
    cot = cotangent[...]
    grad_hidden = product(cot, weight(2), 1, 1)
    grad_pre = (grad_hidden * (gate * (1.0 + pre * (1.0 - gate)))).astype(LOW)
    result[...] = (middle + (product(hidden, weight(2)) + down_bias[...])).astype(LOW)
    grad_normal = product(grad_pre, weight(1))
    scaled = grad_normal * gain[...]
    inner = jnp.mean(scaled * normed, axis=1, keepdims=True)
    cot_full = cot.astype(F32)
    grad_mid = cot_full + inverse * (scaled - normed * inner)
    grad_middle[...] = grad_mid
    branch = grad_mid.astype(LOW)
    grad_attended[...] = product(weight(0), branch, 1, 1).astype(LOW).reshape(grad_attended.shape)
    grads[0] = product(att, branch).astype(LOW).reshape(wide_shape)
    grads[1] = product(grad_pre, normal, 0, 0).astype(LOW).reshape(wide_shape)
    grads[2] = product(hidden, cot, 0, 0).astype(LOW).reshape(wide_shape)
    sums[...] = jnp.zeros_like(sums)
    sums[0:1, :] = jnp.sum(grad_normal * normed, axis=0, keepdims=True)
    sums[1:2, :] = jnp.sum(cot_full, axis=0, keepdims=True)
    sums[2:3, :] = jnp.sum(grad_pre.astype(F32), axis=0, keepdims=True)


def backward_head(
    head,
    ends,
    queries,
    query_full,
    keys,
    keys_t,
    values,
    grad_out,
    logsum,
    scale,
    grads_t,
    sum_keys,
    sum_values,
    sum_scale,
):
    sum_keys[...] = jnp.zeros_like(sum_keys)
    sum_values[...] = jnp.zeros_like(sum_values)

    def first_half(tile):
        offset, starts = tile_keys(tile)
        first, position = first_key(ends, offset)
        span = slice(offset, offset + TILE)
        query, grad, log_row = queries[head, :, span], grad_out[head, :, span], logsum[head, :, span]
        blocks, inner = [], None
        for start in starts:
            scores = product(keys[head, start : start + TILE, :], query)
            scores = allowed_scores(scores, start, offset, first, position)
            probs = jnp.exp(scores - log_row)
            grad_probs = product(values[head, start : start + TILE, :], grad)
            share = jnp.sum(probs * grad_probs, axis=0, keepdims=True)
            inner = share if inner is None else inner + share
            blocks.append((probs, grad_probs))
        return blocks, inner, query, grad

    def second_half(tile, held):
        blocks, inner, query, grad = held
        offset, starts = tile_keys(tile)
        span = slice(offset, offset + TILE)
        grad_scaled = None
        for (probs, grad_probs), start in zip(blocks, starts):
            there = slice(start, start + TILE)
            grad_scores = (probs * (grad_probs - inner)).astype(LOW)
            term = product(keys_t[head, :, there], grad_scores)
            grad_scaled = term if grad_scaled is None else grad_scaled + term
            sum_keys[:, there] += product(query, grad_scores, 1, 1)
            sum_values[:, there] += product(grad, probs.astype(LOW), 1, 1)
        grads_t[0, head, :, span] = (grad_scaled * scale[...]).astype(LOW)
        terms = grad_scaled * query_full[part(head, HEAD_DIM), span]
        sum_scale[...] += terms[:, : TILE // 2] + terms[:, TILE // 2 :]

    pipelined(LEN // TILE, first_half, second_half)
    grads_t[1, head] = sum_keys[...].astype(LOW)
    grads_t[2, head] = sum_values[...].astype(LOW)


def backward_kernel(
    group,
    lengths,
    tokens,
    gain,
    scale,
    sums,
    grad_middle,
    grad_own,
    w_grads,
    x_in,
    query_full,
    query_t,
    key_t,
    key_n,
    value_n,
    w_qkv_in,
    logsum,
    tokens_out,
    mlp_out,
    qkv_out,
    sums_out,
    x_all,
    grad_att,
    grads_t,
    sum_keys,
    sum_values,
    sum_scale,
    w_own,
    w_core,
    w_y,
    w_x,
    w_z,
    w_far,
    w_last,
    dx_own,
    dx_x,
    dx_z,
    dx_z_last,
    dx_x_last,
    w_qkv,
    dw_core,
    dw_y,
    dw_far,
    dw_last,
    all_sums,
    got_sums,
    send_sem,
    recv_sem,
    local_sem,
):
    place = Place(group)
    core, y, quarter, half, narrow = (
        place.core,
        place.y,
        place.quarter,
        place.half,
        place.narrow,
    )
    rows = tokens.shape[0]
    mid = rows // 2
    slab = qkv_out.shape[2]
    cols = qkv_out.shape[3]
    pair_cols = 2 * cols
    cols_y = part(y, pair_cols)
    cols_other = part(1 - y, pair_cols)
    x_dev, z_dev, far_dev = (
        place.along_narrow(1),
        place.along_narrow(2),
        place.along_narrow(group),
    )
    core_dev, y_dev = place.along_wide(1), place.along_wide(2)
    ids = iter(range(send_sem.shape[0]))
    sent = []
    dxs = w_core
    dw = w_qkv

    def copy(source, target, device, index):
        return pltpu.make_async_remote_copy(
            src_ref=source,
            dst_ref=target,
            send_sem=send_sem.at[index],
            recv_sem=recv_sem.at[index],
            device_id=device,
            device_id_type=MESH,
        )

    def exchange(source, target, device):
        index = next(ids)
        out = copy(source, target, device, index)
        out.start()
        sent.append(out)
        return out

    greet(place, range(1, group + 1), (1, 2))

    heads = query_t.shape[0]
    first_id = next(ids)
    for _ in range(3 * heads - 1):
        next(ids)

    def att_copy(head, mask, incoming):
        peer = flip(quarter, mask)
        index = first_id + 3 * head + mask - 1
        if incoming:
            there = grad_att.at[head, :, part(peer, rows)]
            return copy(there, there, place.along_narrow(mask), index)
        return copy(
            grad_own.at[lax.div(head, 2), lax.rem(head, 2), peer],
            grad_att.at[head, :, part(quarter, rows)],
            place.along_narrow(mask),
            index,
        )

    for head in range(heads):
        for mask in (3, 1, 2):
            att_copy(head, mask, False).start()
        grad_att[head, :, part(quarter, rows)] = grad_own[head // 2, head % 2, quarter]
    span_m = w_own.shape[1]
    loads = []
    m_core = []
    for m in range(3):
        m_core.append(
            exchange(w_grads.at[m, 1 - core], w_core.at[m * span_m : (m + 1) * span_m], core_dev)
        )
        loads.append(pltpu.make_async_copy(w_grads.at[m, core], w_own.at[m], local_sem.at[m]))
        loads[-1].start()
    late = [
        pltpu.make_async_copy(source, target, local_sem.at[3 + k])
        for k, (source, target) in enumerate(
            ((x_in, x_all), (w_qkv_in, w_qkv), (grad_middle, tokens_out))
        )
    ]
    for one in late:
        one.start()

    def y_step(m):
        m_core[m].wait_recv()
        loads[m].wait()
        add_rows(w_own.at[m], w_core.at[m * span_m : (m + 1) * span_m], 128)
        return exchange(w_own.at[m, :, cols_other], w_y.at[m], y_dev)

    def block(m, mask):
        return (m, part(flip(narrow, mask), slab), cols_y)

    def add_block(m, mask, arrived):
        where = block(m, mask)
        w_own[where] = (w_own[where].astype(F32) + arrived.astype(F32)).astype(LOW)

    def x_step(m, arrived):
        arrived.wait_recv()
        add_rows(w_own.at[m, :, cols_y], w_y.at[m], 128)
        return [
            exchange(w_own.at[block(m, o)], w_x.at[m, (o ^ 1) // 2], x_dev)
            for o in (1, 3, group + 1, group + 3)
        ]

    def z_step(m, arrived):
        for k, one in enumerate(arrived):
            one.wait_recv()
        for k in range(4):
            add_block(m, 2 * k, w_x[m, k])
        return [
            exchange(w_own.at[block(m, o)], w_z.at[m, (o ^ 2) // group], z_dev)
            for o in (2, group + 2)
        ]

    def far_step(m, arrived):
        for one in arrived:
            one.wait_recv()
        for k in range(2):
            add_block(m, group * k, w_z[m, k])
        return exchange(w_own.at[block(m, group)], w_far.at[m], far_dev)

    def last_step(total, out_ref, m, buffer):
        mine = jnp.where(core == 0, total[:, :cols], total[:, cols:])
        theirs = jnp.where(core == 0, total[:, cols:], total[:, :cols])
        out_ref[m, core] = mine
        buffer[m] = theirs
        return exchange(buffer.at[m], out_ref.at[m, core], core_dev)

    def m_last(m, arrived):
        arrived.wait_recv()
        total = w_own[block(m, 0)].astype(F32) + w_far[m].astype(F32)
        return last_step(total, mlp_out, m, w_last)

    ends = document_ends(lengths, half)
    sum_scale[...] = jnp.zeros_like(sum_scale)

    def one_head(head, carry):
        for mask in (1, 2, 3):
            att_copy(head, mask, True).wait_recv()
        backward_head(
            head,
            ends,
            query_t,
            query_full,
            key_n,
            key_t,
            value_n,
            grad_att,
            logsum,
            scale,
            grads_t,
            sum_keys,
            sum_values,
            sum_scale,
        )
        return carry

    m_y = [y_step(0), y_step(1), y_step(2)]
    lax.fori_loop(0, heads - 1, one_head, 0)
    m_x = [x_step(0, m_y[0])]
    lax.fori_loop(heads - 1, heads, one_head, 0)

    size = 3 * heads * HEAD_DIM
    for one in late:
        one.wait()

    def grad_inputs(mask, target, start):
        first = flip(quarter, mask) * 2
        for which in range(2):
            span = part(first + which, mid)
            there = slice(start + which * mid, start + (which + 1) * mid)
            target[there] = product(
                grads_t[:, :, :, span].reshape(size, mid), w_qkv[...].reshape(size, -1), 0, 0
            ).astype(target.dtype)

    slot = {1: 0, 2: 1, 3: 2}

    def dx_part(mask, which):
        start = slot[mask] * rows + which * mid
        return slice(start, start + mid)

    def keep(mask):
        grad_inputs(mask, dxs, slot[mask] * rows)

    keep(3)
    from_x1 = exchange(dxs.at[dx_part(3, 0)], dx_x.at[1], x_dev)
    from_z1 = exchange(dxs.at[dx_part(3, 1)], dx_z.at[1], z_dev)
    keep(1)
    from_x0 = exchange(dxs.at[dx_part(1, 0)], dx_x.at[0], x_dev)
    keep(2)
    from_z0 = exchange(dxs.at[dx_part(2, 1)], dx_z.at[0], z_dev)
    grad_inputs(0, dx_own, 0)

    all_sums[0] = sums[...]
    all_sums[0, 3:4, :HEAD_DIM] = jnp.sum(sum_scale[...].T, axis=0, keepdims=True)
    for mask in (3, 1, 2, 0):
        where = flip(quarter, mask)
        start = slot[mask] * rows if mask else 0
        grads = dxs.at[start : start + rows] if mask else dx_own

        def gain_rows(span, where=where, grads=grads):
            inputs = x_all[where, span, :].astype(F32)
            normed = inputs * norm_rows(inputs)
            terms = grads[span, :].astype(F32) * normed
            all_sums[0, 4:5, :] += jnp.sum(terms, axis=0, keepdims=True)
            x_all[where, span, :] = (normed * gain[...]).astype(LOW)

        chunks(rows, 128, gain_rows)

    sum_devices = [core_dev, y_dev, x_dev, z_dev, far_dev]

    def sum_step(stage):
        return exchange(all_sums.at[stage], got_sums.at[stage], sum_devices[stage])

    def sum_add(stage, arrived):
        arrived.wait_recv()
        all_sums[stage + 1] = all_sums[stage] + got_sums[stage]

    sums_now = sum_step(0)
    for m in range(3):
        dw[m] = (
            product(grads_t[m].reshape(size // 3, LEN), x_all[...].reshape(LEN, -1))
            .astype(LOW)
            .reshape(dw.shape[1:])
        )
    q_core = exchange(dw.at[:, 1 - core], dw_core, core_dev)
    sum_add(0, sums_now)
    sums_now = sum_step(1)
    q_core.wait_recv()
    for m in range(3):
        dw[m, core] = (dw[m, core].astype(F32) + dw_core[m].astype(F32)).astype(LOW)
    q_y = exchange(dw.at[:, core, :, :, cols_other], dw_y, y_dev)

    from_x1.wait_recv()
    there = dx_part(2, 0)
    add_rows(dxs.at[there], dx_x.at[1], 128)
    from_z2 = exchange(dxs.at[there], dx_z_last, z_dev)
    from_z1.wait_recv()
    there = dx_part(1, 1)
    add_rows(dxs.at[there], dx_z.at[1], 128)
    from_x2 = exchange(dxs.at[there], dx_x_last, x_dev)

    sum_add(1, sums_now)
    sums_now = sum_step(2)
    m_x += [x_step(1, m_y[1])]
    m_z = [z_step(0, m_x[0])]
    sum_add(2, sums_now)
    sums_now = sum_step(3)
    q_y.wait_recv()
    here = (slice(None), core, slice(None), slice(None), cols_y)
    dw[here] = (dw[here].astype(F32) + dw_y[...].astype(F32)).astype(LOW)
    q_far = exchange(dw.at[:, core, 1 - half, :, cols_y], dw_far, far_dev)
    m_x += [x_step(2, m_y[2])]
    m_z += [z_step(1, m_x[1])]
    m_far = [far_step(0, m_z[0])]
    sum_add(3, sums_now)
    sums_now = sum_step(4)
    m_z += [z_step(2, m_x[2])]
    m_far += [far_step(1, m_z[1])]
    q_far.wait_recv()
    last = []
    for m in range(3):
        total = dw[m, core, half, :, cols_y].astype(F32) + dw_far[m].astype(F32)
        last.append(last_step(total, qkv_out, m, dw_last))
    last.append(m_last(0, m_far[0]))
    m_far += [far_step(2, m_z[2])]
    last.append(m_last(1, m_far[1]))
    sum_add(4, sums_now)
    sums_out[...] = all_sums[5]

    from_x0.wait_recv()
    from_z0.wait_recv()
    from_z2.wait_recv()
    from_x2.wait_recv()
    for which, (first, second) in enumerate(((dx_x, dx_z_last), (dx_z, dx_x_last))):

        def final_rows(span, which=which, first=first, second=second):
            here = pl.ds(which * mid + span.start, span.size)
            inputs = tokens[here, :].astype(F32)
            inverse = norm_rows(inputs)
            normed = inputs * inverse
            grad = dx_own[here, :] + first[0, span, :].astype(F32) + second[span, :].astype(F32)
            scaled = grad * gain[...]
            inner = jnp.mean(scaled * normed, axis=1, keepdims=True)
            tokens_out[here, :] += inverse * (scaled - normed * inner)

        chunks(mid, 128, final_rows)
    last.append(m_last(2, m_far[2]))

    for one in last:
        one.wait_recv()

    def finish_send(head, carry):
        for mask in (1, 2, 3):
            att_copy(head, mask, False).wait_send()
        return carry

    lax.fori_loop(0, heads, finish_send, 0)
    for one in sent:
        one.wait_send()


def struct(shape, dtype):
    return jax.ShapeDtypeStruct(shape, dtype)


def kernel_call(kernel, outputs, in_specs, out_spaces, scratch, collective_id=None):
    extra = {} if collective_id is None else {"collective_id": collective_id, "has_side_effects": True}
    return pl.pallas_call(
        kernel,
        out_shape=tuple(outputs),
        in_specs=[pl.BlockSpec(memory_space=space) for space in in_specs],
        out_specs=tuple(pl.BlockSpec(memory_space=space) for space in out_spaces),
        scratch_shapes=scratch,
        compiler_params=pltpu.CompilerParams(vmem_limit_bytes=VMEM_LIMIT, **extra),
    )


def fused_device(
    group,
    tokens,
    lengths,
    qkv_weight,
    out_weight,
    up_weight,
    up_bias,
    down_weight,
    down_bias,
    attn_gain,
    mlp_gain,
    query_scale,
    cotangent,
):
    rows, dim = tokens.shape
    slab2, cols = out_weight.shape
    slab = slab2 // 2
    halves = lengths.shape[0]
    heads = halves * slab2 // HEAD_DIM
    local = heads * HEAD_DIM
    narrow_count = group * halves
    hidden = slab2 * narrow_count
    vmem, smem, anywhere = pltpu.VMEM, pltpu.SMEM, pl.ANY

    shards = jnp.concatenate(
        [
            jnp.swapaxes(qkv_weight, 1, 2),
            out_weight[None],
            up_weight.T[None],
            down_weight[None],
        ]
    )
    gain_one, gain_two = attn_gain[None], mlp_gain[None]
    scale_dim = LOG_TWO_E / math.sqrt(HEAD_DIM) * jax.nn.softplus(query_scale)
    scale_one = scale_dim[:, None]
    scale_all = jnp.tile(scale_one, (heads, 1))
    bias_rows = jnp.broadcast_to(up_bias.astype(F32)[None], (8, slab2))

    att_shape = (2, halves, group, HEAD_DIM, rows)
    wq_shape = (3, 2, halves, slab, dim)
    wm_shape = (3, 2, narrow_count * slab, dim)
    dma = pltpu.SemaphoreType.DMA

    forward_outputs = [
        struct((group, rows, dim), LOW),
        struct((local, LEN), F32),
        struct((heads, HEAD_DIM, LEN), LOW),
        struct((heads, HEAD_DIM, LEN), LOW),
        struct((heads, LEN, HEAD_DIM), LOW),
        struct((heads, LEN, HEAD_DIM), LOW),
        struct(wq_shape, LOW),
        struct((heads, 1, LEN), F32),
        struct(att_shape, LOW),
        struct(wm_shape, LOW),
        struct((narrow_count, 8, slab2), F32),
    ]
    x_all, query_full, query_t, key_t, key_n, value_n, w_qkv, logsum, att_all, w_mlp, bias_all = (
        kernel_call(
            functools.partial(forward_kernel, group),
            forward_outputs,
            [smem] + [vmem] * 5,
            [anywhere] * len(forward_outputs),
            [
                vmem((group, rows, dim), LOW),
                vmem(wq_shape, LOW),
                vmem(wm_shape, LOW),
                vmem((6, slab, 2 * cols), LOW),
                vmem((6, slab, cols), LOW),
                vmem((narrow_count, 8, slab2), F32),
                vmem((local, LEN), F32),
                vmem((heads, HEAD_DIM, LEN), LOW),
                vmem((heads, HEAD_DIM, LEN), LOW),
                vmem((heads, HEAD_DIM, LEN), LOW),
                vmem((heads, LEN, HEAD_DIM), LOW),
                vmem((heads, LEN, HEAD_DIM), LOW),
                vmem((heads, 1, LEN), F32),
                vmem((heads, HEAD_DIM, LEN), LOW),
                vmem(att_shape, LOW),
                dma((64,)),
                dma((64,)),
                dma((16,)),
            ],
            collective_id=0,
        )(lengths, tokens, shards, gain_one, scale_all, bias_rows)
    )

    def hidden_order(values):
        return values.reshape(narrow_count, 2, slab).swapaxes(0, 1).reshape(1, hidden)

    result, grad_middle, grad_att, w_grads, sums = kernel_call(
        mlp_kernel,
        [
            struct((rows, dim), LOW),
            struct((rows, dim), F32),
            struct(att_shape, LOW),
            struct(wm_shape, LOW),
            struct((8, dim), F32),
        ],
        [vmem] * 7,
        [vmem] * 5,
        [],
    )(
        tokens,
        att_all,
        w_mlp,
        hidden_order(bias_all[:, 0]),
        down_bias.astype(F32)[None],
        gain_two,
        cotangent,
    )

    last_shape = (3, 2, slab, cols)
    grad_tokens, mlp_grads, qkv_grads, totals = kernel_call(
        functools.partial(backward_kernel, group),
        [
            struct((rows, dim), F32),
            struct(last_shape, F32),
            struct(last_shape, F32),
            struct((8, dim), F32),
        ],
        [smem] + [vmem] * 4 + [anywhere, vmem] + [anywhere] * 2 + [vmem] * 5 + [anywhere, vmem],
        [vmem] * 4,
        [
            vmem((group, rows, dim), LOW),
            vmem((heads, HEAD_DIM, LEN), LOW),
            vmem((3, heads, HEAD_DIM, LEN), LOW),
            vmem((HEAD_DIM, LEN), F32),
            vmem((HEAD_DIM, LEN), F32),
            vmem((HEAD_DIM, TILE // 2), F32),
            vmem((3, narrow_count * slab, dim), LOW),
            vmem((3 * narrow_count * slab, dim), LOW),
            vmem((3, narrow_count * slab, 2 * cols), LOW),
            vmem((3, 4, slab, 2 * cols), LOW),
            vmem((3, 2, slab, 2 * cols), LOW),
            vmem((3, slab, 2 * cols), LOW),
            vmem((3, slab, cols), F32),
            vmem((rows, dim), F32),
            vmem((2, rows // 2, dim), LOW),
            vmem((2, rows // 2, dim), LOW),
            vmem((rows // 2, dim), LOW),
            vmem((rows // 2, dim), LOW),
            vmem(wq_shape, LOW),
            vmem((3, halves, slab, dim), LOW),
            vmem((3, halves, slab, 2 * cols), LOW),
            vmem((3, slab, 2 * cols), LOW),
            vmem((3, slab, cols), F32),
            vmem((6, 8, dim), F32),
            vmem((5, 8, dim), F32),
            dma((80,)),
            dma((80,)),
            dma((6,)),
        ],
        collective_id=1,
    )(
        lengths,
        tokens,
        gain_one,
        scale_one,
        sums,
        grad_middle,
        grad_att,
        w_grads,
        x_all,
        query_full,
        query_t,
        key_t,
        key_n,
        value_n,
        w_qkv,
        logsum,
    )

    mlp_grads = mlp_grads.reshape(3, slab2, cols)
    grad_up_bias = lax.dynamic_index_in_dim(
        totals[2].reshape(2, narrow_count, slab), lax.axis_index("narrow"), 1, keepdims=False
    ).reshape(slab2)
    grad_scale = (
        totals[3, :HEAD_DIM] * (LOG_TWO_E / math.sqrt(HEAD_DIM)) * jax.nn.sigmoid(query_scale)
    )
    return (
        result,
        grad_tokens,
        jnp.swapaxes(qkv_grads.reshape(3, slab2, cols), 1, 2),
        mlp_grads[0],
        mlp_grads[1].T,
        grad_up_bias,
        mlp_grads[2],
        totals[1],
        totals[4],
        totals[0],
        grad_scale,
    )


def solution(mesh):
    wide_count, narrow_count = mesh.shape["wide"], mesh.shape["narrow"]

    def per_device(*args):
        tokens, lengths, out_weight = args[0], args[1], args[3]
        group = LEN // tokens.shape[0]
        fits = (
            wide_count == 4
            and group == 4
            and narrow_count == group * lengths.shape[0] == 8
            and out_weight.shape[0] == 2 * HEAD_DIM
            and 2 * out_weight.shape[1] % 128 == 0
        )
        if fits:
            return fused_device(group, *args)
        return general_device(*args)

    return jax.shard_map(
        per_device,
        mesh=mesh,
        in_specs=(
            P(("wide", "narrow"), None),
            P("wide", None),
            P(None, "wide", "narrow"),
            P("narrow", "wide"),
            P("wide", "narrow"),
            P("narrow"),
            P("narrow", "wide"),
            P(),
            P(),
            P(),
            P(),
            P(("wide", "narrow"), None),
        ),
        out_specs=(
            P(("wide", "narrow"), None),
            P(("wide", "narrow"), None),
            P(None, "wide", "narrow"),
            P("narrow", "wide"),
            P("wide", "narrow"),
            P("narrow"),
            P("narrow", "wide"),
            P(),
            P(),
            P(),
            P(),
        ),
        check_vma=False,
    )
```

```python
import functools
import math

import jax
import jax.numpy as jnp
from jax import lax
from jax.experimental import pallas as pl
from jax.experimental.pallas import tpu as pltpu
from jax.sharding import PartitionSpec as P

HEAD_DIM = 80
LEN = 2048
WINDOW = 1024
BLOCK = 512
NDOC = 4
TILE = 256

LOG_TWO_E = 1.4426950408889634
EPSILON = 1e-06
NEG_FILL = -1e30

F32 = jnp.float32
LOW = jnp.bfloat16
MESH = pl.DeviceIdType.MESH
VMEM_LIMIT = 63 * 2**20


def group_rows(values):
    return lax.all_gather(values, "narrow", axis=0, tiled=True)


def group_parts(values):
    return lax.psum_scatter(values, "narrow", scatter_dimension=0, tiled=True)


def contract_last(left, right):
    return lax.dot_general(
        left, right, (((1,), (1,)), ((), ())), preferred_element_type=jnp.float32
    )


def contract_first(left, right):
    return lax.dot_general(
        left, right, (((0,), (0,)), ((), ())), preferred_element_type=jnp.float32
    )


def norm_share(inputs, norm_gain):
    inverse = lax.rsqrt(jnp.mean(inputs * inputs, axis=1) + EPSILON)
    normed = inputs * inverse[:, None]
    return (inverse, normed, (normed * norm_gain).astype(jnp.bfloat16))


def norm_back(grad_normal, norm_gain, inverse, normed):
    scaled = grad_normal * norm_gain
    inner_dots = jnp.mean(scaled * normed, axis=1)
    grad_inputs = inverse[:, None] * (scaled - normed * inner_dots[:, None])
    return (grad_inputs, jnp.sum(grad_normal * normed, axis=0))


def segment_ids(lengths_row):
    positions = jnp.arange(LEN, dtype=jnp.int32)
    ends = jnp.cumsum(lengths_row)
    return jnp.sum((positions[:, None] >= ends[None, :]).astype(jnp.int32), axis=1)


def block_mask(segments, padded_seg, offset):
    query_pos = offset + jnp.arange(BLOCK, dtype=jnp.int32)
    key_pos = offset - WINDOW + jnp.arange(WINDOW + BLOCK, dtype=jnp.int32)
    query_seg = segments[offset : offset + BLOCK]
    key_seg = padded_seg[offset : offset + WINDOW + BLOCK]
    spacing = query_pos[:, None] - key_pos[None, :]
    same_doc = query_seg[:, None] == key_seg[None, :]
    inside = (spacing >= 0) & (spacing < WINDOW)
    real_doc = (query_seg[:, None] < NDOC) | (spacing == 0)
    return same_doc & inside & real_doc


def padded_inputs(keys_in, values_in, segments):
    pad_rows = jnp.zeros((WINDOW,) + keys_in.shape[1:], keys_in.dtype)
    keys_pad = jnp.concatenate([pad_rows, keys_in], axis=0)
    values_pad = jnp.concatenate([pad_rows, values_in], axis=0)
    padded_seg = jnp.concatenate([jnp.full((WINDOW,), -2, jnp.int32), segments])
    return (keys_pad, values_pad, padded_seg)


def attend_forward(queries, keys_in, values_in, segments):
    keys_pad, values_pad, padded_seg = padded_inputs(keys_in, values_in, segments)
    outputs = []
    logsums = []
    for block_index in range(LEN // BLOCK):
        offset = block_index * BLOCK
        query_block = queries[offset : offset + BLOCK]
        key_block = keys_pad[offset : offset + WINDOW + BLOCK]
        value_block = values_pad[offset : offset + WINDOW + BLOCK]
        allowed = block_mask(segments, padded_seg, offset)
        scores = jnp.einsum(
            "ihd,jhd->hij", query_block, key_block, preferred_element_type=jnp.float32
        )
        masked = jnp.where(allowed[None], scores, NEG_FILL)
        maxima = jnp.max(masked, axis=2)
        exponent = jnp.exp(masked - maxima[:, :, None])
        totals = jnp.sum(exponent, axis=2)
        probs_low = (exponent / totals[:, :, None]).astype(jnp.bfloat16)
        block_out = jnp.einsum(
            "hij,jhd->ihd", probs_low, value_block, preferred_element_type=jnp.float32
        )
        outputs.append(block_out.astype(jnp.bfloat16))
        logsums.append(maxima + jnp.log(totals))
    return (jnp.concatenate(outputs, axis=0), jnp.concatenate(logsums, axis=1))


def attend_backward(queries, keys_in, values_in, segments, logsum, grad_out):
    keys_pad, values_pad, padded_seg = padded_inputs(keys_in, values_in, segments)
    grad_keys = jnp.zeros(keys_pad.shape, jnp.float32)
    grad_values = jnp.zeros(values_pad.shape, jnp.float32)
    grad_queries = []
    for block_index in range(LEN // BLOCK):
        offset = block_index * BLOCK
        query_block = queries[offset : offset + BLOCK]
        key_block = keys_pad[offset : offset + WINDOW + BLOCK]
        value_block = values_pad[offset : offset + WINDOW + BLOCK]
        grad_block = grad_out[offset : offset + BLOCK]
        allowed = block_mask(segments, padded_seg, offset)
        scores = jnp.einsum(
            "ihd,jhd->hij", query_block, key_block, preferred_element_type=jnp.float32
        )
        masked = jnp.where(allowed[None], scores, NEG_FILL)
        soft_probs = jnp.exp(masked - logsum[:, offset : offset + BLOCK, None])
        probs_low = soft_probs.astype(jnp.bfloat16)
        grad_probs = jnp.einsum(
            "ihd,jhd->hij", grad_block, value_block, preferred_element_type=jnp.float32
        )
        inner_sums = jnp.sum(soft_probs * grad_probs, axis=2)
        grad_scores = (soft_probs * (grad_probs - inner_sums[:, :, None])).astype(jnp.bfloat16)
        grad_queries.append(
            jnp.einsum("hij,jhd->ihd", grad_scores, key_block, preferred_element_type=jnp.float32)
        )
        key_terms = jnp.einsum(
            "hij,ihd->jhd", grad_scores, query_block, preferred_element_type=jnp.float32
        )
        value_terms = jnp.einsum(
            "hij,ihd->jhd", probs_low, grad_block, preferred_element_type=jnp.float32
        )
        grad_keys = grad_keys.at[offset : offset + WINDOW + BLOCK].add(key_terms)
        grad_values = grad_values.at[offset : offset + WINDOW + BLOCK].add(value_terms)
    return (jnp.concatenate(grad_queries, axis=0), grad_keys[WINDOW:], grad_values[WINDOW:])


def silu_slope(hidden_pre):
    sigmoid_pre = jax.nn.sigmoid(hidden_pre)
    return sigmoid_pre * (1.0 + hidden_pre * (1.0 - sigmoid_pre))


def general_device(
    tokens,
    lengths,
    qkv_weight,
    out_weight,
    up_weight,
    up_bias,
    down_weight,
    down_bias,
    attn_gain,
    mlp_gain,
    query_scale,
    cotangent,
):
    head_count = qkv_weight.shape[2] // HEAD_DIM
    seq_count = lengths.shape[0]
    row_count = seq_count * LEN

    def by_sequence(values):
        return values.reshape((seq_count, LEN) + values.shape[1:])

    qkv_full, out_full, up_full, down_full = (
        lax.all_gather(qkv_weight, "wide", axis=1, tiled=True),
        lax.all_gather(out_weight, "wide", axis=1, tiled=True),
        lax.all_gather(up_weight, "wide", axis=0, tiled=True),
        lax.all_gather(down_weight, "wide", axis=1, tiled=True),
    )
    segments = jax.vmap(segment_ids)(lengths)
    inputs = tokens.astype(jnp.float32)
    inverse_one, normed_one, normal_one = norm_share(inputs, attn_gain)
    rows_one = group_rows(normal_one)
    projected = jnp.einsum("td,cdn->ctn", rows_one, qkv_full, preferred_element_type=jnp.float32)
    scale_dim = LOG_TWO_E / math.sqrt(HEAD_DIM) * jax.nn.softplus(query_scale)
    query_heads = projected[0].reshape(row_count, head_count, HEAD_DIM)
    query_low = (query_heads * scale_dim).astype(jnp.bfloat16)
    key_low = projected[1].astype(jnp.bfloat16).reshape(row_count, head_count, HEAD_DIM)
    value_low = projected[2].astype(jnp.bfloat16).reshape(row_count, head_count, HEAD_DIM)
    attended, logsum = jax.vmap(attend_forward)(
        by_sequence(query_low), by_sequence(key_low), by_sequence(value_low), segments
    )
    attended_rows = attended.reshape(row_count, head_count * HEAD_DIM)
    middle = inputs + group_parts(
        jnp.dot(attended_rows, out_full, preferred_element_type=jnp.float32)
    )
    inverse_two, normed_two, normal_two = norm_share(middle, mlp_gain)
    grad_down_bias = jnp.sum(cotangent.astype(jnp.float32), axis=0)
    rows_two = group_rows(normal_two)
    hidden_pre = jnp.dot(rows_two, up_full, preferred_element_type=jnp.float32) + up_bias
    hidden_low = jax.nn.silu(hidden_pre).astype(jnp.bfloat16)
    branch_two = (
        group_parts(jnp.dot(hidden_low, down_full, preferred_element_type=jnp.float32)) + down_bias
    )
    result = middle + branch_two
    grad_rows = group_rows(cotangent)
    grad_hidden = contract_last(grad_rows, down_full)
    grad_pre = (grad_hidden * silu_slope(hidden_pre)).astype(jnp.bfloat16)
    grad_up = contract_first(rows_two, grad_pre)
    grad_down = contract_first(hidden_low, grad_rows)
    grad_up_bias = jnp.sum(grad_pre.astype(jnp.float32), axis=0)
    grad_normal_two = group_parts(contract_last(grad_pre, up_full))
    grad_middle_norm, grad_mlp_gain = norm_back(grad_normal_two, mlp_gain, inverse_two, normed_two)
    grad_middle = cotangent.astype(jnp.float32) + grad_middle_norm
    grad_branch = group_rows(grad_middle.astype(jnp.bfloat16))
    grad_attended = contract_last(grad_branch, out_full).astype(jnp.bfloat16)
    grad_out = contract_first(attended_rows, grad_branch)
    grad_scaled, grad_key, grad_value = jax.vmap(attend_backward)(
        by_sequence(query_low),
        by_sequence(key_low),
        by_sequence(value_low),
        segments,
        logsum,
        by_sequence(grad_attended.reshape(row_count, head_count, HEAD_DIM)),
    )
    grad_scaled = grad_scaled.reshape(row_count, head_count, HEAD_DIM)
    grad_scale_part = (
        jnp.sum(grad_scaled * query_heads, axis=(0, 1))
        * (LOG_TWO_E / math.sqrt(HEAD_DIM))
        * jax.nn.sigmoid(query_scale)
    )
    grad_projected = jnp.stack(
        [
            (grad_scaled * scale_dim).reshape(row_count, head_count * HEAD_DIM),
            grad_key.reshape(row_count, head_count * HEAD_DIM),
            grad_value.reshape(row_count, head_count * HEAD_DIM),
        ]
    ).astype(jnp.bfloat16)
    grad_qkv = jnp.einsum(
        "td,ctn->cdn", rows_one, grad_projected, preferred_element_type=jnp.float32
    )
    grad_normal_one = group_parts(
        jnp.einsum("ctn,cdn->td", grad_projected, qkv_full, preferred_element_type=jnp.float32)
    )
    grad_input_norm, grad_attn_gain = norm_back(grad_normal_one, attn_gain, inverse_one, normed_one)
    grad_tokens = grad_middle + grad_input_norm
    grad_qkv, grad_out, grad_up, grad_down = (
        lax.psum_scatter(grad_qkv, "wide", scatter_dimension=1, tiled=True),
        lax.psum_scatter(grad_out, "wide", scatter_dimension=1, tiled=True),
        lax.psum_scatter(grad_up, "wide", scatter_dimension=0, tiled=True),
        lax.psum_scatter(grad_down, "wide", scatter_dimension=1, tiled=True),
    )
    grad_attn_gain, grad_mlp_gain, grad_down_bias, grad_scale = lax.psum(
        (grad_attn_gain, grad_mlp_gain, grad_down_bias, grad_scale_part), ("wide", "narrow")
    )
    grad_up_bias = lax.psum(grad_up_bias, "wide")
    return (
        result.astype(jnp.bfloat16),
        grad_tokens,
        grad_qkv,
        grad_out,
        grad_up,
        grad_up_bias,
        grad_down,
        grad_down_bias,
        grad_attn_gain,
        grad_mlp_gain,
        grad_scale,
    )


def product(left, right, left_dim=1, right_dim=0):
    return lax.dot_general(
        left, right, (((left_dim,), (right_dim,)), ((), ())), preferred_element_type=F32
    )


def flip(value, mask):
    bit = 1
    while bit <= mask:
        if mask & bit:
            value = value + bit * (1 - 2 * lax.rem(lax.div(value, bit), 2))
        bit *= 2
    return value


def part(start, size):
    return pl.ds(pl.multiple_of(start * size, size), size)


def chunks(total, size, body):
    def step(index, carry):
        body(part(index, size))
        return carry

    lax.fori_loop(0, total // size, step, 0)


def add_rows(target, source, size):
    def body(span):
        target[span, :] = (target[span, :].astype(F32) + source[span, :].astype(F32)).astype(LOW)

    chunks(source.shape[0], size, body)


class Place:
    def __init__(self, group):
        self.wide = lax.axis_index("wide")
        self.narrow = lax.axis_index("narrow")
        self.core = lax.rem(self.wide, 2)
        self.y = lax.div(self.wide, 2)
        self.quarter = lax.rem(self.narrow, group)
        self.half = lax.div(self.narrow, group)
        self.x = lax.rem(self.narrow, 2)
        self.z = lax.div(self.quarter, 2)
        self.column = lax.div(self.narrow, 2)
        self.collector = self.core == self.z

    def along_wide(self, mask):
        return (flip(self.wide, mask), self.narrow)

    def along_narrow(self, mask):
        return (self.wide, flip(self.narrow, mask))

    def at(self, core, narrow):
        return (self.y * 2 + core, narrow)


def greet(place, group):
    barrier = pltpu.get_barrier_semaphore()
    peers = [place.along_narrow(m) for m in range(1, 2 * group)]
    peers += [place.along_wide(m) for m in (1, 2, 3)]
    peers += [(flip(place.wide, 1), flip(place.narrow, m)) for m in range(1, group + 1)]
    for peer in peers:
        pl.semaphore_signal(barrier, inc=1, device_id=peer, device_id_type=MESH)
    pl.semaphore_wait(barrier, len(peers))


class Wires:
    def __init__(self, send_sem, recv_sem):
        self.send_sem, self.recv_sem = send_sem, recv_sem
        self.next_id = 0
        self.sent = []

    def ids(self, count):
        first = self.next_id
        self.next_id += count
        assert self.next_id <= self.send_sem.shape[0]
        return first

    def copy(self, source, target, device, index, arrival=None):
        return pltpu.make_async_remote_copy(
            src_ref=source,
            dst_ref=target,
            send_sem=self.send_sem.at[index],
            recv_sem=self.recv_sem.at[index if arrival is None else arrival],
            device_id=device,
            device_id_type=MESH,
        )

    def exchange(self, source, target, incoming, device):
        index = self.ids(1)
        out = self.copy(source, target, device, index)
        out.start()
        self.sent.append((None, lambda: out))
        return self.copy(incoming, incoming, device, index)

    def trade(self, make):
        index = self.ids(1)

        def out():
            source, target, device = make()
            return self.copy(source, target, device, index)

        out().start()
        self.sent.append((None, out))

        def arrive():
            _, target, device = make()
            self.copy(target, target, device, index).wait_recv()

        return arrive

    def start_if(self, condition, make):
        pl.when(condition)(lambda: make().start())
        self.sent.append((condition, make))

    def finish(self):
        for condition, make in self.sent:
            if condition is None:
                make().wait_send()
            else:
                pl.when(condition)(lambda make=make: make().wait_send())


def wait_if(condition, make):
    pl.when(condition)(lambda: make().wait_recv())


def ends_row(lengths, row):
    lane = lax.broadcasted_iota(jnp.int32, (8, 128), 1)
    result, total = jnp.zeros((8, 128), jnp.int32), 0
    for index in range(NDOC):
        total = total + lengths[row, index]
        result = jnp.where(lane == index, total, result)
    return result.astype(F32)


def document_ends(row):
    return [
        jnp.broadcast_to(row[0:1, k : k + 1], (1, TILE)).astype(jnp.int32) for k in range(NDOC)
    ]


def first_key(ends, offset):
    position = offset + lax.broadcasted_iota(jnp.int32, (1, TILE), 1)
    start = jnp.zeros_like(position)
    for end in ends:
        start = jnp.where(position >= end, end, start)
    start = jnp.maximum(start, position - (WINDOW - 1))
    return jnp.where(position >= ends[-1], position, start), position


def allowed_scores(scores, key_start, offset, first, position):
    key = key_start + lax.broadcasted_iota(jnp.int32, scores.shape, 0)
    allowed = key >= first
    if key_start + scores.shape[0] > offset:
        allowed = allowed & (key <= position)
    return jnp.where(allowed, scores, NEG_FILL)


def tile_keys(tile):
    offset = tile * TILE
    return offset, range(max(0, offset - WINDOW), offset + TILE, TILE)


def pipelined(tiles, first_half, second_half):
    waiting = None
    for tile in tiles:
        current = (tile, first_half(tile))
        if waiting is not None:
            second_half(*waiting)
        waiting = current
    second_half(*waiting)


def attend_head(head, ends, queries, keys, values_t, attended, logsum):
    def first_half(tile):
        offset, starts = tile_keys(tile)
        first, position = first_key(ends, offset)
        query = queries[head, :, offset : offset + TILE]
        blocks, maxima = [], None
        for start in starts:
            scores = product(keys[head, start : start + TILE, :], query)
            scores = allowed_scores(scores, start, offset, first, position)
            top = jnp.max(scores, axis=0, keepdims=True)
            maxima = top if maxima is None else jnp.maximum(maxima, top)
            blocks.append(scores)
        return blocks, maxima

    def second_half(tile, held):
        blocks, maxima = held
        offset, starts = tile_keys(tile)
        total, output = None, None
        for scores, start in zip(blocks, starts):
            exponent = jnp.exp(scores - maxima)
            share = jnp.sum(exponent, axis=0, keepdims=True)
            term = product(values_t[head, :, start : start + TILE], exponent.astype(LOW))
            total, output = (
                (share, term) if total is None else (total + share, output + term)
            )
        attended[head, :, offset : offset + TILE] = (output * (1.0 / total)).astype(LOW)
        logsum[head, :, offset : offset + TILE] = maxima + jnp.log(total)

    pipelined(range(LEN // TILE), first_half, second_half)


def norm_rows(inputs):
    return lax.rsqrt(jnp.mean(inputs * inputs, axis=1, keepdims=True) + EPSILON)


def column(row, count):
    return jnp.broadcast_to(row, (128, 128)).T[:count, :1]


GATHER_ORDERS = ("fzy", "fzy", "zfy", "fyxz", "fxzy", "zfxy")


def forward_kernel(
    group,
    lengths,
    tokens,
    shards,
    params,
    cotangent,
    x_out,
    normal_out,
    qf_out,
    q_out,
    kt_out,
    kn_out,
    vn_out,
    wq_out,
    lse_out,
    result_out,
    middle_out,
    att_out,
    wm_out,
    sums,
    ends_out,
    x_all,
    normal,
    w_qkv,
    w_mlp,
    w_pair,
    w_half,
    bias_all,
    bias_row,
    ends_own,
    ends_other,
    query_full,
    query_t,
    key_t,
    value_t,
    key_n,
    value_n,
    logsum,
    attended,
    att_all,
    grad_att,
    grad_middle,
    send_sem,
    recv_sem,
    local_sem,
):
    place = Place(group)
    core, y, quarter, narrow = place.core, place.y, place.quarter, place.narrow
    collector = place.collector
    other_core = jnp.logical_not(collector)
    rows = tokens.shape[0]
    mid = rows // 2
    slab2 = shards.shape[1]
    slab = slab2 // 2
    pair_cols = 2 * shards.shape[2]
    cols_y = part(y, pair_cols)
    cols_other = part(1 - y, pair_cols)
    x_dev, z_dev, far_dev = (
        place.along_narrow(1),
        place.along_narrow(2),
        place.along_narrow(group),
    )
    core_dev, y_dev = place.along_wide(1), place.along_wide(2)
    wires = Wires(send_sem, recv_sem)
    exchange = wires.exchange
    gain_one, gain_two, down_bias = params[0:1, :], params[1:2, :], params[2:3, :]

    greet(place, group)

    halves = (slice(0, mid), slice(mid, rows))

    def x_part(mask, which):
        return x_all.at[flip(quarter, mask), halves[which]]

    x_first, z_first, on_first, core_first = (
        wires.ids(2),
        wires.ids(2),
        wires.ids(2),
        wires.ids(5),
    )

    def x_own(which):
        return wires.copy(tokens.at[halves[which]], x_part(0, which), x_dev, x_first + which)

    def x_in(which):
        return wires.copy(x_part(1, which), x_part(1, which), x_dev, x_first + which)

    def z_own(which):
        return wires.copy(tokens.at[halves[which]], x_part(0, which), z_dev, z_first + which)

    def z_in(which):
        return wires.copy(x_part(2, which), x_part(2, which), z_dev, z_first + which)

    def on_out(which):
        return wires.copy(x_part(2, which), x_part(2, which), x_dev, on_first + which)

    def on_in(which):
        return wires.copy(x_part(3, which), x_part(3, which), x_dev, on_first + which)

    def core_copy(index, mask, which=None):
        there = x_all.at[flip(quarter, mask)] if which is None else x_part(mask, which)
        source = tokens if mask == 0 else there
        return wires.copy(source, there, core_dev, core_first + index)

    w_arrived = exchange(shards.at[:, part(1 - core, slab), :], w_half, w_half, core_dev)
    for which in range(2):
        wires.start_if(collector, lambda which=which: x_own(which))
        wires.start_if(other_core, lambda which=which: z_own(which))
    ends_own[...] = ends_row(lengths, place.half)
    ends_from = exchange(ends_own, ends_other, ends_other, core_dev)
    wires.start_if(collector, lambda: core_copy(0, 0))
    bias_all[narrow] = jnp.broadcast_to(params[3:4, :slab2], bias_all.shape[1:])
    bias_from = [
        exchange(
            bias_all.at[narrow],
            bias_all.at[narrow],
            bias_all.at[flip(narrow, mask)],
            place.along_narrow(mask),
        )
        for mask in range(1, 2 * group)
    ]

    @pl.when(collector)
    def _():
        x_all[quarter] = tokens[...]

    w_arrived.wait_recv()
    own = shards[:, part(core, slab), :]
    other = w_half[...]
    w_pair[:, :, : pair_cols // 2] = jnp.where(core == 0, own, other)
    w_pair[:, :, pair_cols // 2 :] = jnp.where(core == 0, other, own)
    for m in range(3):
        w_qkv[m, place.column, :, cols_y] = w_pair[m]
        w_mlp[m, core, part(narrow, slab), cols_y] = w_pair[3 + m]

    masks = {"x": 1, "z": 2, "f": group}
    devices = {"x": x_dev, "z": z_dev, "f": far_dev, "y": y_dev}

    def block(m, mask, columns):
        where = flip(narrow, mask)
        columns = {"own": cols_y, "other": cols_other, "both": slice(None)}[columns]
        if m < 3:
            return w_qkv.at[m, lax.div(where, 2), :, columns]
        return w_mlp.at[m - 3, core, part(where, slab), columns]

    def whole(m, columns):
        if m < 3:
            return w_qkv.at[m, :, :, columns]
        return w_mlp.at[m - 3, core, :, columns]

    held = [{0: "own"} for _ in range(6)]
    gathered = [[] for _ in range(6)]
    turned = {"own": "other", "other": "own", "both": "both"}

    def arrive(m):
        for one in gathered[m]:
            one.wait_recv()
        gathered[m] = []

    def gather(m, stage):
        arrive(m)
        order = GATHER_ORDERS[m]
        if stage == len(order):
            gathered[m] = [
                exchange(
                    w_mlp.at[m - 3, core],
                    w_mlp.at[m - 3, core],
                    w_mlp.at[m - 3, 1 - core],
                    core_dev,
                )
            ]
            return
        way = order[stage]
        device = devices[way]
        if way == "y" and stage == len(order) - 1:
            mine = whole(m, cols_y)
            gathered[m] = [exchange(mine, mine, whole(m, cols_other), device)]
            return
        more = {}
        for mask, columns in held[m].items():
            mine = block(m, mask, columns)
            if way == "y":
                incoming = block(m, mask, turned[columns])
                more[mask] = "both"
            else:
                incoming = block(m, mask ^ masks[way], columns)
                more[mask ^ masks[way]] = columns
            gathered[m].append(exchange(mine, mine, incoming, device))
        held[m].update(more)

    scale = jnp.tile(column(params[4:5, :128], HEAD_DIM), (query_t.shape[0], 1))

    def project(mask):
        where = flip(quarter, mask)
        span = part(where, rows)
        inputs = x_all[where].astype(F32)
        normal[where] = (inputs * norm_rows(inputs) * gain_one).astype(LOW)
        weight = w_qkv[...].reshape(-1, inputs.shape[1])
        out = product(weight, normal[where], 1, 1)
        size = out.shape[0] // 3
        heads = size // HEAD_DIM
        query_full[:, span] = out[:size]
        query_t[:, :, span] = (out[:size] * scale).astype(LOW).reshape(heads, HEAD_DIM, rows)
        key = out[size : 2 * size].astype(LOW).reshape(heads, HEAD_DIM, rows)
        value = out[2 * size :].astype(LOW).reshape(heads, HEAD_DIM, rows)
        key_t[:, :, span] = key
        value_t[:, :, span] = value
        for head in range(heads):
            key_n[head, span, :] = key[head].T
            value_n[head, span, :] = value[head].T

    stores = []

    def store(source, target):
        one = pltpu.make_async_copy(source, target, local_sem.at[len(stores)])
        one.start()
        stores.append(one)

    heads = query_t.shape[0]
    att_first = wires.ids(4 * heads)

    def att_send(head, mask):
        peer = flip(quarter, mask)
        return wires.copy(
            attended.at[head, :, part(peer, rows)],
            att_all.at[core, head, place.x],
            place.at(place.z, flip(narrow, mask)),
            att_first + mask * heads + head,
            att_first + (core * 2 + place.x) * heads + head,
        )

    def att_in(head, from_core, from_x):
        there = att_all.at[from_core, head, from_x]
        return wires.copy(there, there, core_dev, att_first + (from_core * 2 + from_x) * heads + head)

    def one_head(head, carry):
        attend_head(head, ends, query_t, key_n, value_t, attended, logsum)
        for mask in (3, 1, 2):
            att_send(head, mask).start()

        @pl.when(collector)
        def _():
            att_all[core, head, place.x] = attended[head, :, part(quarter, rows)]

        pl.when(other_core)(lambda: att_send(head, 0).start())
        return carry

    def pass_on(which):
        wait_if(collector, lambda: z_in(which))
        wires.start_if(collector, lambda: on_out(which))
        wires.start_if(collector, lambda: core_copy(2 + which, 2, which))

    gather(3, 0)
    gather(0, 0)
    pass_on(0)
    for which in range(2):
        wait_if(collector, lambda which=which: x_in(which))
    wires.start_if(collector, lambda: core_copy(1, 1))
    gather(1, 0)
    gather(4, 0)
    gather(1, 1)
    gather(0, 1)
    gather(2, 0)
    gather(3, 1)
    gather(5, 0)
    gather(4, 1)
    gather(3, 2)
    gather(1, 2)
    gather(4, 2)
    gather(2, 1)
    pass_on(1)
    gather(0, 2)
    gather(2, 2)
    gather(5, 1)
    ends_from.wait_recv()
    ends_out[...] = jnp.where(collector, ends_own[...], ends_other[...])
    ends = document_ends(ends_out)
    for m in range(3):
        arrive(m)
    gather(3, 3)
    for which in range(2):
        wait_if(collector, lambda which=which: on_in(which))
    wires.start_if(collector, lambda: core_copy(4, 3))
    gather(4, 3)
    wait_if(other_core, lambda: core_copy(0, 0))
    project(0)
    wait_if(other_core, lambda: core_copy(1, 1))
    project(1)
    gather(5, 2)
    for which in range(2):
        wait_if(other_core, lambda which=which: core_copy(2 + which, 2, which))
    project(2)
    wait_if(other_core, lambda: core_copy(4, 3))
    project(3)
    gather(5, 3)
    store(x_all, x_out)
    store(normal, normal_out)
    store(query_full, qf_out)
    store(query_t, q_out)
    store(key_t, kt_out)
    store(key_n, kn_out)
    store(value_n, vn_out)
    store(w_qkv, wq_out)
    lax.fori_loop(0, 2, one_head, 0)
    gather(4, 4)
    lax.fori_loop(2, 3, one_head, 0)
    gather(3, 4)
    lax.fori_loop(3, heads, one_head, 0)
    store(logsum, lse_out)

    cot = cotangent[...]
    cot_full = cot.astype(F32)
    sums[...] = jnp.zeros_like(sums)
    sums[1:2, :] = jnp.sum(cot_full, axis=0, keepdims=True)
    for one in bias_from:
        one.wait_recv()
    for c in range(2):
        for n in range(2 * group):
            start = (c * 2 * group + n) * slab
            bias_row[0:1, start : start + slab] = bias_all[n, 0:1, c * slab : (c + 1) * slab]

    def finish_head(head, carry):
        for from_core in range(2):
            for from_x in range(2):
                local = collector & (core == from_core) & (place.x == from_x)
                wait_if(
                    jnp.logical_not(local),
                    lambda from_core=from_core, from_x=from_x: att_in(head, from_core, from_x),
                )
        return carry

    lax.fori_loop(0, heads, finish_head, 0)
    arrive(3)

    size = 2 * w_mlp.shape[2]
    grad_shape = w_mlp.shape[1:]

    def weight(m):
        return w_mlp[m].reshape(size, -1)

    att = att_all[...].reshape(size, rows)
    middle = tokens[...].astype(F32) + product(att, weight(0), 0, 0)
    inverse = norm_rows(middle)
    normed = middle * inverse
    normal_two = (normed * gain_two).astype(LOW)
    arrive(4)
    gather(5, 4)
    pre = product(normal_two, weight(1), 1, 1) + bias_row[...]
    gate = 1.0 / (1.0 + jnp.exp(-pre))
    hidden = (pre * gate).astype(LOW)
    arrive(5)

    def finish_send(head, carry):
        for mask in (1, 2, 3):
            att_send(head, mask).wait_send()
        pl.when(other_core)(lambda: att_send(head, 0).wait_send())
        return carry

    lax.fori_loop(0, heads, finish_send, 0)
    wires.finish()
    stores[0].wait()
    grad_hidden = product(cot, weight(2), 1, 1)
    grad_pre = (grad_hidden * (gate * (1.0 + pre * (1.0 - gate)))).astype(LOW)
    grad_normal = product(grad_pre, weight(1))
    scaled = grad_normal * gain_two
    inner = jnp.mean(scaled * normed, axis=1, keepdims=True)
    grad_middle[...] = cot_full + inverse * (scaled - normed * inner)
    store(grad_middle, middle_out)
    branch = grad_middle[...].astype(LOW)
    grad_att[...] = product(weight(0), branch, 1, 1).astype(LOW).reshape(grad_att.shape)
    store(grad_att, att_out)
    x_all[0] = (middle + (product(hidden, weight(2)) + down_bias)).astype(LOW)
    store(x_all.at[0], result_out)

    w_mlp[0] = product(att, branch).astype(LOW).reshape(grad_shape)
    store(w_mlp.at[0], wm_out.at[0])
    w_mlp[1] = product(grad_pre, normal_two, 0, 0).astype(LOW).reshape(grad_shape)
    store(w_mlp.at[1], wm_out.at[1])
    w_mlp[2] = product(hidden, cot, 0, 0).astype(LOW).reshape(grad_shape)
    store(w_mlp.at[2], wm_out.at[2])
    sums[0:1, :] = jnp.sum(grad_normal * normed, axis=0, keepdims=True)
    sums[2:3, :] = jnp.sum(grad_pre.astype(F32), axis=0, keepdims=True)
    for one in stores[1:]:
        one.wait()


def backward_head(
    head,
    ends,
    queries,
    query_full,
    keys,
    keys_t,
    values,
    grad_out,
    logsum,
    scale,
    grads_t,
    sum_keys,
    sum_values,
    sum_scale,
    halfway,
):
    sum_keys[...] = jnp.zeros_like(sum_keys)
    sum_values[...] = jnp.zeros_like(sum_values)

    def first_half(tile):
        offset, starts = tile_keys(tile)
        first, position = first_key(ends, offset)
        span = slice(offset, offset + TILE)
        query, grad, log_row = queries[head, :, span], grad_out[head, :, span], logsum[head, :, span]
        blocks, inner = [], None
        for start in starts:
            scores = product(keys[head, start : start + TILE, :], query)
            scores = allowed_scores(scores, start, offset, first, position)
            probs = jnp.exp(scores - log_row)
            grad_probs = product(values[head, start : start + TILE, :], grad)
            share = jnp.sum(probs * grad_probs, axis=0, keepdims=True)
            inner = share if inner is None else inner + share
            blocks.append((probs, grad_probs))
        return blocks, inner, query, grad

    def second_half(tile, held):
        blocks, inner, query, grad = held
        offset, starts = tile_keys(tile)
        span = slice(offset, offset + TILE)
        grad_scaled = None
        for (probs, grad_probs), start in zip(blocks, starts):
            there = slice(start, start + TILE)
            grad_scores = (probs * (grad_probs - inner)).astype(LOW)
            term = product(keys_t[head, :, there], grad_scores)
            grad_scaled = term if grad_scaled is None else grad_scaled + term
            sum_keys[:, there] += product(query, grad_scores, 1, 1)
            sum_values[:, there] += product(grad, probs.astype(LOW), 1, 1)
        grads_t[0, head, :, span] = (grad_scaled * scale).astype(LOW)
        terms = grad_scaled * query_full[part(head, HEAD_DIM), span]
        sum_scale[...] += terms[:, : TILE // 2] + terms[:, TILE // 2 :]

    count = LEN // TILE
    pipelined(range(count // 2), first_half, second_half)
    halfway()
    pipelined(range(count // 2, count), first_half, second_half)
    grads_t[1, head] = sum_keys[...].astype(LOW)
    grads_t[2, head] = sum_values[...].astype(LOW)


SCATTER_ORDERS = ("yxzf", "xyzf", "zyxf")


def backward_kernel(
    group,
    ends_in,
    tokens,
    params,
    sums,
    grad_middle,
    grad_own,
    w_grads,
    x_in,
    normal_in,
    query_full,
    query_t,
    key_t,
    key_n,
    value_n,
    w_qkv_in,
    logsum,
    tokens_out,
    mlp_out,
    qkv_out,
    sums_out,
    normal,
    grad_att,
    grads_t,
    sum_keys,
    sum_values,
    sum_scale,
    w_own,
    w_core,
    w_y,
    w_eight,
    w_four,
    w_two,
    w_last,
    dx_own,
    dx_core,
    dx_x,
    dx_last,
    w_qkv,
    dw,
    dw_y,
    dw_z_in,
    dw_far,
    dw_last,
    all_sums,
    got_sums,
    send_sem,
    recv_sem,
    local_sem,
):
    place = Place(group)
    core, y, quarter, narrow = place.core, place.y, place.quarter, place.narrow
    collector = place.collector
    other_core = jnp.logical_not(collector)
    rows = tokens.shape[0]
    mid = rows // 2
    slab = qkv_out.shape[2]
    cols = qkv_out.shape[3]
    pair_cols = 2 * cols
    cols_y = part(y, pair_cols)
    cols_other = part(1 - y, pair_cols)
    x_dev, z_dev, far_dev = (
        place.along_narrow(1),
        place.along_narrow(2),
        place.along_narrow(group),
    )
    core_dev, y_dev = place.along_wide(1), place.along_wide(2)
    wires = Wires(send_sem, recv_sem)
    gain = params[0:1, :]
    scale = column(params[4:5, :128], HEAD_DIM)
    dxs = w_core

    trade = wires.trade

    greet(place, group)

    heads = query_t.shape[0]
    att_first = wires.ids(4 * heads)

    def att_out(head, to_core, to_x):
        target = place.half * group + core * 2 + to_x
        return wires.copy(
            grad_own.at[to_core, head, to_x],
            grad_att.at[head, :, part(quarter, rows)],
            place.at(to_core, target),
            att_first + (to_core * 2 + to_x) * heads + head,
            att_first + quarter * heads + head,
        )

    def att_local(to_core, to_x):
        return collector & (core == to_core) & (place.x == to_x)

    def att_in(head, mask):
        peer = flip(quarter, mask)
        there = grad_att.at[head, :, part(peer, rows)]
        return wires.copy(there, there, core_dev, att_first + peer * heads + head)

    def block_at(index, row):
        low = 1 - lax.div(index, 2)
        high = lax.rem(index + 1, 2) * lax.div(index, 2) + lax.rem(index, 2) * low
        row = jnp.where(low == 1, flip(row, 1), row)
        return jnp.where(high == 1, flip(row, 2), row)

    def head_at(index):
        return block_at(jnp.int32(index), place.column)

    for index in range(heads):
        head = block_at(jnp.int32(index), place.half * 2 + core)
        for to_core in range(2):
            for to_x in range(2):
                pl.when(jnp.logical_not(att_local(to_core, to_x)))(
                    lambda head=head, to_core=to_core, to_x=to_x: att_out(
                        head, to_core, to_x
                    ).start()
                )

        @pl.when(collector)
        def _():
            grad_att[head, :, part(quarter, rows)] = grad_own[core, head, place.x]

    span_m = w_own.shape[1]

    def core_rows(m):
        return slice(m * span_m, (m + 1) * span_m)

    arrived = [None] * 3
    loads = []
    for m in range(3):
        arrived[m] = [
            trade(lambda m=m: (w_grads.at[m, 1 - core], w_core.at[core_rows(m)], core_dev))
        ]
        loads.append(pltpu.make_async_copy(w_grads.at[m, core], w_own.at[m], local_sem.at[m]))
        loads[-1].start()
    late = [
        pltpu.make_async_copy(source, target, local_sem.at[3 + k])
        for k, (source, target) in enumerate(
            ((normal_in, normal), (w_qkv_in, w_qkv), (grad_middle, tokens_out))
        )
    ]
    for one in late:
        one.start()

    masks = {"x": 1, "z": 2, "f": group}
    devices = {"x": x_dev, "z": z_dev, "f": far_dev, "y": y_dev}
    every = tuple(o for o in range(2 * group))
    kept = [every] * 3
    landing = [None] * 3

    def block(m, mask, columns):
        return w_own.at[m, part(flip(narrow, mask), slab), columns]

    def add_to(target, source):
        target[...] = (target[...].astype(F32) + source[...].astype(F32)).astype(LOW)

    def y_rows(m, k):
        start = span_m + (m - 1) * span_m // 2 + k * slab
        return w_y.at[start : start + slab]

    def scatter(m, stage):
        for one in arrived[m]:
            one()
        if stage == 0:
            pltpu.make_async_copy(w_grads.at[m, core], w_own.at[m], local_sem.at[m]).wait()
            add_rows(w_own.at[m], w_core.at[core_rows(m)], 128)
        elif SCATTER_ORDERS[m][stage - 1] == "y":
            columns = cols_y
            if stage == 1:
                add_rows(w_own.at[m, :, cols_y], w_y.at[:span_m], 128)
            else:
                for k, mask in enumerate(kept[m]):
                    add_to(block(m, mask, cols_y), y_rows(m, k))
        else:
            width = "y" in SCATTER_ORDERS[m][: stage - 1]
            for k, mask in enumerate(kept[m]):
                columns = cols_y if width else slice(None)
                add_to(block(m, mask, columns), landing[m](k))
        if stage == 4:
            total = w_own[m, part(narrow, slab), cols_y].astype(F32)
            arrived[m] = [last_step(total, mlp_out, m, w_last)]
            return
        way = SCATTER_ORDERS[m][stage]
        if way == "y":
            if stage == 0:
                arrived[m] = [
                    trade(lambda: (w_own.at[m, :, cols_other], w_y.at[:span_m], y_dev))
                ]
            else:
                arrived[m] = [
                    trade(
                        lambda k=k, mask=mask: (
                            block(m, mask, cols_other),
                            y_rows(m, k),
                            y_dev,
                        )
                    )
                    for k, mask in enumerate(kept[m])
                ]
            return
        bit = masks[way]
        width = "y" in SCATTER_ORDERS[m][:stage]
        columns = cols_y if width else slice(None)
        mine = tuple(o for o in kept[m] if not o & bit)
        buffers = {8: w_eight, 4: w_four, 2: w_two}
        buffer = buffers[len(kept[m])]

        def land(k, buffer=buffer, width=width):
            if width and buffer is w_eight:
                return buffer.at[m, k, :, : 2 * cols]
            return buffer.at[m, k]

        arrived[m] = [
            trade(lambda k=k, o=o: (block(m, o | bit, columns), land(k), devices[way]))
            for k, o in enumerate(mine)
        ]
        kept[m] = mine
        landing[m] = land

    def last_step(total, out_ref, m, buffer):
        mine = jnp.where(core == 0, total[:, :cols], total[:, cols:])
        theirs = jnp.where(core == 0, total[:, cols:], total[:, :cols])
        out_ref[m, core] = mine
        buffer[m] = theirs
        return trade(lambda: (buffer.at[m], out_ref.at[m, core], core_dev))

    def column_at(mask):
        return lax.div(flip(narrow, mask), 2)

    def dw_add(where, source):
        there = dw.at[:, where, :, cols_y]
        there[...] = (there[...].astype(F32) + source[...].astype(F32)).astype(LOW)

    def weight_grads(head):
        dw[:, head] = (
            product(
                grads_t[:, head].reshape(3 * HEAD_DIM, LEN), normal[...].reshape(LEN, -1)
            )
            .astype(LOW)
            .reshape(3, HEAD_DIM, -1)
        )

    def dw_y_copy(head, slot):
        return wires.copy(
            dw.at[:, head, :, cols_other], dw_y.at[:, head], y_dev, dw_first + slot
        )

    dw_first = wires.ids(heads)

    def dw_z_step():
        return [
            trade(
                lambda k=k, o=o: (dw.at[:, column_at(o), :, cols_y], dw_z_in.at[:, k], z_dev)
            )
            for k, o in enumerate((2, group + 2))
        ]

    def dw_far_step(came):
        for k in range(2):
            came[k]()
            dw_add(column_at(group * k), dw_z_in.at[:, k])
        return trade(lambda: (dw.at[:, column_at(group), :, cols_y], dw_far, far_dev))

    def dw_last_step(came):
        came()
        last = []
        for m in range(3):
            total = dw[m, place.column, :, cols_y].astype(F32) + dw_far[m].astype(F32)
            last.append(last_step(total, qkv_out, m, dw_last))
        return last

    ends = document_ends(ends_in)
    sum_scale[...] = jnp.zeros_like(sum_scale)

    steps = {}

    def at_step(step, action):
        steps.setdefault(step, []).append(action)

    came = {}

    def rows_in(slot):
        dw_y_copy(head_at(slot), slot).wait_recv()
        dw_add(head_at(slot), dw_y.at[:, head_at(slot)])

    def rows_on():
        came["dw_z"] = dw_z_step()

    at_step((0, 0), lambda: scatter(0, 0))
    at_step((1, 0), lambda: scatter(1, 0))
    at_step((1, 0), lambda: scatter(2, 0))
    at_step((2, 0), lambda: scatter(0, 1))
    at_step((2, 1), lambda: rows_in(0))
    at_step((3, 1), lambda: rows_in(1))
    at_step((3, 1), rows_on)

    def between(index, point):
        for (wanted, where), actions in steps.items():
            if where == point:

                @pl.when(index == wanted)
                def _():
                    for action in actions:
                        action()

    def one_head(index, carry):
        head = head_at(index)
        between(index, 0)
        wait_if(other_core, lambda: att_in(head, 0))
        for mask in range(1, group):
            att_in(head, mask).wait_recv()
        backward_head(
            head,
            ends,
            query_t,
            query_full,
            key_n,
            key_t,
            value_n,
            grad_att,
            logsum,
            scale,
            grads_t,
            sum_keys,
            sum_values,
            sum_scale,
            lambda: between(index, 1),
        )

        @pl.when(index < heads - 1)
        def _():
            weight_grads(head)
            dw_y_copy(head, index).start()

        return carry

    for one in late[:1]:
        one.wait()
    lax.fori_loop(0, heads, one_head, 0)

    size = 3 * heads * HEAD_DIM
    for one in late[1:]:
        one.wait()

    def kept_rows(mask):
        if mask == 0:
            return dx_own
        start = (group + mask - 1) * mid
        return dxs.at[start : start + mid]

    def grad_inputs(mask):
        first = flip(quarter, mask) * 2
        weight = w_qkv[...].reshape(size, -1)

        def half_rows(which):
            span = part(first + which, mid)
            return product(grads_t[:, :, :, span].reshape(size, mid), weight, 0, 0).astype(LOW)

        there = slice(mask * mid, (mask + 1) * mid)
        dxs[there] = half_rows(1 - core)
        out = trade(lambda: (dxs.at[there], dx_core.at[mask], core_dev))
        kept_rows(mask)[...] = half_rows(core)
        return out

    def add_core(mask, came):
        came()
        add_rows(kept_rows(mask), dx_core.at[mask], 128)

    scatter(0, 2)
    scatter(1, 1)
    from_core = {}
    from_core[3] = grad_inputs(3)
    from_core[0] = grad_inputs(0)
    rows_in(2)
    from_core[1] = grad_inputs(1)
    from_core[2] = grad_inputs(2)
    add_core(3, from_core[3])
    from_x3 = trade(lambda: (kept_rows(3), dx_x.at[1], x_dev))
    add_core(0, from_core[0])
    weight_grads(head_at(heads - 1))
    dw_y_copy(head_at(heads - 1), heads - 1).start()
    add_core(1, from_core[1])
    from_x1 = trade(lambda: (kept_rows(1), dx_x.at[0], x_dev))
    scatter(1, 2)
    add_core(2, from_core[2])

    raw = [
        pltpu.make_async_copy(
            x_in.at[flip(quarter, mask), part(core, mid)], dx_core.at[mask], local_sem.at[6 + mask]
        )
        for mask in range(group)
    ]
    for one in raw:
        one.start()
    dw_f = dw_far_step(came["dw_z"])
    rows_in(3)
    scatter(2, 1)
    scatter(0, 3)
    for one in raw:
        one.wait()
    all_sums[0] = sums[...]
    all_sums[0, 3:4, :HEAD_DIM] = jnp.sum(sum_scale[...].T, axis=0, keepdims=True)
    for mask in range(group):

        def gain_rows(span, mask=mask):
            inputs = dx_core[mask, span, :].astype(F32)
            normed = inputs * norm_rows(inputs)
            terms = kept_rows(mask)[span, :].astype(F32) * normed
            all_sums[0, 4:5, :] += jnp.sum(terms, axis=0, keepdims=True)

        chunks(mid, 128, gain_rows)

    sum_devices = [core_dev, place.along_wide(3)] + [
        (flip(place.wide, 1), flip(narrow, mask)) for mask in (1, 2, group)
    ]

    def sum_step(stage):
        return trade(lambda: (all_sums.at[stage], got_sums.at[stage], sum_devices[stage]))

    def sum_add(stage, came):
        came()
        all_sums[stage + 1] = all_sums[stage] + got_sums[stage]

    sums_now = sum_step(0)
    scatter(1, 3)
    last_first = wires.ids(2)

    def last_out():
        return wires.copy(
            kept_rows(2),
            dx_last.at[core],
            place.at(place.z, flip(narrow, 2)),
            last_first,
            last_first + core,
        )

    def last_core():
        return wires.copy(kept_rows(0), dx_last.at[core], core_dev, last_first + 1, last_first + core)

    def last_in(which):
        return wires.copy(dx_last.at[which], dx_last.at[which], core_dev, last_first + which)

    from_x3()
    add_rows(kept_rows(2), dx_x.at[1], 128)
    last_out().start()
    wires.sent.append((None, last_out))
    sum_add(0, sums_now)
    sums_now = sum_step(1)
    sum_add(1, sums_now)
    sums_now = sum_step(2)
    scatter(2, 2)
    scatter(1, 4)
    from_x1()
    add_rows(kept_rows(0), dx_x.at[0], 128)
    own_rows = [
        pltpu.make_async_copy(
            tokens.at[which * mid : (which + 1) * mid], dx_x.at[which], local_sem.at[10 + which]
        )
        for which in range(2)
    ]
    for one in own_rows:
        one.start()
    wires.start_if(other_core, last_core)

    @pl.when(collector)
    def _():
        dx_last[core] = dx_own[...]

    scatter(2, 3)
    scatter(0, 4)
    sum_add(2, sums_now)
    sums_now = sum_step(3)
    for which in range(2):
        wait_if(
            jnp.logical_not(collector & (core == which)), lambda which=which: last_in(which)
        )

    def final_rows(span):
        for which in range(2):
            here = pl.ds(which * mid + span.start, span.size)
            inputs = dx_x[which, span, :].astype(F32)
            inverse = norm_rows(inputs)
            normed = inputs * inverse
            scaled = dx_last[which, span, :].astype(F32) * gain
            inner = jnp.mean(scaled * normed, axis=1, keepdims=True)
            tokens_out[here, :] += inverse * (scaled - normed * inner)

    for one in own_rows:
        one.wait()
    chunks(mid, 128, final_rows)
    sum_add(3, sums_now)
    sums_now = sum_step(4)
    last = dw_last_step(dw_f)
    scatter(2, 4)
    sum_add(4, sums_now)
    sums_out[...] = all_sums[5]
    for one in last + arrived[0] + arrived[1] + arrived[2]:
        one()
    for slot in range(heads):
        dw_y_copy(head_at(slot), slot).wait_send()

    def finish_send(head, carry):
        for to_core in range(2):
            for to_x in range(2):
                pl.when(jnp.logical_not(att_local(to_core, to_x)))(
                    lambda to_core=to_core, to_x=to_x: att_out(head, to_core, to_x).wait_send()
                )
        return carry

    lax.fori_loop(0, heads, finish_send, 0)
    wires.finish()


def struct(shape, dtype):
    return jax.ShapeDtypeStruct(shape, dtype)


def kernel_call(kernel, outputs, in_specs, out_spaces, scratch, collective_id=None):
    extra = {} if collective_id is None else {"collective_id": collective_id, "has_side_effects": True}
    return pl.pallas_call(
        kernel,
        out_shape=tuple(outputs),
        in_specs=[pl.BlockSpec(memory_space=space) for space in in_specs],
        out_specs=tuple(pl.BlockSpec(memory_space=space) for space in out_spaces),
        scratch_shapes=scratch,
        compiler_params=pltpu.CompilerParams(vmem_limit_bytes=VMEM_LIMIT, **extra),
    )


def fused_device(
    group,
    tokens,
    lengths,
    qkv_weight,
    out_weight,
    up_weight,
    up_bias,
    down_weight,
    down_bias,
    attn_gain,
    mlp_gain,
    query_scale,
    cotangent,
):
    rows, dim = tokens.shape
    slab2, cols = out_weight.shape
    slab = slab2 // 2
    halves = lengths.shape[0]
    heads = halves * slab2 // HEAD_DIM
    local = heads * HEAD_DIM
    narrow_count = group * halves
    hidden = slab2 * narrow_count
    vmem, smem, anywhere = pltpu.VMEM, pltpu.SMEM, pl.ANY

    shards = jnp.concatenate(
        [
            jnp.swapaxes(qkv_weight, 1, 2),
            out_weight[None],
            up_weight.T[None],
            down_weight[None],
        ]
    )
    scale_dim = LOG_TWO_E / math.sqrt(HEAD_DIM) * jax.nn.softplus(query_scale)

    def row(values):
        return jnp.pad(values.astype(F32), (0, dim - values.shape[0]))

    params = jnp.stack(
        [row(attn_gain), row(mlp_gain), row(down_bias), row(up_bias), row(scale_dim)]
        + [jnp.zeros((dim,), F32)] * 3
    )

    att_shape = (2, heads, 2, HEAD_DIM, rows)
    wq_shape = (3, heads, slab, dim)
    wm_shape = (3, 2, narrow_count * slab, dim)
    dma = pltpu.SemaphoreType.DMA

    forward_outputs = [
        struct((group, rows, dim), LOW),
        struct((group, rows, dim), LOW),
        struct((local, LEN), F32),
        struct((heads, HEAD_DIM, LEN), LOW),
        struct((heads, HEAD_DIM, LEN), LOW),
        struct((heads, LEN, HEAD_DIM), LOW),
        struct((heads, LEN, HEAD_DIM), LOW),
        struct(wq_shape, LOW),
        struct((heads, 1, LEN), F32),
        struct((rows, dim), LOW),
        struct((rows, dim), F32),
        struct(att_shape, LOW),
        struct(wm_shape, LOW),
        struct((8, dim), F32),
        struct((8, 128), F32),
    ]
    (
        x_all,
        normal,
        query_full,
        query_t,
        key_t,
        key_n,
        value_n,
        w_qkv,
        logsum,
        result,
        grad_middle,
        grad_att,
        w_grads,
        sums,
        ends,
    ) = kernel_call(
        functools.partial(forward_kernel, group),
        forward_outputs,
        [smem] + [vmem] * 4,
        [anywhere] * (len(forward_outputs) - 2) + [vmem] * 2,
        [
            vmem((group, rows, dim), LOW),
            vmem((group, rows, dim), LOW),
            vmem(wq_shape, LOW),
            vmem(wm_shape, LOW),
            vmem((6, slab, 2 * cols), LOW),
            vmem((6, slab, cols), LOW),
            vmem((narrow_count, 8, slab2), F32),
            vmem((1, hidden), F32),
            vmem((8, 128), F32),
            vmem((8, 128), F32),
            vmem((local, LEN), F32),
            vmem((heads, HEAD_DIM, LEN), LOW),
            vmem((heads, HEAD_DIM, LEN), LOW),
            vmem((heads, HEAD_DIM, LEN), LOW),
            vmem((heads, LEN, HEAD_DIM), LOW),
            vmem((heads, LEN, HEAD_DIM), LOW),
            vmem((heads, 1, LEN), F32),
            vmem((heads, HEAD_DIM, LEN), LOW),
            vmem(att_shape, LOW),
            vmem(att_shape, LOW),
            vmem((rows, dim), F32),
            dma((110,)),
            dma((110,)),
            dma((16,)),
        ],
        collective_id=0,
    )(lengths, tokens, shards, params, cotangent)

    last_shape = (3, 2, slab, cols)
    grad_tokens, mlp_grads, qkv_grads, totals = kernel_call(
        functools.partial(backward_kernel, group),
        [
            struct((rows, dim), F32),
            struct(last_shape, F32),
            struct(last_shape, F32),
            struct((8, dim), F32),
        ],
        [vmem, anywhere, vmem, vmem] + [anywhere, vmem] + [anywhere] * 3 + [vmem] * 5 + [anywhere, vmem],
        [vmem] * 4,
        [
            vmem((group, rows, dim), LOW),
            vmem((heads, HEAD_DIM, LEN), LOW),
            vmem((3, heads, HEAD_DIM, LEN), LOW),
            vmem((HEAD_DIM, LEN), F32),
            vmem((HEAD_DIM, LEN), F32),
            vmem((HEAD_DIM, TILE // 2), F32),
            vmem((3, narrow_count * slab, dim), LOW),
            vmem((3 * narrow_count * slab, dim), LOW),
            vmem((2 * narrow_count * slab, 2 * cols), LOW),
            vmem((3, 4, slab, dim), LOW),
            vmem((3, 2, slab, 2 * cols), LOW),
            vmem((3, 1, slab, 2 * cols), LOW),
            vmem((3, slab, cols), F32),
            vmem((rows // 2, dim), LOW),
            vmem((group, rows // 2, dim), LOW),
            vmem((2, rows // 2, dim), LOW),
            vmem((2, rows // 2, dim), LOW),
            vmem(wq_shape, LOW),
            vmem(wq_shape, LOW),
            vmem((3, heads, slab, 2 * cols), LOW),
            vmem((3, 2, slab, 2 * cols), LOW),
            vmem((3, slab, 2 * cols), LOW),
            vmem((3, slab, cols), F32),
            vmem((6, 8, dim), F32),
            vmem((5, 8, dim), F32),
            dma((100,)),
            dma((100,)),
            dma((12,)),
        ],
        collective_id=1,
    )(
        ends,
        tokens,
        params,
        sums,
        grad_middle,
        grad_att,
        w_grads,
        x_all,
        normal,
        query_full,
        query_t,
        key_t,
        key_n,
        value_n,
        w_qkv,
        logsum,
    )

    mlp_grads = mlp_grads.reshape(3, slab2, cols)
    grad_up_bias = lax.dynamic_index_in_dim(
        totals[2].reshape(2, narrow_count, slab), lax.axis_index("narrow"), 1, keepdims=False
    ).reshape(slab2)
    grad_scale = (
        totals[3, :HEAD_DIM] * (LOG_TWO_E / math.sqrt(HEAD_DIM)) * jax.nn.sigmoid(query_scale)
    )
    return (
        result,
        grad_tokens,
        jnp.swapaxes(qkv_grads.reshape(3, slab2, cols), 1, 2),
        mlp_grads[0],
        mlp_grads[1].T,
        grad_up_bias,
        mlp_grads[2],
        totals[1],
        totals[4],
        totals[0],
        grad_scale,
    )


def solution(mesh):
    wide_count, narrow_count = mesh.shape["wide"], mesh.shape["narrow"]

    def per_device(*args):
        tokens, lengths, out_weight = args[0], args[1], args[3]
        group = LEN // tokens.shape[0]
        fits = (
            wide_count == 4
            and group == 4
            and narrow_count == group * lengths.shape[0] == 8
            and out_weight.shape[0] == 2 * HEAD_DIM
            and 2 * out_weight.shape[1] % 128 == 0
        )
        if fits:
            return fused_device(group, *args)
        return general_device(*args)

    return jax.shard_map(
        per_device,
        mesh=mesh,
        in_specs=(
            P(("wide", "narrow"), None),
            P("wide", None),
            P(None, "wide", "narrow"),
            P("narrow", "wide"),
            P("wide", "narrow"),
            P("narrow"),
            P("narrow", "wide"),
            P(),
            P(),
            P(),
            P(),
            P(("wide", "narrow"), None),
        ),
        out_specs=(
            P(("wide", "narrow"), None),
            P(("wide", "narrow"), None),
            P(None, "wide", "narrow"),
            P("narrow", "wide"),
            P("wide", "narrow"),
            P("narrow"),
            P("narrow", "wide"),
            P(),
            P(),
            P(),
            P(),
        ),
        check_vma=False,
    )
```

```python
import functools
import math

import jax
import jax.numpy as jnp
from jax import lax
from jax.experimental import pallas as pl
from jax.experimental.pallas import tpu as pltpu
from jax.sharding import PartitionSpec as P

HEAD_DIM = 80
LEN = 2048
WINDOW = 1024
BLOCK = 512
NDOC = 4
TILE = 256

LOG_TWO_E = 1.4426950408889634
EPSILON = 1e-06
NEG_FILL = -1e30

F32 = jnp.float32
LOW = jnp.bfloat16
MESH = pl.DeviceIdType.MESH
VMEM_LIMIT = 63 * 2**20


def group_rows(values):
    return lax.all_gather(values, "narrow", axis=0, tiled=True)


def group_parts(values):
    return lax.psum_scatter(values, "narrow", scatter_dimension=0, tiled=True)


def contract_last(left, right):
    return lax.dot_general(
        left, right, (((1,), (1,)), ((), ())), preferred_element_type=jnp.float32
    )


def contract_first(left, right):
    return lax.dot_general(
        left, right, (((0,), (0,)), ((), ())), preferred_element_type=jnp.float32
    )


def norm_share(inputs, norm_gain):
    inverse = lax.rsqrt(jnp.mean(inputs * inputs, axis=1) + EPSILON)
    normed = inputs * inverse[:, None]
    return (inverse, normed, (normed * norm_gain).astype(jnp.bfloat16))


def norm_back(grad_normal, norm_gain, inverse, normed):
    scaled = grad_normal * norm_gain
    inner_dots = jnp.mean(scaled * normed, axis=1)
    grad_inputs = inverse[:, None] * (scaled - normed * inner_dots[:, None])
    return (grad_inputs, jnp.sum(grad_normal * normed, axis=0))


def segment_ids(lengths_row):
    positions = jnp.arange(LEN, dtype=jnp.int32)
    ends = jnp.cumsum(lengths_row)
    return jnp.sum((positions[:, None] >= ends[None, :]).astype(jnp.int32), axis=1)


def block_mask(segments, padded_seg, offset):
    query_pos = offset + jnp.arange(BLOCK, dtype=jnp.int32)
    key_pos = offset - WINDOW + jnp.arange(WINDOW + BLOCK, dtype=jnp.int32)
    query_seg = segments[offset : offset + BLOCK]
    key_seg = padded_seg[offset : offset + WINDOW + BLOCK]
    spacing = query_pos[:, None] - key_pos[None, :]
    same_doc = query_seg[:, None] == key_seg[None, :]
    inside = (spacing >= 0) & (spacing < WINDOW)
    real_doc = (query_seg[:, None] < NDOC) | (spacing == 0)
    return same_doc & inside & real_doc


def padded_inputs(keys_in, values_in, segments):
    pad_rows = jnp.zeros((WINDOW,) + keys_in.shape[1:], keys_in.dtype)
    keys_pad = jnp.concatenate([pad_rows, keys_in], axis=0)
    values_pad = jnp.concatenate([pad_rows, values_in], axis=0)
    padded_seg = jnp.concatenate([jnp.full((WINDOW,), -2, jnp.int32), segments])
    return (keys_pad, values_pad, padded_seg)


def attend_forward(queries, keys_in, values_in, segments):
    keys_pad, values_pad, padded_seg = padded_inputs(keys_in, values_in, segments)
    outputs = []
    logsums = []
    for block_index in range(LEN // BLOCK):
        offset = block_index * BLOCK
        query_block = queries[offset : offset + BLOCK]
        key_block = keys_pad[offset : offset + WINDOW + BLOCK]
        value_block = values_pad[offset : offset + WINDOW + BLOCK]
        allowed = block_mask(segments, padded_seg, offset)
        scores = jnp.einsum(
            "ihd,jhd->hij", query_block, key_block, preferred_element_type=jnp.float32
        )
        masked = jnp.where(allowed[None], scores, NEG_FILL)
        maxima = jnp.max(masked, axis=2)
        exponent = jnp.exp(masked - maxima[:, :, None])
        totals = jnp.sum(exponent, axis=2)
        probs_low = (exponent / totals[:, :, None]).astype(jnp.bfloat16)
        block_out = jnp.einsum(
            "hij,jhd->ihd", probs_low, value_block, preferred_element_type=jnp.float32
        )
        outputs.append(block_out.astype(jnp.bfloat16))
        logsums.append(maxima + jnp.log(totals))
    return (jnp.concatenate(outputs, axis=0), jnp.concatenate(logsums, axis=1))


def attend_backward(queries, keys_in, values_in, segments, logsum, grad_out):
    keys_pad, values_pad, padded_seg = padded_inputs(keys_in, values_in, segments)
    grad_keys = jnp.zeros(keys_pad.shape, jnp.float32)
    grad_values = jnp.zeros(values_pad.shape, jnp.float32)
    grad_queries = []
    for block_index in range(LEN // BLOCK):
        offset = block_index * BLOCK
        query_block = queries[offset : offset + BLOCK]
        key_block = keys_pad[offset : offset + WINDOW + BLOCK]
        value_block = values_pad[offset : offset + WINDOW + BLOCK]
        grad_block = grad_out[offset : offset + BLOCK]
        allowed = block_mask(segments, padded_seg, offset)
        scores = jnp.einsum(
            "ihd,jhd->hij", query_block, key_block, preferred_element_type=jnp.float32
        )
        masked = jnp.where(allowed[None], scores, NEG_FILL)
        soft_probs = jnp.exp(masked - logsum[:, offset : offset + BLOCK, None])
        probs_low = soft_probs.astype(jnp.bfloat16)
        grad_probs = jnp.einsum(
            "ihd,jhd->hij", grad_block, value_block, preferred_element_type=jnp.float32
        )
        inner_sums = jnp.sum(soft_probs * grad_probs, axis=2)
        grad_scores = (soft_probs * (grad_probs - inner_sums[:, :, None])).astype(jnp.bfloat16)
        grad_queries.append(
            jnp.einsum("hij,jhd->ihd", grad_scores, key_block, preferred_element_type=jnp.float32)
        )
        key_terms = jnp.einsum(
            "hij,ihd->jhd", grad_scores, query_block, preferred_element_type=jnp.float32
        )
        value_terms = jnp.einsum(
            "hij,ihd->jhd", probs_low, grad_block, preferred_element_type=jnp.float32
        )
        grad_keys = grad_keys.at[offset : offset + WINDOW + BLOCK].add(key_terms)
        grad_values = grad_values.at[offset : offset + WINDOW + BLOCK].add(value_terms)
    return (jnp.concatenate(grad_queries, axis=0), grad_keys[WINDOW:], grad_values[WINDOW:])


def silu_slope(hidden_pre):
    sigmoid_pre = jax.nn.sigmoid(hidden_pre)
    return sigmoid_pre * (1.0 + hidden_pre * (1.0 - sigmoid_pre))


def general_device(
    tokens,
    lengths,
    qkv_weight,
    out_weight,
    up_weight,
    up_bias,
    down_weight,
    down_bias,
    attn_gain,
    mlp_gain,
    query_scale,
    cotangent,
):
    head_count = qkv_weight.shape[2] // HEAD_DIM
    seq_count = lengths.shape[0]
    row_count = seq_count * LEN

    def by_sequence(values):
        return values.reshape((seq_count, LEN) + values.shape[1:])

    qkv_full, out_full, up_full, down_full = (
        lax.all_gather(qkv_weight, "wide", axis=1, tiled=True),
        lax.all_gather(out_weight, "wide", axis=1, tiled=True),
        lax.all_gather(up_weight, "wide", axis=0, tiled=True),
        lax.all_gather(down_weight, "wide", axis=1, tiled=True),
    )
    segments = jax.vmap(segment_ids)(lengths)
    inputs = tokens.astype(jnp.float32)
    inverse_one, normed_one, normal_one = norm_share(inputs, attn_gain)
    rows_one = group_rows(normal_one)
    projected = jnp.einsum("td,cdn->ctn", rows_one, qkv_full, preferred_element_type=jnp.float32)
    scale_dim = LOG_TWO_E / math.sqrt(HEAD_DIM) * jax.nn.softplus(query_scale)
    query_heads = projected[0].reshape(row_count, head_count, HEAD_DIM)
    query_low = (query_heads * scale_dim).astype(jnp.bfloat16)
    key_low = projected[1].astype(jnp.bfloat16).reshape(row_count, head_count, HEAD_DIM)
    value_low = projected[2].astype(jnp.bfloat16).reshape(row_count, head_count, HEAD_DIM)
    attended, logsum = jax.vmap(attend_forward)(
        by_sequence(query_low), by_sequence(key_low), by_sequence(value_low), segments
    )
    attended_rows = attended.reshape(row_count, head_count * HEAD_DIM)
    middle = inputs + group_parts(
        jnp.dot(attended_rows, out_full, preferred_element_type=jnp.float32)
    )
    inverse_two, normed_two, normal_two = norm_share(middle, mlp_gain)
    grad_down_bias = jnp.sum(cotangent.astype(jnp.float32), axis=0)
    rows_two = group_rows(normal_two)
    hidden_pre = jnp.dot(rows_two, up_full, preferred_element_type=jnp.float32) + up_bias
    hidden_low = jax.nn.silu(hidden_pre).astype(jnp.bfloat16)
    branch_two = (
        group_parts(jnp.dot(hidden_low, down_full, preferred_element_type=jnp.float32)) + down_bias
    )
    result = middle + branch_two
    grad_rows = group_rows(cotangent)
    grad_hidden = contract_last(grad_rows, down_full)
    grad_pre = (grad_hidden * silu_slope(hidden_pre)).astype(jnp.bfloat16)
    grad_up = contract_first(rows_two, grad_pre)
    grad_down = contract_first(hidden_low, grad_rows)
    grad_up_bias = jnp.sum(grad_pre.astype(jnp.float32), axis=0)
    grad_normal_two = group_parts(contract_last(grad_pre, up_full))
    grad_middle_norm, grad_mlp_gain = norm_back(grad_normal_two, mlp_gain, inverse_two, normed_two)
    grad_middle = cotangent.astype(jnp.float32) + grad_middle_norm
    grad_branch = group_rows(grad_middle.astype(jnp.bfloat16))
    grad_attended = contract_last(grad_branch, out_full).astype(jnp.bfloat16)
    grad_out = contract_first(attended_rows, grad_branch)
    grad_scaled, grad_key, grad_value = jax.vmap(attend_backward)(
        by_sequence(query_low),
        by_sequence(key_low),
        by_sequence(value_low),
        segments,
        logsum,
        by_sequence(grad_attended.reshape(row_count, head_count, HEAD_DIM)),
    )
    grad_scaled = grad_scaled.reshape(row_count, head_count, HEAD_DIM)
    grad_scale_part = (
        jnp.sum(grad_scaled * query_heads, axis=(0, 1))
        * (LOG_TWO_E / math.sqrt(HEAD_DIM))
        * jax.nn.sigmoid(query_scale)
    )
    grad_projected = jnp.stack(
        [
            (grad_scaled * scale_dim).reshape(row_count, head_count * HEAD_DIM),
            grad_key.reshape(row_count, head_count * HEAD_DIM),
            grad_value.reshape(row_count, head_count * HEAD_DIM),
        ]
    ).astype(jnp.bfloat16)
    grad_qkv = jnp.einsum(
        "td,ctn->cdn", rows_one, grad_projected, preferred_element_type=jnp.float32
    )
    grad_normal_one = group_parts(
        jnp.einsum("ctn,cdn->td", grad_projected, qkv_full, preferred_element_type=jnp.float32)
    )
    grad_input_norm, grad_attn_gain = norm_back(grad_normal_one, attn_gain, inverse_one, normed_one)
    grad_tokens = grad_middle + grad_input_norm
    grad_qkv, grad_out, grad_up, grad_down = (
        lax.psum_scatter(grad_qkv, "wide", scatter_dimension=1, tiled=True),
        lax.psum_scatter(grad_out, "wide", scatter_dimension=1, tiled=True),
        lax.psum_scatter(grad_up, "wide", scatter_dimension=0, tiled=True),
        lax.psum_scatter(grad_down, "wide", scatter_dimension=1, tiled=True),
    )
    grad_attn_gain, grad_mlp_gain, grad_down_bias, grad_scale = lax.psum(
        (grad_attn_gain, grad_mlp_gain, grad_down_bias, grad_scale_part), ("wide", "narrow")
    )
    grad_up_bias = lax.psum(grad_up_bias, "wide")
    return (
        result.astype(jnp.bfloat16),
        grad_tokens,
        grad_qkv,
        grad_out,
        grad_up,
        grad_up_bias,
        grad_down,
        grad_down_bias,
        grad_attn_gain,
        grad_mlp_gain,
        grad_scale,
    )


def product(left, right, left_dim=1, right_dim=0):
    return lax.dot_general(
        left, right, (((left_dim,), (right_dim,)), ((), ())), preferred_element_type=F32
    )


def flip(value, mask):
    bit = 1
    while bit <= mask:
        if mask & bit:
            value = value + bit * (1 - 2 * lax.rem(lax.div(value, bit), 2))
        bit *= 2
    return value


def part(start, size):
    return pl.ds(pl.multiple_of(start * size, size), size)


def chunks(total, size, body):
    def step(index, carry):
        body(part(index, size))
        return carry

    lax.fori_loop(0, total // size, step, 0)


def add_rows(target, source, size):
    def body(span):
        target[span, :] = (target[span, :].astype(F32) + source[span, :].astype(F32)).astype(LOW)

    chunks(source.shape[0], size, body)


class Place:
    def __init__(self, group):
        self.wide = lax.axis_index("wide")
        self.narrow = lax.axis_index("narrow")
        self.core = lax.rem(self.wide, 2)
        self.y = lax.div(self.wide, 2)
        self.quarter = lax.rem(self.narrow, group)
        self.half = lax.div(self.narrow, group)
        self.x = lax.rem(self.narrow, 2)
        self.z = lax.div(self.quarter, 2)
        self.column = lax.div(self.narrow, 2)
        self.collector = self.core == self.z

    def along_wide(self, mask):
        return (flip(self.wide, mask), self.narrow)

    def along_narrow(self, mask):
        return (self.wide, flip(self.narrow, mask))

    def at(self, core, narrow):
        return (self.y * 2 + core, narrow)


def greet(place, group):
    barrier = pltpu.get_barrier_semaphore()
    peers = [place.along_narrow(m) for m in range(1, 2 * group)]
    peers += [place.along_wide(m) for m in (1, 2, 3)]
    peers += [(flip(place.wide, 1), flip(place.narrow, m)) for m in range(1, group + 1)]
    for peer in peers:
        pl.semaphore_signal(barrier, inc=1, device_id=peer, device_id_type=MESH)
    pl.semaphore_wait(barrier, len(peers))


class Wires:
    def __init__(self, send_sem, recv_sem):
        self.send_sem, self.recv_sem = send_sem, recv_sem
        self.next_id = 0
        self.sent = []

    def ids(self, count):
        first = self.next_id
        self.next_id += count
        assert self.next_id <= self.send_sem.shape[0]
        return first

    def copy(self, source, target, device, index, arrival=None):
        return pltpu.make_async_remote_copy(
            src_ref=source,
            dst_ref=target,
            send_sem=self.send_sem.at[index],
            recv_sem=self.recv_sem.at[index if arrival is None else arrival],
            device_id=device,
            device_id_type=MESH,
        )

    def exchange(self, source, target, incoming, device):
        index = self.ids(1)
        out = self.copy(source, target, device, index)
        out.start()
        self.sent.append((None, lambda: out))
        return self.copy(incoming, incoming, device, index)

    def trade(self, make):
        index = self.ids(1)

        def out():
            source, target, device = make()
            return self.copy(source, target, device, index)

        out().start()
        self.sent.append((None, out))

        def arrive():
            _, target, device = make()
            self.copy(target, target, device, index).wait_recv()

        return arrive

    def start_if(self, condition, make):
        pl.when(condition)(lambda: make().start())
        self.sent.append((condition, make))

    def finish(self, conditional=(True, False)):
        for condition, make in self.sent:
            if (condition is not None) not in conditional:
                continue
            if condition is None:
                make().wait_send()
            else:
                pl.when(condition)(lambda make=make: make().wait_send())
        self.sent = [one for one in self.sent if (one[0] is not None) not in conditional]


def wait_if(condition, make):
    pl.when(condition)(lambda: make().wait_recv())


def ends_row(lengths, row):
    lane = lax.broadcasted_iota(jnp.int32, (8, 128), 1)
    result, total = jnp.zeros((8, 128), jnp.int32), 0
    for index in range(NDOC):
        total = total + lengths[row, index]
        result = jnp.where(lane == index, total, result)
    return result.astype(F32)


def document_ends(row):
    return [
        jnp.broadcast_to(row[0:1, k : k + 1], (1, TILE)).astype(jnp.int32) for k in range(NDOC)
    ]


def first_key(ends, offset):
    position = offset + lax.broadcasted_iota(jnp.int32, (1, TILE), 1)
    start = jnp.zeros_like(position)
    for end in ends:
        start = jnp.where(position >= end, end, start)
    start = jnp.maximum(start, position - (WINDOW - 1))
    return jnp.where(position >= ends[-1], position, start), position


def allowed_scores(scores, key_start, offset, first, position):
    key = key_start + lax.broadcasted_iota(jnp.int32, scores.shape, 0)
    allowed = key >= first
    if key_start + scores.shape[0] > offset:
        allowed = allowed & (key <= position)
    return jnp.where(allowed, scores, NEG_FILL)


def tile_keys(tile):
    offset = tile * TILE
    return offset, range(max(0, offset - WINDOW), offset + TILE, TILE)


def pipelined(tiles, first_half, second_half):
    waiting = None
    for tile in tiles:
        current = (tile, first_half(tile))
        if waiting is not None:
            second_half(*waiting)
        waiting = current
    second_half(*waiting)


def attend_head(head, ends, queries, keys, values_t, attended, logsum):
    def first_half(tile):
        offset, starts = tile_keys(tile)
        first, position = first_key(ends, offset)
        query = queries[head, :, offset : offset + TILE]
        blocks, maxima = [], None
        for start in starts:
            scores = product(keys[head, start : start + TILE, :], query)
            scores = allowed_scores(scores, start, offset, first, position)
            top = jnp.max(scores, axis=0, keepdims=True)
            maxima = top if maxima is None else jnp.maximum(maxima, top)
            blocks.append(scores)
        return blocks, maxima

    def second_half(tile, held):
        blocks, maxima = held
        offset, starts = tile_keys(tile)
        total, output = None, None
        for scores, start in zip(blocks, starts):
            exponent = jnp.exp(scores - maxima)
            share = jnp.sum(exponent, axis=0, keepdims=True)
            term = product(values_t[head, :, start : start + TILE], exponent.astype(LOW))
            total, output = (
                (share, term) if total is None else (total + share, output + term)
            )
        attended[head, :, offset : offset + TILE] = (output * (1.0 / total)).astype(LOW)
        logsum[head, :, offset : offset + TILE] = maxima + jnp.log(total)

    pipelined(range(LEN // TILE), first_half, second_half)


def norm_rows(inputs):
    return lax.rsqrt(jnp.mean(inputs * inputs, axis=1, keepdims=True) + EPSILON)


def scale_column(query_scale):
    values = query_scale[...].reshape(1, -1)
    softplus = jnp.maximum(values, 0.0) + jnp.log(1.0 + jnp.exp(-jnp.abs(values)))
    row = LOG_TWO_E / math.sqrt(HEAD_DIM) * softplus
    return jnp.broadcast_to(row, (128, HEAD_DIM)).T[:, :1]


GATHER_ORDERS = ("zfy", "fzy", "fyz", "fxyz", "fzyx", "zfxy")


def forward_kernel(
    group,
    lengths,
    tokens,
    qkv_weight,
    out_weight,
    up_weight,
    up_bias_in,
    down_weight,
    down_bias_in,
    attn_gain,
    mlp_gain,
    query_scale,
    cotangent,
    x_out,
    normal_out,
    qf_out,
    q_out,
    kt_out,
    kn_out,
    vn_out,
    wq_out,
    lse_out,
    result_out,
    middle_out,
    att_out,
    wo_out,
    acts_out,
    sums,
    ends_out,
    x_all,
    normal,
    shards,
    w_qkv,
    w_mlp,
    w_pair,
    w_half,
    bias_all,
    bias_row,
    ends_own,
    ends_other,
    query_full,
    query_t,
    key_t,
    value_t,
    key_n,
    value_n,
    logsum,
    attended,
    att_all,
    grad_att,
    grad_middle,
    send_sem,
    recv_sem,
    local_sem,
):
    place = Place(group)
    core, y, quarter, narrow = place.core, place.y, place.quarter, place.narrow
    collector = place.collector
    other_core = jnp.logical_not(collector)
    rows = tokens.shape[0]
    mid = rows // 2
    slab2 = shards.shape[1]
    slab = slab2 // 2
    pair_cols = 2 * shards.shape[2]
    cols_y = part(y, pair_cols)
    cols_other = part(1 - y, pair_cols)
    x_dev, z_dev, far_dev = (
        place.along_narrow(1),
        place.along_narrow(2),
        place.along_narrow(group),
    )
    core_dev, y_dev = place.along_wide(1), place.along_wide(2)
    wires = Wires(send_sem, recv_sem)
    exchange = wires.exchange
    gain_one, gain_two = attn_gain[...].reshape(1, -1), mlp_gain[...].reshape(1, -1)
    down_bias = down_bias_in[...].astype(F32).reshape(1, -1)

    greet(place, group)

    halves = (slice(0, mid), slice(mid, rows))

    def x_part(mask, which):
        return x_all.at[flip(quarter, mask), halves[which]]

    x_first, z_first, on_first, core_first = (
        wires.ids(2),
        wires.ids(2),
        wires.ids(2),
        wires.ids(5),
    )

    def x_own(which):
        return wires.copy(tokens.at[halves[which]], x_part(0, which), x_dev, x_first + which)

    def x_in(which):
        return wires.copy(x_part(1, which), x_part(1, which), x_dev, x_first + which)

    def z_own(which):
        return wires.copy(tokens.at[halves[which]], x_part(0, which), z_dev, z_first + which)

    def z_in(which):
        return wires.copy(x_part(2, which), x_part(2, which), z_dev, z_first + which)

    def on_out(which):
        return wires.copy(x_part(2, which), x_part(2, which), x_dev, on_first + which)

    def on_in(which):
        return wires.copy(x_part(3, which), x_part(3, which), x_dev, on_first + which)

    def core_copy(index, mask, which=None):
        there = x_all.at[flip(quarter, mask)] if which is None else x_part(mask, which)
        source = tokens if mask == 0 else there
        return wires.copy(source, there, core_dev, core_first + index)

    for which in range(2):
        wires.start_if(collector, lambda which=which: x_own(which))
        wires.start_if(other_core, lambda which=which: z_own(which))
    for m in range(3):
        shards[m] = qkv_weight[m]
    shards[3] = out_weight[...]
    shards[4] = up_weight[...]
    shards[5] = down_weight[...]
    w_arrived = exchange(shards.at[:, part(1 - core, slab), :], w_half, w_half, core_dev)
    ends_own[...] = ends_row(lengths, place.half)
    ends_from = exchange(ends_own, ends_other, ends_other, core_dev)
    wires.start_if(collector, lambda: core_copy(0, 0))
    bias_all[narrow] = jnp.broadcast_to(
        up_bias_in[...].astype(F32).reshape(1, -1), bias_all.shape[1:]
    )
    bias_from = [
        exchange(
            bias_all.at[narrow],
            bias_all.at[narrow],
            bias_all.at[flip(narrow, mask)],
            place.along_narrow(mask),
        )
        for mask in range(1, 2 * group)
    ]

    @pl.when(collector)
    def _():
        x_all[quarter] = tokens[...]

    w_arrived.wait_recv()
    own = shards[:, part(core, slab), :]
    other = w_half[...]
    w_pair[:, :, : pair_cols // 2] = jnp.where(core == 0, own, other)
    w_pair[:, :, pair_cols // 2 :] = jnp.where(core == 0, other, own)
    for m in range(3):
        w_qkv[m, place.column, :, cols_y] = w_pair[m]
        w_mlp[m, core, part(narrow, slab), cols_y] = w_pair[3 + m]

    masks = {"x": 1, "z": 2, "f": group}
    devices = {"x": x_dev, "z": z_dev, "f": far_dev, "y": y_dev}

    def block(m, mask, columns):
        where = flip(narrow, mask)
        columns = {"own": cols_y, "other": cols_other, "both": slice(None)}[columns]
        if m < 3:
            return w_qkv.at[m, lax.div(where, 2), :, columns]
        return w_mlp.at[m - 3, core, part(where, slab), columns]

    def whole(m, columns):
        if m < 3:
            return w_qkv.at[m, :, :, columns]
        return w_mlp.at[m - 3, core, :, columns]

    held = [{0: "own"} for _ in range(6)]
    gathered = [[] for _ in range(6)]
    turned = {"own": "other", "other": "own", "both": "both"}

    def arrive(m):
        for one in gathered[m]:
            one.wait_recv()
        gathered[m] = []

    def gather(m, stage):
        arrive(m)
        order = GATHER_ORDERS[m]
        if stage == len(order):
            gathered[m] = [
                exchange(
                    w_mlp.at[m - 3, core],
                    w_mlp.at[m - 3, core],
                    w_mlp.at[m - 3, 1 - core],
                    core_dev,
                )
            ]
            return
        way = order[stage]
        device = devices[way]
        if way == "y" and stage == len(order) - 1:
            mine = whole(m, cols_y)
            gathered[m] = [exchange(mine, mine, whole(m, cols_other), device)]
            return
        more = {}
        for mask, columns in held[m].items():
            mine = block(m, mask, columns)
            if way == "y":
                incoming = block(m, mask, turned[columns])
                more[mask] = "both"
            else:
                incoming = block(m, mask ^ masks[way], columns)
                more[mask ^ masks[way]] = columns
            gathered[m].append(exchange(mine, mine, incoming, device))
        held[m].update(more)

    scale = jnp.tile(scale_column(query_scale), (query_t.shape[0], 1))

    def project(mask):
        where = flip(quarter, mask)
        span = part(where, rows)
        inputs = x_all[where].astype(F32)
        normal[where] = (inputs * norm_rows(inputs) * gain_one).astype(LOW)
        weight = w_qkv[...].reshape(-1, inputs.shape[1])
        out = product(weight, normal[where], 1, 1)
        size = out.shape[0] // 3
        heads = size // HEAD_DIM
        query_full[:, span] = out[:size]
        query_t[:, :, span] = (out[:size] * scale).astype(LOW).reshape(heads, HEAD_DIM, rows)
        key = out[size : 2 * size].astype(LOW).reshape(heads, HEAD_DIM, rows)
        value = out[2 * size :].astype(LOW).reshape(heads, HEAD_DIM, rows)
        key_t[:, :, span] = key
        value_t[:, :, span] = value
        for head in range(heads):
            key_n[head, span, :] = key[head].T
            value_n[head, span, :] = value[head].T

    stores = []

    def store(source, target):
        one = pltpu.make_async_copy(source, target, local_sem.at[len(stores)])
        one.start()
        stores.append(one)

    heads = query_t.shape[0]
    att_first = wires.ids(4 * heads)

    def att_send(head, mask):
        peer = flip(quarter, mask)
        return wires.copy(
            attended.at[head, :, part(peer, rows)],
            att_all.at[core, head, place.x],
            place.at(place.z, flip(narrow, mask)),
            att_first + mask * heads + head,
            att_first + (core * 2 + place.x) * heads + head,
        )

    def att_in(head, from_core, from_x):
        there = att_all.at[from_core, head, from_x]
        return wires.copy(there, there, core_dev, att_first + (from_core * 2 + from_x) * heads + head)

    def one_head(head, carry):
        attend_head(head, ends, query_t, key_n, value_t, attended, logsum)
        for mask in (3, 1, 2):
            att_send(head, mask).start()

        @pl.when(collector)
        def _():
            att_all[core, head, place.x] = attended[head, :, part(quarter, rows)]

        pl.when(other_core)(lambda: att_send(head, 0).start())
        return carry

    def pass_on(which):
        wait_if(collector, lambda: z_in(which))
        wires.start_if(collector, lambda: on_out(which))
        wires.start_if(collector, lambda: core_copy(2 + which, 2, which))

    gather(3, 0)
    gather(3, 1)
    gather(0, 0)
    gather(4, 0)
    gather(5, 0)
    gather(1, 0)
    gather(3, 2)
    gather(1, 1)
    gather(2, 0)
    pass_on(0)
    gather(2, 1)
    gather(0, 1)
    gather(4, 1)
    for which in range(2):
        wait_if(collector, lambda which=which: x_in(which))
    wires.start_if(collector, lambda: core_copy(1, 1))
    pass_on(1)
    gather(2, 2)
    gather(1, 2)
    gather(5, 1)
    gather(3, 3)
    gather(0, 2)
    gather(5, 2)
    for which in range(2):
        wait_if(collector, lambda which=which: on_in(which))
    wires.start_if(collector, lambda: core_copy(4, 3))
    gather(4, 2)
    ends_from.wait_recv()
    ends_out[...] = jnp.where(collector, ends_own[...], ends_other[...])
    ends = document_ends(ends_out)
    for m in range(3):
        arrive(m)
    wait_if(other_core, lambda: core_copy(0, 0))
    project(0)
    gather(4, 3)
    wait_if(other_core, lambda: core_copy(1, 1))
    project(1)
    for which in range(2):
        wait_if(other_core, lambda which=which: core_copy(2 + which, 2, which))
    project(2)
    wait_if(other_core, lambda: core_copy(4, 3))
    project(3)
    gather(5, 3)
    store(x_all, x_out)
    store(normal, normal_out)
    store(query_full, qf_out)
    store(query_t, q_out)
    store(key_t, kt_out)
    store(key_n, kn_out)
    store(value_n, vn_out)
    store(w_qkv, wq_out)
    lax.fori_loop(0, 2, one_head, 0)
    gather(3, 4)
    lax.fori_loop(2, 3, one_head, 0)
    gather(4, 4)
    lax.fori_loop(3, heads, one_head, 0)
    store(logsum, lse_out)

    sums[...] = jnp.zeros_like(sums)
    sums[1:2, :] = jnp.sum(cotangent[...].astype(F32), axis=0, keepdims=True)
    for one in bias_from:
        one.wait_recv()
    for c in range(2):
        for n in range(2 * group):
            start = (c * 2 * group + n) * slab
            bias_row[0:1, start : start + slab] = bias_all[n, 0:1, c * slab : (c + 1) * slab]

    def finish_head(head, carry):
        for from_core in range(2):
            for from_x in range(2):
                local = collector & (core == from_core) & (place.x == from_x)
                wait_if(
                    jnp.logical_not(local),
                    lambda from_core=from_core, from_x=from_x: att_in(head, from_core, from_x),
                )
        return carry

    lax.fori_loop(0, heads, finish_head, 0)
    arrive(3)

    size = 2 * w_mlp.shape[2]
    grad_shape = w_mlp.shape[1:]

    def weight(m):
        return w_mlp[m].reshape(size, -1)

    gather(5, 4)
    wires.finish((True,))
    stores[0].wait()
    result, grad_pre, normal_two, hidden = (x_all.at[slot] for slot in range(4))
    att = att_all[...].reshape(size, rows)
    middle = grad_middle
    middle[...] = tokens[...].astype(F32) + product(att, weight(0), 0, 0)
    inverse = norm_rows(middle[...])
    normal_two[...] = (middle[...] * inverse * gain_two).astype(LOW)
    arrive(4)
    pre = product(normal_two[...], weight(1), 1, 1) + bias_row[...]
    gate = 1.0 / (1.0 + jnp.exp(-pre))
    hidden[...] = (pre * gate).astype(LOW)
    slope = gate * (1.0 + pre * (1.0 - gate))
    arrive(5)
    grad_pre[...] = (product(cotangent[...], weight(2), 1, 1) * slope).astype(LOW)
    for slot in range(3):
        store(x_all.at[1 + slot], acts_out.at[slot])
    result[...] = (middle[...] + (product(hidden[...], weight(2)) + down_bias)).astype(LOW)
    store(result, result_out)
    grad_normal = product(grad_pre[...], weight(1))
    normed = middle[...] * inverse
    sums[0:1, :] = jnp.sum(grad_normal * normed, axis=0, keepdims=True)
    scaled = grad_normal * gain_two
    inner = jnp.mean(scaled * normed, axis=1, keepdims=True)
    grad_middle[...] = cotangent[...].astype(F32) + inverse * (scaled - normed * inner)
    store(grad_middle, middle_out)
    branch = grad_middle[...].astype(LOW)
    grad_att[...] = product(weight(0), branch, 1, 1).astype(LOW).reshape(grad_att.shape)
    store(grad_att, att_out)

    def finish_send(head, carry):
        for mask in (1, 2, 3):
            att_send(head, mask).wait_send()
        pl.when(other_core)(lambda: att_send(head, 0).wait_send())
        return carry

    lax.fori_loop(0, heads, finish_send, 0)
    wires.finish()
    w_mlp[0] = product(att, branch).astype(LOW).reshape(grad_shape)
    store(w_mlp.at[0], wo_out)
    sums[2:3, :] = jnp.sum(grad_pre[...].astype(F32), axis=0, keepdims=True)
    for one in stores[1:]:
        one.wait()


def backward_head(
    head,
    ends,
    queries,
    query_full,
    keys,
    keys_t,
    values,
    grad_out,
    logsum,
    scale,
    grads_t,
    sum_keys,
    sum_values,
    sum_scale,
    halfway,
):
    sum_keys[...] = jnp.zeros_like(sum_keys)
    sum_values[...] = jnp.zeros_like(sum_values)

    def first_half(tile):
        offset, starts = tile_keys(tile)
        first, position = first_key(ends, offset)
        span = slice(offset, offset + TILE)
        query, grad, log_row = queries[head, :, span], grad_out[head, :, span], logsum[head, :, span]
        blocks, inner = [], None
        for start in starts:
            scores = product(keys[head, start : start + TILE, :], query)
            scores = allowed_scores(scores, start, offset, first, position)
            probs = jnp.exp(scores - log_row)
            grad_probs = product(values[head, start : start + TILE, :], grad)
            share = jnp.sum(probs * grad_probs, axis=0, keepdims=True)
            inner = share if inner is None else inner + share
            blocks.append((probs, grad_probs))
        return blocks, inner, query, grad

    def second_half(tile, held):
        blocks, inner, query, grad = held
        offset, starts = tile_keys(tile)
        span = slice(offset, offset + TILE)
        grad_scaled = None
        for (probs, grad_probs), start in zip(blocks, starts):
            there = slice(start, start + TILE)
            grad_scores = (probs * (grad_probs - inner)).astype(LOW)
            term = product(keys_t[head, :, there], grad_scores)
            grad_scaled = term if grad_scaled is None else grad_scaled + term
            sum_keys[:, there] += product(query, grad_scores, 1, 1)
            sum_values[:, there] += product(grad, probs.astype(LOW), 1, 1)
        grads_t[0, head, :, span] = (grad_scaled * scale).astype(LOW)
        terms = grad_scaled * query_full[part(head, HEAD_DIM), span]
        sum_scale[...] += terms[:, : TILE // 2] + terms[:, TILE // 2 :]

    count = LEN // TILE
    pipelined(range(count // 2), first_half, second_half)
    halfway()
    pipelined(range(count // 2, count), first_half, second_half)
    grads_t[1, head] = sum_keys[...].astype(LOW)
    grads_t[2, head] = sum_values[...].astype(LOW)


SCATTER_ORDERS = ("yzxf", "xyzf", "zyxf")


def backward_kernel(
    group,
    ends_in,
    query_scale,
    sums,
    grad_own,
    out_grads,
    acts,
    cotangent,
    x_in,
    normal_in,
    query_full,
    query_t,
    key_t,
    key_n,
    value_n,
    w_qkv_in,
    logsum,
    dx_last,
    mlp_out,
    qkv_out,
    sums_out,
    normal,
    grad_att,
    grads_t,
    sum_keys,
    sum_values,
    sum_scale,
    w_own,
    w_core,
    w_y,
    w_eight,
    w_four,
    w_two,
    w_last,
    dx_own,
    dx_core,
    dx_x,
    w_qkv,
    dw,
    dw_y,
    dw_z_in,
    dw_far,
    dw_last,
    all_sums,
    got_sums,
    send_sem,
    recv_sem,
    local_sem,
):
    place = Place(group)
    core, y, quarter, narrow = place.core, place.y, place.quarter, place.narrow
    collector = place.collector
    other_core = jnp.logical_not(collector)
    mid = dx_last.shape[1]
    rows = 2 * mid
    slab = qkv_out.shape[2]
    cols = qkv_out.shape[3]
    pair_cols = 2 * cols
    cols_y = part(y, pair_cols)
    cols_other = part(1 - y, pair_cols)
    x_dev, z_dev, far_dev = (
        place.along_narrow(1),
        place.along_narrow(2),
        place.along_narrow(group),
    )
    core_dev, y_dev = place.along_wide(1), place.along_wide(2)
    wires = Wires(send_sem, recv_sem)
    scale = scale_column(query_scale)
    dxs = w_core

    trade = wires.trade

    act_loads = [
        pltpu.make_async_copy(source, normal.at[slot], local_sem.at[12 + slot])
        for slot, source in enumerate((acts.at[0], acts.at[1], acts.at[2], cotangent))
    ]
    for one in act_loads:
        one.start()
    greet(place, group)

    heads = query_t.shape[0]
    att_first = wires.ids(4 * heads)

    def att_out(head, to_core, to_x):
        target = place.half * group + core * 2 + to_x
        return wires.copy(
            grad_own.at[to_core, head, to_x],
            grad_att.at[head, :, part(quarter, rows)],
            place.at(to_core, target),
            att_first + (to_core * 2 + to_x) * heads + head,
            att_first + quarter * heads + head,
        )

    def att_local(to_core, to_x):
        return collector & (core == to_core) & (place.x == to_x)

    def att_in(head, mask):
        peer = flip(quarter, mask)
        there = grad_att.at[head, :, part(peer, rows)]
        return wires.copy(there, there, core_dev, att_first + peer * heads + head)

    def block_at(index, row):
        low = 1 - lax.div(index, 2)
        high = lax.rem(index + 1, 2) * lax.div(index, 2) + lax.rem(index, 2) * low
        row = jnp.where(low == 1, flip(row, 1), row)
        return jnp.where(high == 1, flip(row, 2), row)

    def head_at(index):
        return block_at(jnp.int32(index), place.column)

    for index in range(heads):
        head = block_at(jnp.int32(index), place.half * 2 + core)
        for to_core in range(2):
            for to_x in range(2):
                pl.when(jnp.logical_not(att_local(to_core, to_x)))(
                    lambda head=head, to_core=to_core, to_x=to_x: att_out(
                        head, to_core, to_x
                    ).start()
                )

        @pl.when(collector)
        def _():
            grad_att[head, :, part(quarter, rows)] = grad_own[core, head, place.x]

    span_m = w_own.shape[1]

    def core_rows(m):
        return slice(m * span_m, (m + 1) * span_m)

    arrived = [None] * 3
    arrived[0] = [trade(lambda: (out_grads.at[1 - core], w_core.at[core_rows(0)], core_dev))]

    def load_own():
        return pltpu.make_async_copy(out_grads.at[core], w_own.at[0], local_sem.at[0])

    def load_normal():
        return pltpu.make_async_copy(normal_in, normal, local_sem.at[3])

    def load_qkv():
        return pltpu.make_async_copy(w_qkv_in, w_qkv, local_sem.at[4])

    load_own().start()

    def give_half(m, left, right, place_for):
        def half(which):
            return product(left[:, part(which, span_m)], right, 0, 0).astype(LOW)

        place_for[0:2] = half(1 - core).reshape((2,) + place_for.shape[1:])
        count = place_for.shape[1]
        arrived[m] = [
            trade(
                lambda k=k: (
                    place_for.at[k // count, k % count],
                    w_core.at[m * span_m + k * slab : m * span_m + (k + 1) * slab],
                    core_dev,
                )
            )
            for k in range(2 * count)
        ]
        w_own[m] = half(core)

    for one in act_loads:
        one.wait()
    first_given = len(wires.sent)
    give_half(1, normal.at[0], normal[1], dw)
    give_half(2, normal.at[2], normal[3], w_qkv)
    given = wires.sent[first_given:]
    del wires.sent[first_given:]
    load_normal().start()

    def given_gone():
        for _, out in given:
            out().wait_send()
        load_qkv().start()
        load_normal().wait()

    masks = {"x": 1, "z": 2, "f": group}
    devices = {"x": x_dev, "z": z_dev, "f": far_dev, "y": y_dev}
    every = tuple(o for o in range(2 * group))
    kept = [every] * 3
    landing = [None] * 3

    def block(m, mask, columns):
        return w_own.at[m, part(flip(narrow, mask), slab), columns]

    def add_to(target, source):
        target[...] = (target[...].astype(F32) + source[...].astype(F32)).astype(LOW)

    def y_rows(m, k):
        start = span_m + (m - 1) * span_m // 2 + k * slab
        return w_y.at[start : start + slab]

    def scatter(m, stage):
        for one in arrived[m]:
            one()
        if stage == 0:
            if m == 0:
                load_own().wait()
            add_rows(w_own.at[m], w_core.at[core_rows(m)], 128)
        elif SCATTER_ORDERS[m][stage - 1] == "y":
            columns = cols_y
            if stage == 1:
                add_rows(w_own.at[m, :, cols_y], w_y.at[:span_m], 128)
            else:
                for k, mask in enumerate(kept[m]):
                    add_to(block(m, mask, cols_y), y_rows(m, k))
        else:
            width = "y" in SCATTER_ORDERS[m][: stage - 1]
            for k, mask in enumerate(kept[m]):
                columns = cols_y if width else slice(None)
                add_to(block(m, mask, columns), landing[m](k))
        if stage == 4:
            total = w_own[m, part(narrow, slab), cols_y].astype(F32)
            arrived[m] = [last_step(total, mlp_out, m, w_last)]
            return
        way = SCATTER_ORDERS[m][stage]
        if way == "y":
            if stage == 0:
                arrived[m] = [
                    trade(lambda: (w_own.at[m, :, cols_other], w_y.at[:span_m], y_dev))
                ]
            else:
                arrived[m] = [
                    trade(
                        lambda k=k, mask=mask: (
                            block(m, mask, cols_other),
                            y_rows(m, k),
                            y_dev,
                        )
                    )
                    for k, mask in enumerate(kept[m])
                ]
            return
        bit = masks[way]
        width = "y" in SCATTER_ORDERS[m][:stage]
        columns = cols_y if width else slice(None)
        mine = tuple(o for o in kept[m] if not o & bit)
        buffers = {8: w_eight, 4: w_four, 2: w_two}
        buffer = buffers[len(kept[m])]

        def land(k, buffer=buffer, width=width):
            if width and buffer is w_eight:
                return buffer.at[m, k, :, : 2 * cols]
            return buffer.at[m, k]

        arrived[m] = [
            trade(lambda k=k, o=o: (block(m, o | bit, columns), land(k), devices[way]))
            for k, o in enumerate(mine)
        ]
        kept[m] = mine
        landing[m] = land

    def last_step(total, out_ref, m, buffer):
        mine = jnp.where(core == 0, total[:, :cols], total[:, cols:])
        theirs = jnp.where(core == 0, total[:, cols:], total[:, :cols])
        out_ref[m, core] = mine
        buffer[m] = theirs
        return trade(lambda: (buffer.at[m], out_ref.at[m, core], core_dev))

    def column_at(mask):
        return lax.div(flip(narrow, mask), 2)

    def dw_add(where, source):
        there = dw.at[:, where, :, cols_y]
        there[...] = (there[...].astype(F32) + source[...].astype(F32)).astype(LOW)

    def weight_grads(head):
        dw[:, head] = (
            product(
                grads_t[:, head].reshape(3 * HEAD_DIM, LEN), normal[...].reshape(LEN, -1)
            )
            .astype(LOW)
            .reshape(3, HEAD_DIM, -1)
        )

    def dw_y_copy(head, slot):
        return wires.copy(
            dw.at[:, head, :, cols_other], dw_y.at[:, head], y_dev, dw_first + slot
        )

    dw_first = wires.ids(heads)

    def dw_z_step():
        return [
            trade(
                lambda k=k, o=o: (dw.at[:, column_at(o), :, cols_y], dw_z_in.at[:, k], z_dev)
            )
            for k, o in enumerate((2, group + 2))
        ]

    def dw_far_step(came):
        came[1]()
        dw_add(column_at(group), dw_z_in.at[:, 1])
        return trade(lambda: (dw.at[:, column_at(group), :, cols_y], dw_far, far_dev))

    def dw_last_step(came, far):
        came[0]()
        dw_add(column_at(0), dw_z_in.at[:, 0])
        far()
        last = []
        for m in range(3):
            total = dw[m, place.column, :, cols_y].astype(F32) + dw_far[m].astype(F32)
            last.append(last_step(total, qkv_out, m, dw_last))
        return last

    ends = document_ends(ends_in)
    sum_scale[...] = jnp.zeros_like(sum_scale)

    steps = {}

    def at_step(step, action):
        steps.setdefault(step, []).append(action)

    came = {}

    def rows_in(slot):
        dw_y_copy(head_at(slot), slot).wait_recv()
        dw_add(head_at(slot), dw_y.at[:, head_at(slot)])

    def rows_on():
        came["dw_z"] = dw_z_step()

    at_step((0, 1), given_gone)
    at_step((0, 0), lambda: scatter(0, 0))
    at_step((1, 0), lambda: scatter(2, 0))
    at_step((1, 0), lambda: scatter(1, 0))
    at_step((2, 0), lambda: scatter(0, 1))
    at_step((3, 0), lambda: rows_in(0))
    at_step((3, 1), lambda: scatter(1, 1))
    at_step((3, 1), lambda: rows_in(1))
    at_step((3, 1), rows_on)

    def between(index, point):
        for (wanted, where), actions in steps.items():
            if where == point:

                @pl.when(index == wanted)
                def _():
                    for action in actions:
                        action()

    def one_head(index, carry):
        head = head_at(index)
        between(index, 0)
        wait_if(other_core, lambda: att_in(head, 0))
        for mask in range(1, group):
            att_in(head, mask).wait_recv()
        backward_head(
            head,
            ends,
            query_t,
            query_full,
            key_n,
            key_t,
            value_n,
            grad_att,
            logsum,
            scale,
            grads_t,
            sum_keys,
            sum_values,
            sum_scale,
            lambda: between(index, 1),
        )

        @pl.when(index < heads - 1)
        def _():
            weight_grads(head)
            dw_y_copy(head, index).start()

        return carry

    lax.fori_loop(0, heads, one_head, 0)

    size = 3 * heads * HEAD_DIM
    load_qkv().wait()

    def kept_rows(mask):
        if mask == 0:
            return dx_own
        start = (group + mask - 1) * mid
        return dxs.at[start : start + mid]

    def grad_inputs(mask):
        first = flip(quarter, mask) * 2
        weight = w_qkv[...].reshape(size, -1)

        def half_rows(which):
            span = part(first + which, mid)
            return product(grads_t[:, :, :, span].reshape(size, mid), weight, 0, 0).astype(LOW)

        there = slice(mask * mid, (mask + 1) * mid)
        dxs[there] = half_rows(1 - core)
        out = trade(lambda: (dxs.at[there], dx_core.at[mask], core_dev))
        kept_rows(mask)[...] = half_rows(core)
        return out

    def add_core(mask, came):
        came()
        add_rows(kept_rows(mask), dx_core.at[mask], 128)

    from_core = {}
    last_first = wires.ids(2)

    def last_out():
        return wires.copy(
            kept_rows(2),
            dx_last.at[core],
            place.at(place.z, flip(narrow, 2)),
            last_first,
            last_first + core,
        )

    def last_core():
        return wires.copy(kept_rows(0), dx_last.at[core], core_dev, last_first + 1, last_first + core)

    def last_in(which):
        return wires.copy(dx_last.at[which], dx_last.at[which], core_dev, last_first + which)

    sum_devices = [core_dev, place.along_wide(3)] + [
        (flip(place.wide, 1), flip(narrow, mask)) for mask in (1, 2, group)
    ]

    def sum_step(stage):
        return trade(lambda: (all_sums.at[stage], got_sums.at[stage], sum_devices[stage]))

    def sum_add(stage, came):
        came()
        all_sums[stage + 1] = all_sums[stage] + got_sums[stage]

    scatter(0, 2)
    from_core[3] = grad_inputs(3)
    add_core(3, from_core[3])
    from_x3 = trade(lambda: (kept_rows(3), dx_x.at[1], x_dev))
    scatter(0, 3)
    from_core[1] = grad_inputs(1)
    from_core[0] = grad_inputs(0)
    from_core[2] = grad_inputs(2)
    add_core(1, from_core[1])
    from_x1 = trade(lambda: (kept_rows(1), dx_x.at[0], x_dev))
    scatter(1, 2)
    add_core(0, from_core[0])
    rows_in(2)
    dw_f = dw_far_step(came["dw_z"])
    add_core(2, from_core[2])
    raw = [
        pltpu.make_async_copy(
            x_in.at[flip(quarter, mask), part(core, mid)], dx_core.at[mask], local_sem.at[6 + mask]
        )
        for mask in range(group)
    ]
    for one in raw:
        one.start()
    for one in raw:
        one.wait()
    all_sums[0] = sums[...]
    all_sums[0, 3:4, :HEAD_DIM] = jnp.sum(sum_scale[...].T, axis=0, keepdims=True)
    for mask in range(group):

        def gain_rows(span, mask=mask):
            inputs = dx_core[mask, span, :].astype(F32)
            normed = inputs * norm_rows(inputs)
            terms = kept_rows(mask)[span, :].astype(F32) * normed
            all_sums[0, 4:5, :] += jnp.sum(terms, axis=0, keepdims=True)

        chunks(mid, 128, gain_rows)

    sums_now = sum_step(0)
    from_x3()
    add_rows(kept_rows(2), dx_x.at[1], 128)
    last_out().start()
    wires.sent.append((None, last_out))
    scatter(2, 1)
    weight_grads(head_at(heads - 1))
    dw_y_copy(head_at(heads - 1), heads - 1).start()
    scatter(1, 3)
    sum_add(0, sums_now)
    sums_now = sum_step(1)
    scatter(0, 4)
    scatter(2, 2)
    rows_in(3)
    scatter(2, 3)
    sum_add(1, sums_now)
    sums_now = sum_step(2)
    scatter(1, 4)
    from_x1()
    add_rows(kept_rows(0), dx_x.at[0], 128)
    wires.start_if(other_core, last_core)

    @pl.when(collector)
    def _():
        dx_last[core] = dx_own[...]

    sum_add(2, sums_now)
    sums_now = sum_step(3)
    last = dw_last_step(came["dw_z"], dw_f)
    sum_add(3, sums_now)
    sums_now = sum_step(4)
    for which in range(2):
        wait_if(
            jnp.logical_not(collector & (core == which)), lambda which=which: last_in(which)
        )

    scatter(2, 4)
    sum_add(4, sums_now)
    sums_out[...] = all_sums[5]

    for one in last + arrived[0] + arrived[1] + arrived[2]:
        one()
    for slot in range(heads):
        dw_y_copy(head_at(slot), slot).wait_send()

    def finish_send(head, carry):
        for to_core in range(2):
            for to_x in range(2):
                pl.when(jnp.logical_not(att_local(to_core, to_x)))(
                    lambda to_core=to_core, to_x=to_x: att_out(head, to_core, to_x).wait_send()
                )
        return carry

    lax.fori_loop(0, heads, finish_send, 0)
    wires.finish()


def final_kernel(
    tokens, gain, grad_rows, grad_middle, result, mlp_raw, qkv_raw, sums, query_scale,
    tokens_out, result_out, qkv_out, out_out, up_out, down_out,
    up_bias_out, bias_out, attn_out, mlp_out, scale_out,
):
    inputs = tokens[...].astype(F32)
    inverse = norm_rows(inputs)
    normed = inputs * inverse
    scaled = grad_rows[...].astype(F32) * gain[...].reshape(1, -1)
    inner = jnp.mean(scaled * normed, axis=1, keepdims=True)
    tokens_out[...] = grad_middle[...] + inverse * (scaled - normed * inner)
    result_out[...] = result[...]

    @pl.when(pl.program_id(0) == 0)
    def _():
        qkv_out[...] = qkv_raw[...]
        out_out[...] = mlp_raw[0]
        up_out[...] = mlp_raw[1]
        down_out[...] = mlp_raw[2]
        count, slab = sums.shape[1], up_bias_out.shape[0] // 2
        shift = lax.rem(count - slab * lax.axis_index("narrow"), count)
        here = pltpu.roll(sums[...], shift, 1)[2:3]
        both = [here[:, :slab], here[:, count // 2 : count // 2 + slab]]
        up_bias_out[...] = jnp.concatenate(both, axis=1)[0, :]
        mlp_out[...] = sums[0, :]
        bias_out[...] = sums[1, :]
        attn_out[...] = sums[4, :]
        slope = 1.0 / (1.0 + jnp.exp(-query_scale[...].reshape(1, -1)))
        terms = sums[3:4, :HEAD_DIM] * (LOG_TWO_E / math.sqrt(HEAD_DIM)) * slope
        scale_out[...] = terms[0, :]


def struct(shape, dtype):
    return jax.ShapeDtypeStruct(shape, dtype)


def kernel_call(kernel, outputs, in_specs, out_spaces, scratch, collective_id=None):
    extra = {} if collective_id is None else {"collective_id": collective_id, "has_side_effects": True}
    return pl.pallas_call(
        kernel,
        out_shape=tuple(outputs),
        in_specs=[pl.BlockSpec(memory_space=space) for space in in_specs],
        out_specs=tuple(pl.BlockSpec(memory_space=space) for space in out_spaces),
        scratch_shapes=scratch,
        compiler_params=pltpu.CompilerParams(vmem_limit_bytes=VMEM_LIMIT, **extra),
    )


def fused_device(
    group,
    tokens,
    lengths,
    qkv_weight,
    out_weight,
    up_weight,
    up_bias,
    down_weight,
    down_bias,
    attn_gain,
    mlp_gain,
    query_scale,
    cotangent,
):
    rows, dim = tokens.shape
    slab2, cols = out_weight.shape
    slab = slab2 // 2
    halves = lengths.shape[0]
    heads = halves * slab2 // HEAD_DIM
    local = heads * HEAD_DIM
    narrow_count = group * halves
    hidden = slab2 * narrow_count
    vmem, smem, anywhere = pltpu.VMEM, pltpu.SMEM, pl.ANY

    att_shape = (2, heads, 2, HEAD_DIM, rows)
    wq_shape = (3, heads, slab, dim)
    wm_shape = (3, 2, narrow_count * slab, dim)
    dma = pltpu.SemaphoreType.DMA

    forward_outputs = [
        struct((group, rows, dim), LOW),
        struct((group, rows, dim), LOW),
        struct((local, LEN), F32),
        struct((heads, HEAD_DIM, LEN), LOW),
        struct((heads, HEAD_DIM, LEN), LOW),
        struct((heads, LEN, HEAD_DIM), LOW),
        struct((heads, LEN, HEAD_DIM), LOW),
        struct(wq_shape, LOW),
        struct((heads, 1, LEN), F32),
        struct((rows, dim), LOW),
        struct((rows, dim), F32),
        struct(att_shape, LOW),
        struct(wm_shape[1:], LOW),
        struct((3, rows, dim), LOW),
        struct((8, dim), F32),
        struct((8, 128), F32),
    ]
    (
        x_all,
        normal,
        query_full,
        query_t,
        key_t,
        key_n,
        value_n,
        w_qkv,
        logsum,
        result,
        grad_middle,
        grad_att,
        out_grads,
        acts,
        sums,
        ends,
    ) = kernel_call(
        functools.partial(forward_kernel, group),
        forward_outputs,
        [smem] + [vmem] * 11,
        [anywhere] * (len(forward_outputs) - 2) + [vmem] * 2,
        [
            vmem((group, rows, dim), LOW),
            vmem((group, rows, dim), LOW),
            vmem((6, slab2, cols), LOW),
            vmem(wq_shape, LOW),
            vmem(wm_shape, LOW),
            vmem((6, slab, 2 * cols), LOW),
            vmem((6, slab, cols), LOW),
            vmem((narrow_count, 8, slab2), F32),
            vmem((1, hidden), F32),
            vmem((8, 128), F32),
            vmem((8, 128), F32),
            vmem((local, LEN), F32),
            vmem((heads, HEAD_DIM, LEN), LOW),
            vmem((heads, HEAD_DIM, LEN), LOW),
            vmem((heads, HEAD_DIM, LEN), LOW),
            vmem((heads, LEN, HEAD_DIM), LOW),
            vmem((heads, LEN, HEAD_DIM), LOW),
            vmem((heads, 1, LEN), F32),
            vmem((heads, HEAD_DIM, LEN), LOW),
            vmem(att_shape, LOW),
            vmem(att_shape, LOW),
            vmem((rows, dim), F32),
            dma((110,)),
            dma((110,)),
            dma((16,)),
        ],
        collective_id=0,
    )(
        lengths,
        tokens,
        jnp.swapaxes(qkv_weight, 1, 2),
        out_weight,
        up_weight.T,
        up_bias,
        down_weight,
        down_bias,
        attn_gain,
        mlp_gain,
        query_scale,
        cotangent,
    )

    last_shape = (3, 2, slab, cols)
    grad_rows, mlp_grads, qkv_grads, totals = kernel_call(
        functools.partial(backward_kernel, group),
        [
            struct((2, rows // 2, dim), LOW),
            struct(last_shape, F32),
            struct(last_shape, F32),
            struct((8, dim), F32),
        ],
        [vmem] * 4 + [anywhere] * 5 + [vmem] * 5 + [anywhere, vmem],
        [vmem] * 4,
        [
            vmem((group, rows, dim), LOW),
            vmem((heads, HEAD_DIM, LEN), LOW),
            vmem((3, heads, HEAD_DIM, LEN), LOW),
            vmem((HEAD_DIM, LEN), F32),
            vmem((HEAD_DIM, LEN), F32),
            vmem((HEAD_DIM, TILE // 2), F32),
            vmem((3, narrow_count * slab, dim), LOW),
            vmem((3 * narrow_count * slab, dim), LOW),
            vmem((2 * narrow_count * slab, 2 * cols), LOW),
            vmem((3, 4, slab, dim), LOW),
            vmem((3, 2, slab, 2 * cols), LOW),
            vmem((3, 1, slab, 2 * cols), LOW),
            vmem((3, slab, cols), F32),
            vmem((rows // 2, dim), LOW),
            vmem((group, rows // 2, dim), LOW),
            vmem((2, rows // 2, dim), LOW),
            vmem(wq_shape, LOW),
            vmem(wq_shape, LOW),
            vmem((3, heads, slab, 2 * cols), LOW),
            vmem((3, 2, slab, 2 * cols), LOW),
            vmem((3, slab, 2 * cols), LOW),
            vmem((3, slab, cols), F32),
            vmem((6, 8, dim), F32),
            vmem((5, 8, dim), F32),
            dma((100,)),
            dma((100,)),
            dma((16,)),
        ],
        collective_id=1,
    )(
        ends,
        query_scale,
        sums,
        grad_att,
        out_grads,
        acts,
        cotangent,
        x_all,
        normal,
        query_full,
        query_t,
        key_t,
        key_n,
        value_n,
        w_qkv,
        logsum,
    )


    def block(*shape):
        return pl.BlockSpec(shape, lambda step: (0,) * len(shape))

    row_block = pl.BlockSpec((rows // 4, dim), lambda step: (step, 0))
    outputs = [
        (row_block, struct((rows, dim), F32)),
        (row_block, struct((rows, dim), LOW)),
        (block(3, slab2, cols), struct((3, slab2, cols), F32)),
    ]
    outputs += [(block(slab2, cols), struct((slab2, cols), F32))] * 3
    outputs += [
        (block(size), struct((size,), F32)) for size in (slab2, dim, dim, dim, HEAD_DIM)
    ]
    (
        grad_tokens,
        result,
        grad_qkv,
        grad_out,
        grad_up,
        grad_down,
        grad_up_bias,
        grad_down_bias,
        grad_attn_gain,
        grad_mlp_gain,
        grad_scale,
    ) = pl.pallas_call(
        final_kernel,
        grid=(4,),
        out_shape=tuple(shape for _, shape in outputs),
        in_specs=[
            row_block,
            block(dim),
            row_block,
            row_block,
            row_block,
            block(3, slab2, cols),
            block(3, slab2, cols),
            block(8, dim),
            block(HEAD_DIM),
        ],
        out_specs=tuple(spec for spec, _ in outputs),
    )(
        tokens,
        attn_gain,
        grad_rows.reshape(rows, dim),
        grad_middle,
        result,
        mlp_grads.reshape(3, slab2, cols),
        qkv_grads.reshape(3, slab2, cols),
        totals,
        query_scale,
    )
    return (
        result,
        grad_tokens,
        jnp.swapaxes(grad_qkv, 1, 2),
        grad_out,
        grad_up.T,
        grad_up_bias,
        grad_down,
        grad_down_bias,
        grad_attn_gain,
        grad_mlp_gain,
        grad_scale,
    )


def solution(mesh):
    wide_count, narrow_count = mesh.shape["wide"], mesh.shape["narrow"]

    def per_device(*args):
        tokens, lengths, out_weight = args[0], args[1], args[3]
        group = LEN // tokens.shape[0]
        fits = (
            wide_count == 4
            and group == 4
            and narrow_count == group * lengths.shape[0] == 8
            and out_weight.shape[0] == 2 * HEAD_DIM
            and 2 * out_weight.shape[1] % 128 == 0
        )
        if fits:
            return fused_device(group, *args)
        return general_device(*args)

    return jax.shard_map(
        per_device,
        mesh=mesh,
        in_specs=(
            P(("wide", "narrow"), None),
            P("wide", None),
            P(None, "wide", "narrow"),
            P("narrow", "wide"),
            P("wide", "narrow"),
            P("narrow"),
            P("narrow", "wide"),
            P(),
            P(),
            P(),
            P(),
            P(("wide", "narrow"), None),
        ),
        out_specs=(
            P(("wide", "narrow"), None),
            P(("wide", "narrow"), None),
            P(None, "wide", "narrow"),
            P("narrow", "wide"),
            P("wide", "narrow"),
            P("narrow"),
            P("narrow", "wide"),
            P(),
            P(),
            P(),
            P(),
        ),
        check_vma=False,
    )
```

```python
import functools
import math

import jax
import jax.numpy as jnp
from jax import lax
from jax.experimental import pallas as pl
from jax.experimental.pallas import tpu as pltpu
from jax.sharding import PartitionSpec as P

HEAD_DIM = 80
LEN = 2048
WINDOW = 1024
BLOCK = 512
NDOC = 4
TILE = 256

LOG_TWO_E = 1.4426950408889634
EPSILON = 1e-06
NEG_FILL = -1e30

F32 = jnp.float32
LOW = jnp.bfloat16
MESH = pl.DeviceIdType.MESH
VMEM_LIMIT = 63 * 2**20


def group_rows(values):
    return lax.all_gather(values, "narrow", axis=0, tiled=True)


def group_parts(values):
    return lax.psum_scatter(values, "narrow", scatter_dimension=0, tiled=True)


def contract_last(left, right):
    return lax.dot_general(
        left, right, (((1,), (1,)), ((), ())), preferred_element_type=jnp.float32
    )


def contract_first(left, right):
    return lax.dot_general(
        left, right, (((0,), (0,)), ((), ())), preferred_element_type=jnp.float32
    )


def norm_share(inputs, norm_gain):
    inverse = lax.rsqrt(jnp.mean(inputs * inputs, axis=1) + EPSILON)
    normed = inputs * inverse[:, None]
    return (inverse, normed, (normed * norm_gain).astype(jnp.bfloat16))


def norm_back(grad_normal, norm_gain, inverse, normed):
    scaled = grad_normal * norm_gain
    inner_dots = jnp.mean(scaled * normed, axis=1)
    grad_inputs = inverse[:, None] * (scaled - normed * inner_dots[:, None])
    return (grad_inputs, jnp.sum(grad_normal * normed, axis=0))


def segment_ids(lengths_row):
    positions = jnp.arange(LEN, dtype=jnp.int32)
    ends = jnp.cumsum(lengths_row)
    return jnp.sum((positions[:, None] >= ends[None, :]).astype(jnp.int32), axis=1)


def block_mask(segments, padded_seg, offset):
    query_pos = offset + jnp.arange(BLOCK, dtype=jnp.int32)
    key_pos = offset - WINDOW + jnp.arange(WINDOW + BLOCK, dtype=jnp.int32)
    query_seg = segments[offset : offset + BLOCK]
    key_seg = padded_seg[offset : offset + WINDOW + BLOCK]
    spacing = query_pos[:, None] - key_pos[None, :]
    same_doc = query_seg[:, None] == key_seg[None, :]
    inside = (spacing >= 0) & (spacing < WINDOW)
    real_doc = (query_seg[:, None] < NDOC) | (spacing == 0)
    return same_doc & inside & real_doc


def padded_inputs(keys_in, values_in, segments):
    pad_rows = jnp.zeros((WINDOW,) + keys_in.shape[1:], keys_in.dtype)
    keys_pad = jnp.concatenate([pad_rows, keys_in], axis=0)
    values_pad = jnp.concatenate([pad_rows, values_in], axis=0)
    padded_seg = jnp.concatenate([jnp.full((WINDOW,), -2, jnp.int32), segments])
    return (keys_pad, values_pad, padded_seg)


def attend_forward(queries, keys_in, values_in, segments):
    keys_pad, values_pad, padded_seg = padded_inputs(keys_in, values_in, segments)
    outputs = []
    logsums = []
    for block_index in range(LEN // BLOCK):
        offset = block_index * BLOCK
        query_block = queries[offset : offset + BLOCK]
        key_block = keys_pad[offset : offset + WINDOW + BLOCK]
        value_block = values_pad[offset : offset + WINDOW + BLOCK]
        allowed = block_mask(segments, padded_seg, offset)
        scores = jnp.einsum(
            "ihd,jhd->hij", query_block, key_block, preferred_element_type=jnp.float32
        )
        masked = jnp.where(allowed[None], scores, NEG_FILL)
        maxima = jnp.max(masked, axis=2)
        exponent = jnp.exp(masked - maxima[:, :, None])
        totals = jnp.sum(exponent, axis=2)
        probs_low = (exponent / totals[:, :, None]).astype(jnp.bfloat16)
        block_out = jnp.einsum(
            "hij,jhd->ihd", probs_low, value_block, preferred_element_type=jnp.float32
        )
        outputs.append(block_out.astype(jnp.bfloat16))
        logsums.append(maxima + jnp.log(totals))
    return (jnp.concatenate(outputs, axis=0), jnp.concatenate(logsums, axis=1))


def attend_backward(queries, keys_in, values_in, segments, logsum, grad_out):
    keys_pad, values_pad, padded_seg = padded_inputs(keys_in, values_in, segments)
    grad_keys = jnp.zeros(keys_pad.shape, jnp.float32)
    grad_values = jnp.zeros(values_pad.shape, jnp.float32)
    grad_queries = []
    for block_index in range(LEN // BLOCK):
        offset = block_index * BLOCK
        query_block = queries[offset : offset + BLOCK]
        key_block = keys_pad[offset : offset + WINDOW + BLOCK]
        value_block = values_pad[offset : offset + WINDOW + BLOCK]
        grad_block = grad_out[offset : offset + BLOCK]
        allowed = block_mask(segments, padded_seg, offset)
        scores = jnp.einsum(
            "ihd,jhd->hij", query_block, key_block, preferred_element_type=jnp.float32
        )
        masked = jnp.where(allowed[None], scores, NEG_FILL)
        soft_probs = jnp.exp(masked - logsum[:, offset : offset + BLOCK, None])
        probs_low = soft_probs.astype(jnp.bfloat16)
        grad_probs = jnp.einsum(
            "ihd,jhd->hij", grad_block, value_block, preferred_element_type=jnp.float32
        )
        inner_sums = jnp.sum(soft_probs * grad_probs, axis=2)
        grad_scores = (soft_probs * (grad_probs - inner_sums[:, :, None])).astype(jnp.bfloat16)
        grad_queries.append(
            jnp.einsum("hij,jhd->ihd", grad_scores, key_block, preferred_element_type=jnp.float32)
        )
        key_terms = jnp.einsum(
            "hij,ihd->jhd", grad_scores, query_block, preferred_element_type=jnp.float32
        )
        value_terms = jnp.einsum(
            "hij,ihd->jhd", probs_low, grad_block, preferred_element_type=jnp.float32
        )
        grad_keys = grad_keys.at[offset : offset + WINDOW + BLOCK].add(key_terms)
        grad_values = grad_values.at[offset : offset + WINDOW + BLOCK].add(value_terms)
    return (jnp.concatenate(grad_queries, axis=0), grad_keys[WINDOW:], grad_values[WINDOW:])


def silu_slope(hidden_pre):
    sigmoid_pre = jax.nn.sigmoid(hidden_pre)
    return sigmoid_pre * (1.0 + hidden_pre * (1.0 - sigmoid_pre))


def general_device(
    tokens,
    lengths,
    qkv_weight,
    out_weight,
    up_weight,
    up_bias,
    down_weight,
    down_bias,
    attn_gain,
    mlp_gain,
    query_scale,
    cotangent,
):
    head_count = qkv_weight.shape[2] // HEAD_DIM
    seq_count = lengths.shape[0]
    row_count = seq_count * LEN

    def by_sequence(values):
        return values.reshape((seq_count, LEN) + values.shape[1:])

    qkv_full, out_full, up_full, down_full = (
        lax.all_gather(qkv_weight, "wide", axis=1, tiled=True),
        lax.all_gather(out_weight, "wide", axis=1, tiled=True),
        lax.all_gather(up_weight, "wide", axis=0, tiled=True),
        lax.all_gather(down_weight, "wide", axis=1, tiled=True),
    )
    segments = jax.vmap(segment_ids)(lengths)
    inputs = tokens.astype(jnp.float32)
    inverse_one, normed_one, normal_one = norm_share(inputs, attn_gain)
    rows_one = group_rows(normal_one)
    projected = jnp.einsum("td,cdn->ctn", rows_one, qkv_full, preferred_element_type=jnp.float32)
    scale_dim = LOG_TWO_E / math.sqrt(HEAD_DIM) * jax.nn.softplus(query_scale)
    query_heads = projected[0].reshape(row_count, head_count, HEAD_DIM)
    query_low = (query_heads * scale_dim).astype(jnp.bfloat16)
    key_low = projected[1].astype(jnp.bfloat16).reshape(row_count, head_count, HEAD_DIM)
    value_low = projected[2].astype(jnp.bfloat16).reshape(row_count, head_count, HEAD_DIM)
    attended, logsum = jax.vmap(attend_forward)(
        by_sequence(query_low), by_sequence(key_low), by_sequence(value_low), segments
    )
    attended_rows = attended.reshape(row_count, head_count * HEAD_DIM)
    middle = inputs + group_parts(
        jnp.dot(attended_rows, out_full, preferred_element_type=jnp.float32)
    )
    inverse_two, normed_two, normal_two = norm_share(middle, mlp_gain)
    grad_down_bias = jnp.sum(cotangent.astype(jnp.float32), axis=0)
    rows_two = group_rows(normal_two)
    hidden_pre = jnp.dot(rows_two, up_full, preferred_element_type=jnp.float32) + up_bias
    hidden_low = jax.nn.silu(hidden_pre).astype(jnp.bfloat16)
    branch_two = (
        group_parts(jnp.dot(hidden_low, down_full, preferred_element_type=jnp.float32)) + down_bias
    )
    result = middle + branch_two
    grad_rows = group_rows(cotangent)
    grad_hidden = contract_last(grad_rows, down_full)
    grad_pre = (grad_hidden * silu_slope(hidden_pre)).astype(jnp.bfloat16)
    grad_up = contract_first(rows_two, grad_pre)
    grad_down = contract_first(hidden_low, grad_rows)
    grad_up_bias = jnp.sum(grad_pre.astype(jnp.float32), axis=0)
    grad_normal_two = group_parts(contract_last(grad_pre, up_full))
    grad_middle_norm, grad_mlp_gain = norm_back(grad_normal_two, mlp_gain, inverse_two, normed_two)
    grad_middle = cotangent.astype(jnp.float32) + grad_middle_norm
    grad_branch = group_rows(grad_middle.astype(jnp.bfloat16))
    grad_attended = contract_last(grad_branch, out_full).astype(jnp.bfloat16)
    grad_out = contract_first(attended_rows, grad_branch)
    grad_scaled, grad_key, grad_value = jax.vmap(attend_backward)(
        by_sequence(query_low),
        by_sequence(key_low),
        by_sequence(value_low),
        segments,
        logsum,
        by_sequence(grad_attended.reshape(row_count, head_count, HEAD_DIM)),
    )
    grad_scaled = grad_scaled.reshape(row_count, head_count, HEAD_DIM)
    grad_scale_part = (
        jnp.sum(grad_scaled * query_heads, axis=(0, 1))
        * (LOG_TWO_E / math.sqrt(HEAD_DIM))
        * jax.nn.sigmoid(query_scale)
    )
    grad_projected = jnp.stack(
        [
            (grad_scaled * scale_dim).reshape(row_count, head_count * HEAD_DIM),
            grad_key.reshape(row_count, head_count * HEAD_DIM),
            grad_value.reshape(row_count, head_count * HEAD_DIM),
        ]
    ).astype(jnp.bfloat16)
    grad_qkv = jnp.einsum(
        "td,ctn->cdn", rows_one, grad_projected, preferred_element_type=jnp.float32
    )
    grad_normal_one = group_parts(
        jnp.einsum("ctn,cdn->td", grad_projected, qkv_full, preferred_element_type=jnp.float32)
    )
    grad_input_norm, grad_attn_gain = norm_back(grad_normal_one, attn_gain, inverse_one, normed_one)
    grad_tokens = grad_middle + grad_input_norm
    grad_qkv, grad_out, grad_up, grad_down = (
        lax.psum_scatter(grad_qkv, "wide", scatter_dimension=1, tiled=True),
        lax.psum_scatter(grad_out, "wide", scatter_dimension=1, tiled=True),
        lax.psum_scatter(grad_up, "wide", scatter_dimension=0, tiled=True),
        lax.psum_scatter(grad_down, "wide", scatter_dimension=1, tiled=True),
    )
    grad_attn_gain, grad_mlp_gain, grad_down_bias, grad_scale = lax.psum(
        (grad_attn_gain, grad_mlp_gain, grad_down_bias, grad_scale_part), ("wide", "narrow")
    )
    grad_up_bias = lax.psum(grad_up_bias, "wide")
    return (
        result.astype(jnp.bfloat16),
        grad_tokens,
        grad_qkv,
        grad_out,
        grad_up,
        grad_up_bias,
        grad_down,
        grad_down_bias,
        grad_attn_gain,
        grad_mlp_gain,
        grad_scale,
    )


def product(left, right, left_dim=1, right_dim=0):
    return lax.dot_general(
        left, right, (((left_dim,), (right_dim,)), ((), ())), preferred_element_type=F32
    )


def flip(value, mask):
    bit = 1
    while bit <= mask:
        if mask & bit:
            value = value + bit * (1 - 2 * lax.rem(lax.div(value, bit), 2))
        bit *= 2
    return value


def part(start, size):
    return pl.ds(pl.multiple_of(start * size, size), size)


def chunks(total, size, body):
    def step(index, carry):
        body(part(index, size))
        return carry

    lax.fori_loop(0, total // size, step, 0)


def add_rows(target, source, size):
    def body(span):
        target[span, :] = (target[span, :].astype(F32) + source[span, :].astype(F32)).astype(LOW)

    chunks(source.shape[0], size, body)


class Place:
    def __init__(self, group):
        self.wide = lax.axis_index("wide")
        self.narrow = lax.axis_index("narrow")
        self.core = lax.rem(self.wide, 2)
        self.y = lax.div(self.wide, 2)
        self.quarter = lax.rem(self.narrow, group)
        self.half = lax.div(self.narrow, group)
        self.x = lax.rem(self.narrow, 2)
        self.z = lax.div(self.quarter, 2)
        self.column = lax.div(self.narrow, 2)
        self.collector = self.core == self.z

    def along_wide(self, mask):
        return (flip(self.wide, mask), self.narrow)

    def along_narrow(self, mask):
        return (self.wide, flip(self.narrow, mask))

    def at(self, core, narrow):
        return (self.y * 2 + core, narrow)


def greet(place, group):
    barrier = pltpu.get_barrier_semaphore()
    peers = [place.along_narrow(m) for m in range(1, 2 * group)]
    peers += [place.along_wide(m) for m in (1, 2, 3)]
    peers += [(flip(place.wide, 1), flip(place.narrow, m)) for m in range(1, group + 1)]
    for peer in peers:
        pl.semaphore_signal(barrier, inc=1, device_id=peer, device_id_type=MESH)
    pl.semaphore_wait(barrier, len(peers))


class Wires:
    def __init__(self, send_sem, recv_sem):
        self.send_sem, self.recv_sem = send_sem, recv_sem
        self.next_id = 0
        self.sent = []

    def ids(self, count):
        first = self.next_id
        self.next_id += count
        assert self.next_id <= self.send_sem.shape[0]
        return first

    def copy(self, source, target, device, index, arrival=None):
        return pltpu.make_async_remote_copy(
            src_ref=source,
            dst_ref=target,
            send_sem=self.send_sem.at[index],
            recv_sem=self.recv_sem.at[index if arrival is None else arrival],
            device_id=device,
            device_id_type=MESH,
        )

    def exchange(self, source, target, incoming, device):
        index = self.ids(1)
        out = self.copy(source, target, device, index)
        out.start()
        self.sent.append((None, lambda: out))
        return self.copy(incoming, incoming, device, index)

    def trade(self, make):
        index = self.ids(1)

        def out():
            source, target, device = make()
            return self.copy(source, target, device, index)

        out().start()
        self.sent.append((None, out))

        def arrive():
            _, target, device = make()
            self.copy(target, target, device, index).wait_recv()

        return arrive

    def start_if(self, condition, make):
        pl.when(condition)(lambda: make().start())
        self.sent.append((condition, make))

    def finish(self, conditional=(True, False)):
        for condition, make in self.sent:
            if (condition is not None) not in conditional:
                continue
            if condition is None:
                make().wait_send()
            else:
                pl.when(condition)(lambda make=make: make().wait_send())
        self.sent = [one for one in self.sent if (one[0] is not None) not in conditional]


def wait_if(condition, make):
    pl.when(condition)(lambda: make().wait_recv())


def ends_row(lengths, row):
    lane = lax.broadcasted_iota(jnp.int32, (8, 128), 1)
    result, total = jnp.zeros((8, 128), jnp.int32), 0
    for index in range(NDOC):
        total = total + lengths[row, index]
        result = jnp.where(lane == index, total, result)
    return result.astype(F32)


def document_ends(row):
    return [
        jnp.broadcast_to(row[0:1, k : k + 1], (1, TILE)).astype(jnp.int32) for k in range(NDOC)
    ]


def first_key(ends, offset):
    position = offset + lax.broadcasted_iota(jnp.int32, (1, TILE), 1)
    start = jnp.zeros_like(position)
    for end in ends:
        start = jnp.where(position >= end, end, start)
    start = jnp.maximum(start, position - (WINDOW - 1))
    return jnp.where(position >= ends[-1], position, start), position


def allowed_scores(scores, key_start, offset, first, position):
    key = key_start + lax.broadcasted_iota(jnp.int32, scores.shape, 0)
    allowed = key >= first
    if key_start + scores.shape[0] > offset:
        allowed = allowed & (key <= position)
    return jnp.where(allowed, scores, NEG_FILL)


def tile_keys(tile):
    offset = tile * TILE
    return offset, range(max(0, offset - WINDOW), offset + TILE, TILE)


def pipelined(tiles, first_half, second_half):
    waiting = None
    for tile in tiles:
        current = (tile, first_half(tile))
        if waiting is not None:
            second_half(*waiting)
        waiting = current
    second_half(*waiting)


def attend_head(head, ends, queries, keys, values_t, attended, logsum):
    def first_half(tile):
        offset, starts = tile_keys(tile)
        first, position = first_key(ends, offset)
        query = queries[head, :, offset : offset + TILE]
        blocks, maxima = [], None
        for start in starts:
            scores = product(keys[head, start : start + TILE, :], query)
            scores = allowed_scores(scores, start, offset, first, position)
            top = jnp.max(scores, axis=0, keepdims=True)
            maxima = top if maxima is None else jnp.maximum(maxima, top)
            blocks.append(scores)
        return blocks, maxima

    def second_half(tile, held):
        blocks, maxima = held
        offset, starts = tile_keys(tile)
        total, output = None, None
        for scores, start in zip(blocks, starts):
            exponent = jnp.exp(scores - maxima)
            share = jnp.sum(exponent, axis=0, keepdims=True)
            term = product(values_t[head, :, start : start + TILE], exponent.astype(LOW))
            total, output = (
                (share, term) if total is None else (total + share, output + term)
            )
        attended[head, :, offset : offset + TILE] = (output * (1.0 / total)).astype(LOW)
        logsum[head, :, offset : offset + TILE] = maxima + jnp.log(total)

    pipelined(range(LEN // TILE), first_half, second_half)


def norm_rows(inputs):
    return lax.rsqrt(jnp.mean(inputs * inputs, axis=1, keepdims=True) + EPSILON)


def scale_column(query_scale):
    values = query_scale[...].reshape(1, -1)
    softplus = jnp.maximum(values, 0.0) + jnp.log(1.0 + jnp.exp(-jnp.abs(values)))
    row = LOG_TWO_E / math.sqrt(HEAD_DIM) * softplus
    return jnp.broadcast_to(row, (128, HEAD_DIM)).T[:, :1]


GATHER_ORDERS = ("zfy", "fyz", "fzy", "zxfy", "fyxz", "fzyx")


def forward_kernel(
    group,
    lengths,
    tokens_in,
    qkv_weight,
    out_weight,
    up_weight,
    up_bias_in,
    down_weight,
    down_bias_in,
    attn_gain,
    mlp_gain,
    query_scale,
    cotangent_in,
    x_out,
    normal_out,
    qf_out,
    q_out,
    kt_out,
    kn_out,
    vn_out,
    wq_out,
    lse_out,
    result_out,
    middle_out,
    att_out,
    wo_out,
    acts_out,
    sums,
    ends_out,
    tokens,
    cotangent,
    x_all,
    normal,
    shards,
    w_qkv,
    w_mlp,
    w_pair,
    w_half,
    bias_all,
    bias_row,
    ends_own,
    ends_other,
    query_full,
    query_t,
    key_t,
    value_t,
    key_n,
    value_n,
    logsum,
    attended,
    att_all,
    grad_att,
    grad_middle,
    send_sem,
    recv_sem,
    local_sem,
):
    place = Place(group)
    core, y, quarter, narrow = place.core, place.y, place.quarter, place.narrow
    collector = place.collector
    other_core = jnp.logical_not(collector)
    rows = tokens.shape[0]
    mid = rows // 2
    slab2 = shards.shape[1]
    slab = slab2 // 2
    pair_cols = 2 * shards.shape[2]
    cols_y = part(y, pair_cols)
    cols_other = part(1 - y, pair_cols)
    x_dev, z_dev, far_dev = (
        place.along_narrow(1),
        place.along_narrow(2),
        place.along_narrow(group),
    )
    core_dev, y_dev = place.along_wide(1), place.along_wide(2)
    wires = Wires(send_sem, recv_sem)
    exchange = wires.exchange
    gain_one, gain_two = attn_gain[...].reshape(1, -1), mlp_gain[...].reshape(1, -1)
    down_bias = down_bias_in[...].astype(F32).reshape(1, -1)

    early = [
        pltpu.make_async_copy(source, target, local_sem.at[16 + k])
        for k, (source, target) in enumerate(((tokens_in, tokens), (cotangent_in, cotangent)))
    ]
    for one in early:
        one.start()
    greet(place, group)

    halves = (slice(0, mid), slice(mid, rows))

    def x_part(mask, which):
        return x_all.at[flip(quarter, mask), halves[which]]

    x_first, z_first, on_first, core_first = (
        wires.ids(2),
        wires.ids(2),
        wires.ids(2),
        wires.ids(5),
    )

    def x_own(which):
        return wires.copy(tokens_in.at[halves[which]], x_part(0, which), x_dev, x_first + which)

    def x_in(which):
        return wires.copy(x_part(1, which), x_part(1, which), x_dev, x_first + which)

    def z_own(which):
        return wires.copy(tokens_in.at[halves[which]], x_part(0, which), z_dev, z_first + which)

    def z_in(which):
        return wires.copy(x_part(2, which), x_part(2, which), z_dev, z_first + which)

    def on_out(which):
        return wires.copy(x_part(2, which), x_part(2, which), x_dev, on_first + which)

    def on_in(which):
        return wires.copy(x_part(3, which), x_part(3, which), x_dev, on_first + which)

    def core_copy(index, mask, which=None):
        there = x_all.at[flip(quarter, mask)] if which is None else x_part(mask, which)
        source = tokens_in if mask == 0 else there
        return wires.copy(source, there, core_dev, core_first + index)

    for which in range(2):
        wires.start_if(collector, lambda which=which: x_own(which))
        wires.start_if(other_core, lambda which=which: z_own(which))
    for m in range(3):
        shards[m] = qkv_weight[m]
    shards[3] = out_weight[...]
    shards[4] = up_weight[...]
    shards[5] = down_weight[...]
    w_arrived = exchange(shards.at[:, part(1 - core, slab), :], w_half, w_half, core_dev)
    ends_own[...] = ends_row(lengths, place.half)
    ends_from = exchange(ends_own, ends_other, ends_other, core_dev)
    wires.start_if(collector, lambda: core_copy(0, 0))
    bias_all[narrow] = jnp.broadcast_to(
        up_bias_in[...].astype(F32).reshape(1, -1), bias_all.shape[1:]
    )
    bias_from = [
        exchange(
            bias_all.at[narrow],
            bias_all.at[narrow],
            bias_all.at[flip(narrow, mask)],
            place.along_narrow(mask),
        )
        for mask in range(1, 2 * group)
    ]

    for one in early:
        one.wait()

    @pl.when(collector)
    def _():
        x_all[quarter] = tokens[...]

    w_arrived.wait_recv()
    own = shards[:, part(core, slab), :]
    other = w_half[...]
    w_pair[:, :, : pair_cols // 2] = jnp.where(core == 0, own, other)
    w_pair[:, :, pair_cols // 2 :] = jnp.where(core == 0, other, own)
    for m in range(3):
        w_qkv[m, place.column, :, cols_y] = w_pair[m]
        w_mlp[m, core, part(narrow, slab), cols_y] = w_pair[3 + m]

    masks = {"x": 1, "z": 2, "f": group}
    devices = {"x": x_dev, "z": z_dev, "f": far_dev, "y": y_dev}

    def block(m, mask, columns):
        where = flip(narrow, mask)
        columns = {"own": cols_y, "other": cols_other, "both": slice(None)}[columns]
        if m < 3:
            return w_qkv.at[m, lax.div(where, 2), :, columns]
        return w_mlp.at[m - 3, core, part(where, slab), columns]

    def whole(m, columns):
        if m < 3:
            return w_qkv.at[m, :, :, columns]
        return w_mlp.at[m - 3, core, :, columns]

    held = [{0: "own"} for _ in range(6)]
    gathered = [[] for _ in range(6)]
    turned = {"own": "other", "other": "own", "both": "both"}

    def arrive(m):
        for one in gathered[m]:
            one.wait_recv()
        gathered[m] = []

    def gather(m, stage):
        arrive(m)
        order = GATHER_ORDERS[m]
        if stage == len(order):
            gathered[m] = [
                exchange(
                    w_mlp.at[m - 3, core],
                    w_mlp.at[m - 3, core],
                    w_mlp.at[m - 3, 1 - core],
                    core_dev,
                )
            ]
            return
        way = order[stage]
        device = devices[way]
        if way == "y" and stage == len(order) - 1:
            mine = whole(m, cols_y)
            gathered[m] = [exchange(mine, mine, whole(m, cols_other), device)]
            return
        more = {}
        for mask, columns in held[m].items():
            mine = block(m, mask, columns)
            if way == "y":
                incoming = block(m, mask, turned[columns])
                more[mask] = "both"
            else:
                incoming = block(m, mask ^ masks[way], columns)
                more[mask ^ masks[way]] = columns
            gathered[m].append(exchange(mine, mine, incoming, device))
        held[m].update(more)

    scale = jnp.tile(scale_column(query_scale), (query_t.shape[0], 1))

    def project(mask):
        where = flip(quarter, mask)
        span = part(where, rows)
        inputs = x_all[where].astype(F32)
        normal[where] = (inputs * norm_rows(inputs) * gain_one).astype(LOW)
        weight = w_qkv[...].reshape(-1, inputs.shape[1])
        out = product(weight, normal[where], 1, 1)
        size = out.shape[0] // 3
        heads = size // HEAD_DIM
        query_full[:, span] = out[:size]
        query_t[:, :, span] = (out[:size] * scale).astype(LOW).reshape(heads, HEAD_DIM, rows)
        key = out[size : 2 * size].astype(LOW).reshape(heads, HEAD_DIM, rows)
        value = out[2 * size :].astype(LOW).reshape(heads, HEAD_DIM, rows)
        key_t[:, :, span] = key
        value_t[:, :, span] = value
        for head in range(heads):
            key_n[head, span, :] = key[head].T
            value_n[head, span, :] = value[head].T

    stores = []

    def store(source, target):
        one = pltpu.make_async_copy(source, target, local_sem.at[len(stores)])
        one.start()
        stores.append(one)

    heads = query_t.shape[0]
    att_first = wires.ids(4 * heads)

    def att_send(head, mask):
        peer = flip(quarter, mask)
        return wires.copy(
            attended.at[head, :, part(peer, rows)],
            att_all.at[core, head, place.x],
            place.at(place.z, flip(narrow, mask)),
            att_first + mask * heads + head,
            att_first + (core * 2 + place.x) * heads + head,
        )

    def att_in(head, from_core, from_x):
        there = att_all.at[from_core, head, from_x]
        return wires.copy(there, there, core_dev, att_first + (from_core * 2 + from_x) * heads + head)

    def one_head(head, carry):
        attend_head(head, ends, query_t, key_n, value_t, attended, logsum)
        for mask in (3, 1, 2):
            att_send(head, mask).start()

        @pl.when(collector)
        def _():
            att_all[core, head, place.x] = attended[head, :, part(quarter, rows)]

        pl.when(other_core)(lambda: att_send(head, 0).start())
        return carry

    def pass_on(which):
        wait_if(collector, lambda: z_in(which))
        wires.start_if(collector, lambda: on_out(which))
        wires.start_if(collector, lambda: core_copy(2 + which, 2, which))

    gather(3, 0)
    gather(5, 0)
    gather(0, 0)
    gather(1, 0)
    gather(1, 1)
    gather(5, 1)
    pass_on(0)
    for which in range(2):
        wait_if(collector, lambda which=which: x_in(which))
    wires.start_if(collector, lambda: core_copy(1, 1))
    gather(4, 0)
    gather(2, 0)
    gather(4, 1)
    gather(3, 1)
    gather(2, 1)
    gather(1, 2)
    pass_on(1)
    gather(5, 2)
    gather(4, 2)
    gather(0, 1)
    gather(0, 2)
    for which in range(2):
        wait_if(collector, lambda which=which: on_in(which))
    wires.start_if(collector, lambda: core_copy(4, 3))
    gather(5, 3)
    gather(2, 2)
    gather(3, 2)
    ends_from.wait_recv()
    ends_out[...] = jnp.where(collector, ends_own[...], ends_other[...])
    ends = document_ends(ends_out)
    for m in range(3):
        arrive(m)
    wait_if(other_core, lambda: core_copy(0, 0))
    project(0)
    gather(4, 3)
    wait_if(other_core, lambda: core_copy(1, 1))
    project(1)
    gather(3, 3)
    for which in range(2):
        wait_if(other_core, lambda which=which: core_copy(2 + which, 2, which))
    project(2)
    wait_if(other_core, lambda: core_copy(4, 3))
    project(3)
    store(x_all, x_out)
    store(normal, normal_out)
    store(query_full, qf_out)
    store(query_t, q_out)
    store(key_t, kt_out)
    store(key_n, kn_out)
    store(value_n, vn_out)
    store(w_qkv, wq_out)
    gather(5, 4)
    lax.fori_loop(0, 2, one_head, 0)
    gather(3, 4)
    lax.fori_loop(2, heads, one_head, 0)
    gather(4, 4)
    store(logsum, lse_out)

    sums[...] = jnp.zeros_like(sums)
    sums[1:2, :] = jnp.sum(cotangent[...].astype(F32), axis=0, keepdims=True)
    for one in bias_from:
        one.wait_recv()
    for c in range(2):
        for n in range(2 * group):
            start = (c * 2 * group + n) * slab
            bias_row[0:1, start : start + slab] = bias_all[n, 0:1, c * slab : (c + 1) * slab]

    def finish_head(head, carry):
        for from_core in range(2):
            for from_x in range(2):
                local = collector & (core == from_core) & (place.x == from_x)
                wait_if(
                    jnp.logical_not(local),
                    lambda from_core=from_core, from_x=from_x: att_in(head, from_core, from_x),
                )
        return carry

    lax.fori_loop(0, heads, finish_head, 0)
    arrive(3)

    size = 2 * w_mlp.shape[2]
    grad_shape = w_mlp.shape[1:]

    def weight(m):
        return w_mlp[m].reshape(size, -1)

    wires.finish((True,))
    stores[0].wait()
    result, grad_pre, normal_two, hidden = (x_all.at[slot] for slot in range(4))
    att = att_all[...].reshape(size, rows)
    middle = grad_middle
    middle[...] = tokens[...].astype(F32) + product(att, weight(0), 0, 0)
    inverse = norm_rows(middle[...])
    normal_two[...] = (middle[...] * inverse * gain_two).astype(LOW)
    arrive(4)
    pre = product(normal_two[...], weight(1), 1, 1) + bias_row[...]
    gate = 1.0 / (1.0 + jnp.exp(-pre))
    hidden[...] = (pre * gate).astype(LOW)
    slope = gate * (1.0 + pre * (1.0 - gate))
    arrive(5)
    grad_pre[...] = (product(cotangent[...], weight(2), 1, 1) * slope).astype(LOW)
    for slot in range(3):
        store(x_all.at[1 + slot], acts_out.at[slot])
    result[...] = (middle[...] + (product(hidden[...], weight(2)) + down_bias)).astype(LOW)
    store(result, result_out)
    grad_normal = product(grad_pre[...], weight(1))
    normed = middle[...] * inverse
    sums[0:1, :] = jnp.sum(grad_normal * normed, axis=0, keepdims=True)
    scaled = grad_normal * gain_two
    inner = jnp.mean(scaled * normed, axis=1, keepdims=True)
    grad_middle[...] = cotangent[...].astype(F32) + inverse * (scaled - normed * inner)
    store(grad_middle, middle_out)
    branch = grad_middle[...].astype(LOW)
    grad_att[...] = product(weight(0), branch, 1, 1).astype(LOW).reshape(grad_att.shape)
    store(grad_att, att_out)

    def finish_send(head, carry):
        for mask in (1, 2, 3):
            att_send(head, mask).wait_send()
        pl.when(other_core)(lambda: att_send(head, 0).wait_send())
        return carry

    lax.fori_loop(0, heads, finish_send, 0)
    wires.finish()
    w_mlp[0] = product(att, branch).astype(LOW).reshape(grad_shape)
    store(w_mlp.at[0], wo_out)
    sums[2:3, :] = jnp.sum(grad_pre[...].astype(F32), axis=0, keepdims=True)
    for one in stores[1:]:
        one.wait()


def backward_head(
    head,
    ends,
    queries,
    query_full,
    keys,
    keys_t,
    values,
    grad_out,
    logsum,
    scale,
    grads_t,
    sum_keys,
    sum_values,
    sum_scale,
    halfway,
):
    sum_keys[...] = jnp.zeros_like(sum_keys)
    sum_values[...] = jnp.zeros_like(sum_values)

    def first_half(tile):
        offset, starts = tile_keys(tile)
        first, position = first_key(ends, offset)
        span = slice(offset, offset + TILE)
        query, grad, log_row = queries[head, :, span], grad_out[head, :, span], logsum[head, :, span]
        blocks, inner = [], None
        for start in starts:
            scores = product(keys[head, start : start + TILE, :], query)
            scores = allowed_scores(scores, start, offset, first, position)
            probs = jnp.exp(scores - log_row)
            grad_probs = product(values[head, start : start + TILE, :], grad)
            share = jnp.sum(probs * grad_probs, axis=0, keepdims=True)
            inner = share if inner is None else inner + share
            blocks.append((probs, grad_probs))
        return blocks, inner, query, grad

    def second_half(tile, held):
        blocks, inner, query, grad = held
        offset, starts = tile_keys(tile)
        span = slice(offset, offset + TILE)
        grad_scaled = None
        for (probs, grad_probs), start in zip(blocks, starts):
            there = slice(start, start + TILE)
            grad_scores = (probs * (grad_probs - inner)).astype(LOW)
            term = product(keys_t[head, :, there], grad_scores)
            grad_scaled = term if grad_scaled is None else grad_scaled + term
            sum_keys[:, there] += product(query, grad_scores, 1, 1)
            sum_values[:, there] += product(grad, probs.astype(LOW), 1, 1)
        grads_t[0, head, :, span] = (grad_scaled * scale).astype(LOW)
        terms = grad_scaled * query_full[part(head, HEAD_DIM), span]
        sum_scale[...] += terms[:, : TILE // 2] + terms[:, TILE // 2 :]

    count = LEN // TILE
    pipelined(range(count // 2), first_half, second_half)
    halfway()
    pipelined(range(count // 2, count), first_half, second_half)
    grads_t[1, head] = sum_keys[...].astype(LOW)
    grads_t[2, head] = sum_values[...].astype(LOW)


SCATTER_ORDERS = ("yzxf", "xyzf", "zyxf")


def backward_kernel(
    group,
    ends_in,
    query_scale,
    sums,
    grad_own,
    out_grads,
    acts,
    cotangent,
    x_in,
    normal_in,
    query_full_in,
    query_t_in,
    key_t_in,
    key_n_in,
    value_n_in,
    w_qkv_in,
    logsum_in,
    dx_last,
    mlp_out,
    qkv_out,
    sums_out,
    normal,
    query_full,
    query_t,
    key_t,
    key_n,
    value_n,
    logsum,
    grad_att,
    grads_t,
    sum_keys,
    sum_values,
    sum_scale,
    w_own,
    w_core,
    w_y,
    w_eight,
    w_four,
    w_two,
    w_last,
    dx_own,
    dx_core,
    dx_x,
    w_qkv,
    dw,
    dw_y,
    dw_z_in,
    dw_far,
    dw_last,
    all_sums,
    got_sums,
    send_sem,
    recv_sem,
    local_sem,
):
    place = Place(group)
    core, y, quarter, narrow = place.core, place.y, place.quarter, place.narrow
    collector = place.collector
    other_core = jnp.logical_not(collector)
    mid = dx_last.shape[1]
    rows = 2 * mid
    slab = qkv_out.shape[2]
    cols = qkv_out.shape[3]
    pair_cols = 2 * cols
    cols_y = part(y, pair_cols)
    cols_other = part(1 - y, pair_cols)
    x_dev, z_dev, far_dev = (
        place.along_narrow(1),
        place.along_narrow(2),
        place.along_narrow(group),
    )
    core_dev, y_dev = place.along_wide(1), place.along_wide(2)
    wires = Wires(send_sem, recv_sem)
    scale = scale_column(query_scale)
    dxs = w_core

    trade = wires.trade

    act_loads = [
        pltpu.make_async_copy(source, normal.at[slot], local_sem.at[12 + slot])
        for slot, source in enumerate((acts.at[0], acts.at[1], acts.at[2], cotangent))
    ]
    head_loads = [
        pltpu.make_async_copy(source, target, local_sem.at[16 + k])
        for k, (source, target) in enumerate(
            (
                (query_t_in, query_t),
                (key_n_in, key_n),
                (value_n_in, value_n),
                (key_t_in, key_t),
                (logsum_in, logsum),
                (query_full_in, query_full),
            )
        )
    ]
    for one in act_loads + head_loads:
        one.start()
    greet(place, group)

    heads = query_t.shape[0]
    att_first = wires.ids(4 * heads)

    def att_out(head, to_core, to_x):
        target = place.half * group + core * 2 + to_x
        return wires.copy(
            grad_own.at[to_core, head, to_x],
            grad_att.at[head, :, part(quarter, rows)],
            place.at(to_core, target),
            att_first + (to_core * 2 + to_x) * heads + head,
            att_first + quarter * heads + head,
        )

    def att_local(to_core, to_x):
        return collector & (core == to_core) & (place.x == to_x)

    def att_in(head, mask):
        peer = flip(quarter, mask)
        there = grad_att.at[head, :, part(peer, rows)]
        return wires.copy(there, there, core_dev, att_first + peer * heads + head)

    def block_at(index, row):
        low = 1 - lax.div(index, 2)
        high = lax.rem(index + 1, 2) * lax.div(index, 2) + lax.rem(index, 2) * low
        row = jnp.where(low == 1, flip(row, 1), row)
        return jnp.where(high == 1, flip(row, 2), row)

    def head_at(index):
        return block_at(jnp.int32(index), place.column)

    for index in range(heads):
        head = block_at(jnp.int32(index), place.half * 2 + core)
        for to_core in range(2):
            for to_x in range(2):
                pl.when(jnp.logical_not(att_local(to_core, to_x)))(
                    lambda head=head, to_core=to_core, to_x=to_x: att_out(
                        head, to_core, to_x
                    ).start()
                )

    def own_head(head):
        return pltpu.make_async_copy(
            grad_own.at[core, head, place.x],
            grad_att.at[head, :, part(quarter, rows)],
            local_sem.at[22 + head],
        )

    for head in range(heads):
        pl.when(collector)(lambda head=head: own_head(head).start())

    span_m = w_own.shape[1]

    def core_rows(m):
        return slice(m * span_m, (m + 1) * span_m)

    arrived = [None] * 3
    arrived[0] = [trade(lambda: (out_grads.at[1 - core], w_core.at[core_rows(0)], core_dev))]

    def load_own():
        return pltpu.make_async_copy(out_grads.at[core], w_own.at[0], local_sem.at[0])

    def load_normal():
        return pltpu.make_async_copy(normal_in, normal, local_sem.at[3])

    def load_qkv():
        return pltpu.make_async_copy(w_qkv_in, w_qkv, local_sem.at[4])

    load_own().start()

    def give_half(m, left, right, place_for):
        def half(which):
            return product(left[:, part(which, span_m)], right, 0, 0).astype(LOW)

        place_for[0:2] = half(1 - core).reshape((2,) + place_for.shape[1:])
        count = place_for.shape[1]
        arrived[m] = [
            trade(
                lambda k=k: (
                    place_for.at[k // count, k % count],
                    w_core.at[m * span_m + k * slab : m * span_m + (k + 1) * slab],
                    core_dev,
                )
            )
            for k in range(2 * count)
        ]
        w_own[m] = half(core)

    for one in act_loads:
        one.wait()
    first_given = len(wires.sent)
    give_half(1, normal.at[0], normal[1], dw)
    give_half(2, normal.at[2], normal[3], w_qkv)
    given = wires.sent[first_given:]
    del wires.sent[first_given:]
    load_normal().start()

    def given_gone():
        for _, out in given:
            out().wait_send()
        load_qkv().start()
        load_normal().wait()

    masks = {"x": 1, "z": 2, "f": group}
    devices = {"x": x_dev, "z": z_dev, "f": far_dev, "y": y_dev}
    every = tuple(o for o in range(2 * group))
    kept = [every] * 3
    landing = [None] * 3

    def block(m, mask, columns):
        return w_own.at[m, part(flip(narrow, mask), slab), columns]

    def add_to(target, source):
        target[...] = (target[...].astype(F32) + source[...].astype(F32)).astype(LOW)

    def y_rows(m, k):
        start = span_m + (m - 1) * span_m // 2 + k * slab
        return w_y.at[start : start + slab]

    def scatter(m, stage):
        for one in arrived[m]:
            one()
        if stage == 0:
            if m == 0:
                load_own().wait()
            add_rows(w_own.at[m], w_core.at[core_rows(m)], 128)
        elif SCATTER_ORDERS[m][stage - 1] == "y":
            columns = cols_y
            if stage == 1:
                add_rows(w_own.at[m, :, cols_y], w_y.at[:span_m], 128)
            else:
                for k, mask in enumerate(kept[m]):
                    add_to(block(m, mask, cols_y), y_rows(m, k))
        else:
            width = "y" in SCATTER_ORDERS[m][: stage - 1]
            for k, mask in enumerate(kept[m]):
                columns = cols_y if width else slice(None)
                add_to(block(m, mask, columns), landing[m](k))
        if stage == 4:
            total = w_own[m, part(narrow, slab), cols_y].astype(F32)
            arrived[m] = [last_step(total, mlp_out, m, w_last)]
            return
        way = SCATTER_ORDERS[m][stage]
        if way == "y":
            if stage == 0:
                arrived[m] = [
                    trade(lambda: (w_own.at[m, :, cols_other], w_y.at[:span_m], y_dev))
                ]
            else:
                arrived[m] = [
                    trade(
                        lambda k=k, mask=mask: (
                            block(m, mask, cols_other),
                            y_rows(m, k),
                            y_dev,
                        )
                    )
                    for k, mask in enumerate(kept[m])
                ]
            return
        bit = masks[way]
        width = "y" in SCATTER_ORDERS[m][:stage]
        columns = cols_y if width else slice(None)
        mine = tuple(o for o in kept[m] if not o & bit)
        buffers = {8: w_eight, 4: w_four, 2: w_two}
        buffer = buffers[len(kept[m])]

        def land(k, buffer=buffer, width=width):
            if width and buffer is w_eight:
                return buffer.at[m, k, :, : 2 * cols]
            return buffer.at[m, k]

        arrived[m] = [
            trade(lambda k=k, o=o: (block(m, o | bit, columns), land(k), devices[way]))
            for k, o in enumerate(mine)
        ]
        kept[m] = mine
        landing[m] = land

    def last_step(total, out_ref, m, buffer):
        mine = jnp.where(core == 0, total[:, :cols], total[:, cols:])
        theirs = jnp.where(core == 0, total[:, cols:], total[:, :cols])
        out_ref[m, core] = mine
        buffer[m] = theirs
        return trade(lambda: (buffer.at[m], out_ref.at[m, core], core_dev))

    def column_at(mask):
        return lax.div(flip(narrow, mask), 2)

    def dw_add(where, source):
        there = dw.at[:, where, :, cols_y]
        there[...] = (there[...].astype(F32) + source[...].astype(F32)).astype(LOW)

    def weight_grads(head):
        dw[:, head] = (
            product(
                grads_t[:, head].reshape(3 * HEAD_DIM, LEN), normal[...].reshape(LEN, -1)
            )
            .astype(LOW)
            .reshape(3, HEAD_DIM, -1)
        )

    def dw_y_copy(head, slot):
        return wires.copy(
            dw.at[:, head, :, cols_other], dw_y.at[:, head], y_dev, dw_first + slot
        )

    dw_first = wires.ids(heads)

    def dw_z_step():
        return [
            trade(
                lambda k=k, o=o: (dw.at[:, column_at(o), :, cols_y], dw_z_in.at[:, k], z_dev)
            )
            for k, o in enumerate((2, group + 2))
        ]

    def dw_far_step(came):
        came[1]()
        dw_add(column_at(group), dw_z_in.at[:, 1])
        return trade(lambda: (dw.at[:, column_at(group), :, cols_y], dw_far, far_dev))

    def dw_last_step(came, far):
        came[0]()
        dw_add(column_at(0), dw_z_in.at[:, 0])
        far()
        last = []
        for m in range(3):
            total = dw[m, place.column, :, cols_y].astype(F32) + dw_far[m].astype(F32)
            last.append(last_step(total, qkv_out, m, dw_last))
        return last

    ends = document_ends(ends_in)
    sum_scale[...] = jnp.zeros_like(sum_scale)

    steps = {}

    def at_step(step, action):
        steps.setdefault(step, []).append(action)

    came = {}

    def rows_in(slot):
        dw_y_copy(head_at(slot), slot).wait_recv()
        dw_add(head_at(slot), dw_y.at[:, head_at(slot)])

    def rows_on():
        came["dw_z"] = dw_z_step()

    at_step((0, 1), given_gone)
    at_step((0, 0), lambda: scatter(0, 0))
    at_step((1, 0), lambda: scatter(2, 0))
    at_step((1, 0), lambda: scatter(1, 0))
    at_step((2, 0), lambda: scatter(0, 1))
    at_step((3, 0), lambda: rows_in(0))
    at_step((3, 1), lambda: scatter(1, 1))
    at_step((3, 1), lambda: rows_in(1))
    at_step((3, 1), rows_on)

    def between(index, point):
        for (wanted, where), actions in steps.items():
            if where == point:

                @pl.when(index == wanted)
                def _():
                    for action in actions:
                        action()

    def one_head(index, carry):
        head = head_at(index)
        between(index, 0)
        wait_if(other_core, lambda: att_in(head, 0))
        pl.when(collector)(lambda: own_head(head).wait())
        for mask in range(1, group):
            att_in(head, mask).wait_recv()
        backward_head(
            head,
            ends,
            query_t,
            query_full,
            key_n,
            key_t,
            value_n,
            grad_att,
            logsum,
            scale,
            grads_t,
            sum_keys,
            sum_values,
            sum_scale,
            lambda: between(index, 1),
        )

        @pl.when(index < heads - 1)
        def _():
            weight_grads(head)
            dw_y_copy(head, index).start()

        return carry

    for one in head_loads:
        one.wait()
    lax.fori_loop(0, heads, one_head, 0)

    size = 3 * heads * HEAD_DIM
    load_qkv().wait()

    def kept_rows(mask):
        if mask == 0:
            return dx_own
        start = (group + mask - 1) * mid
        return dxs.at[start : start + mid]

    def grad_inputs(mask):
        first = flip(quarter, mask) * 2
        weight = w_qkv[...].reshape(size, -1)

        def half_rows(which):
            span = part(first + which, mid)
            return product(grads_t[:, :, :, span].reshape(size, mid), weight, 0, 0).astype(LOW)

        there = slice(mask * mid, (mask + 1) * mid)
        dxs[there] = half_rows(1 - core)
        out = trade(lambda: (dxs.at[there], dx_core.at[mask], core_dev))
        kept_rows(mask)[...] = half_rows(core)
        return out

    def add_core(mask, came):
        came()
        add_rows(kept_rows(mask), dx_core.at[mask], 128)

    from_core = {}
    last_first = wires.ids(2)

    def last_out():
        return wires.copy(
            kept_rows(2),
            dx_last.at[core],
            place.at(place.z, flip(narrow, 2)),
            last_first,
            last_first + core,
        )

    def last_core():
        return wires.copy(kept_rows(0), dx_last.at[core], core_dev, last_first + 1, last_first + core)

    def last_in(which):
        return wires.copy(dx_last.at[which], dx_last.at[which], core_dev, last_first + which)

    sum_devices = [core_dev, place.along_wide(3)] + [
        (flip(place.wide, 1), flip(narrow, mask)) for mask in (1, 2, group)
    ]

    def sum_step(stage):
        return trade(lambda: (all_sums.at[stage], got_sums.at[stage], sum_devices[stage]))

    def sum_add(stage, came):
        came()
        all_sums[stage + 1] = all_sums[stage] + got_sums[stage]

    scatter(0, 2)
    from_core[3] = grad_inputs(3)
    add_core(3, from_core[3])
    from_x3 = trade(lambda: (kept_rows(3), dx_x.at[1], x_dev))
    scatter(0, 3)
    from_core[1] = grad_inputs(1)
    from_core[0] = grad_inputs(0)
    from_core[2] = grad_inputs(2)
    add_core(1, from_core[1])
    from_x1 = trade(lambda: (kept_rows(1), dx_x.at[0], x_dev))
    scatter(1, 2)
    add_core(0, from_core[0])
    rows_in(2)
    dw_f = dw_far_step(came["dw_z"])
    add_core(2, from_core[2])
    raw = [
        pltpu.make_async_copy(
            x_in.at[flip(quarter, mask), part(core, mid)], dx_core.at[mask], local_sem.at[6 + mask]
        )
        for mask in range(group)
    ]
    for one in raw:
        one.start()
    for one in raw:
        one.wait()
    all_sums[0] = sums[...]
    all_sums[0, 3:4, :HEAD_DIM] = jnp.sum(sum_scale[...].T, axis=0, keepdims=True)
    for mask in range(group):

        def gain_rows(span, mask=mask):
            inputs = dx_core[mask, span, :].astype(F32)
            normed = inputs * norm_rows(inputs)
            terms = kept_rows(mask)[span, :].astype(F32) * normed
            all_sums[0, 4:5, :] += jnp.sum(terms, axis=0, keepdims=True)

        chunks(mid, 128, gain_rows)

    sums_now = sum_step(0)
    from_x3()
    add_rows(kept_rows(2), dx_x.at[1], 128)
    last_out().start()
    wires.sent.append((None, last_out))
    scatter(2, 1)
    weight_grads(head_at(heads - 1))
    dw_y_copy(head_at(heads - 1), heads - 1).start()
    scatter(1, 3)
    sum_add(0, sums_now)
    sums_now = sum_step(1)
    scatter(0, 4)
    scatter(2, 2)
    rows_in(3)
    scatter(2, 3)
    sum_add(1, sums_now)
    sums_now = sum_step(2)
    scatter(1, 4)
    from_x1()
    add_rows(kept_rows(0), dx_x.at[0], 128)
    wires.start_if(other_core, last_core)

    @pl.when(collector)
    def _():
        dx_last[core] = dx_own[...]

    sum_add(2, sums_now)
    sums_now = sum_step(3)
    last = dw_last_step(came["dw_z"], dw_f)
    sum_add(3, sums_now)
    sums_now = sum_step(4)
    for which in range(2):
        wait_if(
            jnp.logical_not(collector & (core == which)), lambda which=which: last_in(which)
        )

    scatter(2, 4)
    sum_add(4, sums_now)
    sums_out[...] = all_sums[5]

    for one in last + arrived[0] + arrived[1] + arrived[2]:
        one()
    for slot in range(heads):
        dw_y_copy(head_at(slot), slot).wait_send()

    def finish_send(head, carry):
        for to_core in range(2):
            for to_x in range(2):
                pl.when(jnp.logical_not(att_local(to_core, to_x)))(
                    lambda to_core=to_core, to_x=to_x: att_out(head, to_core, to_x).wait_send()
                )
        return carry

    lax.fori_loop(0, heads, finish_send, 0)
    wires.finish()


def final_kernel(
    tokens, gain, grad_rows, grad_middle, result, mlp_raw, qkv_raw, sums, query_scale,
    tokens_out, result_out, qkv_out, out_out, up_out, down_out,
    up_bias_out, bias_out, attn_out, mlp_out, scale_out,
):
    inputs = tokens[...].astype(F32)
    inverse = norm_rows(inputs)
    normed = inputs * inverse
    scaled = grad_rows[...].astype(F32) * gain[...].reshape(1, -1)
    inner = jnp.mean(scaled * normed, axis=1, keepdims=True)
    tokens_out[...] = grad_middle[...] + inverse * (scaled - normed * inner)
    result_out[...] = result[...]

    @pl.when(pl.program_id(0) == 0)
    def _():
        qkv_out[...] = qkv_raw[...]
        out_out[...] = mlp_raw[0]
        up_out[...] = mlp_raw[1]
        down_out[...] = mlp_raw[2]
        count, slab = sums.shape[1], up_bias_out.shape[0] // 2
        shift = lax.rem(count - slab * lax.axis_index("narrow"), count)
        here = pltpu.roll(sums[...], shift, 1)[2:3]
        both = [here[:, :slab], here[:, count // 2 : count // 2 + slab]]
        up_bias_out[...] = jnp.concatenate(both, axis=1)[0, :]
        mlp_out[...] = sums[0, :]
        bias_out[...] = sums[1, :]
        attn_out[...] = sums[4, :]
        slope = 1.0 / (1.0 + jnp.exp(-query_scale[...].reshape(1, -1)))
        terms = sums[3:4, :HEAD_DIM] * (LOG_TWO_E / math.sqrt(HEAD_DIM)) * slope
        scale_out[...] = terms[0, :]


def struct(shape, dtype):
    return jax.ShapeDtypeStruct(shape, dtype)


def kernel_call(kernel, outputs, in_specs, out_spaces, scratch, collective_id=None):
    extra = {} if collective_id is None else {"collective_id": collective_id, "has_side_effects": True}
    return pl.pallas_call(
        kernel,
        out_shape=tuple(outputs),
        in_specs=[pl.BlockSpec(memory_space=space) for space in in_specs],
        out_specs=tuple(pl.BlockSpec(memory_space=space) for space in out_spaces),
        scratch_shapes=scratch,
        compiler_params=pltpu.CompilerParams(vmem_limit_bytes=VMEM_LIMIT, **extra),
    )


def fused_device(
    group,
    tokens,
    lengths,
    qkv_weight,
    out_weight,
    up_weight,
    up_bias,
    down_weight,
    down_bias,
    attn_gain,
    mlp_gain,
    query_scale,
    cotangent,
):
    rows, dim = tokens.shape
    slab2, cols = out_weight.shape
    slab = slab2 // 2
    halves = lengths.shape[0]
    heads = halves * slab2 // HEAD_DIM
    local = heads * HEAD_DIM
    narrow_count = group * halves
    hidden = slab2 * narrow_count
    vmem, smem, anywhere = pltpu.VMEM, pltpu.SMEM, pl.ANY

    att_shape = (2, heads, 2, HEAD_DIM, rows)
    wq_shape = (3, heads, slab, dim)
    wm_shape = (3, 2, narrow_count * slab, dim)
    dma = pltpu.SemaphoreType.DMA

    forward_outputs = [
        struct((group, rows, dim), LOW),
        struct((group, rows, dim), LOW),
        struct((local, LEN), F32),
        struct((heads, HEAD_DIM, LEN), LOW),
        struct((heads, HEAD_DIM, LEN), LOW),
        struct((heads, LEN, HEAD_DIM), LOW),
        struct((heads, LEN, HEAD_DIM), LOW),
        struct(wq_shape, LOW),
        struct((heads, 1, LEN), F32),
        struct((rows, dim), LOW),
        struct((rows, dim), F32),
        struct(att_shape, LOW),
        struct(wm_shape[1:], LOW),
        struct((3, rows, dim), LOW),
        struct((8, dim), F32),
        struct((8, 128), F32),
    ]
    (
        x_all,
        normal,
        query_full,
        query_t,
        key_t,
        key_n,
        value_n,
        w_qkv,
        logsum,
        result,
        grad_middle,
        grad_att,
        out_grads,
        acts,
        sums,
        ends,
    ) = kernel_call(
        functools.partial(forward_kernel, group),
        forward_outputs,
        [smem, anywhere] + [vmem] * 9 + [anywhere],
        [anywhere] * (len(forward_outputs) - 2) + [vmem] * 2,
        [
            vmem((rows, dim), LOW),
            vmem((rows, dim), LOW),
            vmem((group, rows, dim), LOW),
            vmem((group, rows, dim), LOW),
            vmem((6, slab2, cols), LOW),
            vmem(wq_shape, LOW),
            vmem(wm_shape, LOW),
            vmem((6, slab, 2 * cols), LOW),
            vmem((6, slab, cols), LOW),
            vmem((narrow_count, 8, slab2), F32),
            vmem((1, hidden), F32),
            vmem((8, 128), F32),
            vmem((8, 128), F32),
            vmem((local, LEN), F32),
            vmem((heads, HEAD_DIM, LEN), LOW),
            vmem((heads, HEAD_DIM, LEN), LOW),
            vmem((heads, HEAD_DIM, LEN), LOW),
            vmem((heads, LEN, HEAD_DIM), LOW),
            vmem((heads, LEN, HEAD_DIM), LOW),
            vmem((heads, 1, LEN), F32),
            vmem((heads, HEAD_DIM, LEN), LOW),
            vmem(att_shape, LOW),
            vmem(att_shape, LOW),
            vmem((rows, dim), F32),
            dma((110,)),
            dma((110,)),
            dma((18,)),
        ],
        collective_id=0,
    )(
        lengths,
        tokens,
        jnp.swapaxes(qkv_weight, 1, 2),
        out_weight,
        up_weight.T,
        up_bias,
        down_weight,
        down_bias,
        attn_gain,
        mlp_gain,
        query_scale,
        cotangent,
    )

    last_shape = (3, 2, slab, cols)
    grad_rows, mlp_grads, qkv_grads, totals = kernel_call(
        functools.partial(backward_kernel, group),
        [
            struct((2, rows // 2, dim), LOW),
            struct(last_shape, F32),
            struct(last_shape, F32),
            struct((8, dim), F32),
        ],
        [vmem] * 3 + [anywhere] * 13,
        [vmem] * 4,
        [
            vmem((group, rows, dim), LOW),
            vmem((local, LEN), F32),
            vmem((heads, HEAD_DIM, LEN), LOW),
            vmem((heads, HEAD_DIM, LEN), LOW),
            vmem((heads, LEN, HEAD_DIM), LOW),
            vmem((heads, LEN, HEAD_DIM), LOW),
            vmem((heads, 1, LEN), F32),
            vmem((heads, HEAD_DIM, LEN), LOW),
            vmem((3, heads, HEAD_DIM, LEN), LOW),
            vmem((HEAD_DIM, LEN), F32),
            vmem((HEAD_DIM, LEN), F32),
            vmem((HEAD_DIM, TILE // 2), F32),
            vmem((3, narrow_count * slab, dim), LOW),
            vmem((3 * narrow_count * slab, dim), LOW),
            vmem((2 * narrow_count * slab, 2 * cols), LOW),
            vmem((3, 4, slab, dim), LOW),
            vmem((3, 2, slab, 2 * cols), LOW),
            vmem((3, 1, slab, 2 * cols), LOW),
            vmem((3, slab, cols), F32),
            vmem((rows // 2, dim), LOW),
            vmem((group, rows // 2, dim), LOW),
            vmem((2, rows // 2, dim), LOW),
            vmem(wq_shape, LOW),
            vmem(wq_shape, LOW),
            vmem((3, heads, slab, 2 * cols), LOW),
            vmem((3, 2, slab, 2 * cols), LOW),
            vmem((3, slab, 2 * cols), LOW),
            vmem((3, slab, cols), F32),
            vmem((6, 8, dim), F32),
            vmem((5, 8, dim), F32),
            dma((100,)),
            dma((100,)),
            dma((26,)),
        ],
        collective_id=1,
    )(
        ends,
        query_scale,
        sums,
        grad_att,
        out_grads,
        acts,
        cotangent,
        x_all,
        normal,
        query_full,
        query_t,
        key_t,
        key_n,
        value_n,
        w_qkv,
        logsum,
    )


    def block(*shape):
        return pl.BlockSpec(shape, lambda step: (0,) * len(shape))

    row_block = pl.BlockSpec((rows // 2, dim), lambda step: (step, 0))
    outputs = [
        (row_block, struct((rows, dim), F32)),
        (row_block, struct((rows, dim), LOW)),
        (block(3, slab2, cols), struct((3, slab2, cols), F32)),
    ]
    outputs += [(block(slab2, cols), struct((slab2, cols), F32))] * 3
    outputs += [
        (block(size), struct((size,), F32)) for size in (slab2, dim, dim, dim, HEAD_DIM)
    ]
    (
        grad_tokens,
        result,
        grad_qkv,
        grad_out,
        grad_up,
        grad_down,
        grad_up_bias,
        grad_down_bias,
        grad_attn_gain,
        grad_mlp_gain,
        grad_scale,
    ) = pl.pallas_call(
        final_kernel,
        grid=(2,),
        out_shape=tuple(shape for _, shape in outputs),
        in_specs=[
            row_block,
            block(dim),
            row_block,
            row_block,
            row_block,
            block(3, slab2, cols),
            block(3, slab2, cols),
            block(8, dim),
            block(HEAD_DIM),
        ],
        out_specs=tuple(spec for spec, _ in outputs),
    )(
        tokens,
        attn_gain,
        grad_rows.reshape(rows, dim),
        grad_middle,
        result,
        mlp_grads.reshape(3, slab2, cols),
        qkv_grads.reshape(3, slab2, cols),
        totals,
        query_scale,
    )
    return (
        result,
        grad_tokens,
        jnp.swapaxes(grad_qkv, 1, 2),
        grad_out,
        grad_up.T,
        grad_up_bias,
        grad_down,
        grad_down_bias,
        grad_attn_gain,
        grad_mlp_gain,
        grad_scale,
    )


def solution(mesh):
    wide_count, narrow_count = mesh.shape["wide"], mesh.shape["narrow"]

    def per_device(*args):
        tokens, lengths, out_weight = args[0], args[1], args[3]
        group = LEN // tokens.shape[0]
        fits = (
            wide_count == 4
            and group == 4
            and narrow_count == group * lengths.shape[0] == 8
            and out_weight.shape[0] == 2 * HEAD_DIM
            and 2 * out_weight.shape[1] % 128 == 0
        )
        if fits:
            return fused_device(group, *args)
        return general_device(*args)

    return jax.shard_map(
        per_device,
        mesh=mesh,
        in_specs=(
            P(("wide", "narrow"), None),
            P("wide", None),
            P(None, "wide", "narrow"),
            P("narrow", "wide"),
            P("wide", "narrow"),
            P("narrow"),
            P("narrow", "wide"),
            P(),
            P(),
            P(),
            P(),
            P(("wide", "narrow"), None),
        ),
        out_specs=(
            P(("wide", "narrow"), None),
            P(("wide", "narrow"), None),
            P(None, "wide", "narrow"),
            P("narrow", "wide"),
            P("wide", "narrow"),
            P("narrow"),
            P("narrow", "wide"),
            P(),
            P(),
            P(),
            P(),
        ),
        check_vma=False,
    )
```

```python
import functools
import math

import jax
import jax.numpy as jnp
from jax import lax
from jax.experimental import pallas as pl
from jax.experimental.pallas import tpu as pltpu
from jax.sharding import PartitionSpec as P

HEAD_DIM = 80
LEN = 2048
WINDOW = 1024
BLOCK = 512
NDOC = 4
TILE = 256

LOG_TWO_E = 1.4426950408889634
EPSILON = 1e-06
NEG_FILL = -1e30

F32 = jnp.float32
LOW = jnp.bfloat16
MESH = pl.DeviceIdType.MESH
VMEM_LIMIT = 63 * 2**20


def group_rows(values):
    return lax.all_gather(values, "narrow", axis=0, tiled=True)


def group_parts(values):
    return lax.psum_scatter(values, "narrow", scatter_dimension=0, tiled=True)


def contract_last(left, right):
    return lax.dot_general(
        left, right, (((1,), (1,)), ((), ())), preferred_element_type=jnp.float32
    )


def contract_first(left, right):
    return lax.dot_general(
        left, right, (((0,), (0,)), ((), ())), preferred_element_type=jnp.float32
    )


def norm_share(inputs, norm_gain):
    inverse = lax.rsqrt(jnp.mean(inputs * inputs, axis=1) + EPSILON)
    normed = inputs * inverse[:, None]
    return (inverse, normed, (normed * norm_gain).astype(jnp.bfloat16))


def norm_back(grad_normal, norm_gain, inverse, normed):
    scaled = grad_normal * norm_gain
    inner_dots = jnp.mean(scaled * normed, axis=1)
    grad_inputs = inverse[:, None] * (scaled - normed * inner_dots[:, None])
    return (grad_inputs, jnp.sum(grad_normal * normed, axis=0))


def segment_ids(lengths_row):
    positions = jnp.arange(LEN, dtype=jnp.int32)
    ends = jnp.cumsum(lengths_row)
    return jnp.sum((positions[:, None] >= ends[None, :]).astype(jnp.int32), axis=1)


def block_mask(segments, padded_seg, offset):
    query_pos = offset + jnp.arange(BLOCK, dtype=jnp.int32)
    key_pos = offset - WINDOW + jnp.arange(WINDOW + BLOCK, dtype=jnp.int32)
    query_seg = segments[offset : offset + BLOCK]
    key_seg = padded_seg[offset : offset + WINDOW + BLOCK]
    spacing = query_pos[:, None] - key_pos[None, :]
    same_doc = query_seg[:, None] == key_seg[None, :]
    inside = (spacing >= 0) & (spacing < WINDOW)
    real_doc = (query_seg[:, None] < NDOC) | (spacing == 0)
    return same_doc & inside & real_doc


def padded_inputs(keys_in, values_in, segments):
    pad_rows = jnp.zeros((WINDOW,) + keys_in.shape[1:], keys_in.dtype)
    keys_pad = jnp.concatenate([pad_rows, keys_in], axis=0)
    values_pad = jnp.concatenate([pad_rows, values_in], axis=0)
    padded_seg = jnp.concatenate([jnp.full((WINDOW,), -2, jnp.int32), segments])
    return (keys_pad, values_pad, padded_seg)


def attend_forward(queries, keys_in, values_in, segments):
    keys_pad, values_pad, padded_seg = padded_inputs(keys_in, values_in, segments)
    outputs = []
    logsums = []
    for block_index in range(LEN // BLOCK):
        offset = block_index * BLOCK
        query_block = queries[offset : offset + BLOCK]
        key_block = keys_pad[offset : offset + WINDOW + BLOCK]
        value_block = values_pad[offset : offset + WINDOW + BLOCK]
        allowed = block_mask(segments, padded_seg, offset)
        scores = jnp.einsum(
            "ihd,jhd->hij", query_block, key_block, preferred_element_type=jnp.float32
        )
        masked = jnp.where(allowed[None], scores, NEG_FILL)
        maxima = jnp.max(masked, axis=2)
        exponent = jnp.exp(masked - maxima[:, :, None])
        totals = jnp.sum(exponent, axis=2)
        probs_low = (exponent / totals[:, :, None]).astype(jnp.bfloat16)
        block_out = jnp.einsum(
            "hij,jhd->ihd", probs_low, value_block, preferred_element_type=jnp.float32
        )
        outputs.append(block_out.astype(jnp.bfloat16))
        logsums.append(maxima + jnp.log(totals))
    return (jnp.concatenate(outputs, axis=0), jnp.concatenate(logsums, axis=1))


def attend_backward(queries, keys_in, values_in, segments, logsum, grad_out):
    keys_pad, values_pad, padded_seg = padded_inputs(keys_in, values_in, segments)
    grad_keys = jnp.zeros(keys_pad.shape, jnp.float32)
    grad_values = jnp.zeros(values_pad.shape, jnp.float32)
    grad_queries = []
    for block_index in range(LEN // BLOCK):
        offset = block_index * BLOCK
        query_block = queries[offset : offset + BLOCK]
        key_block = keys_pad[offset : offset + WINDOW + BLOCK]
        value_block = values_pad[offset : offset + WINDOW + BLOCK]
        grad_block = grad_out[offset : offset + BLOCK]
        allowed = block_mask(segments, padded_seg, offset)
        scores = jnp.einsum(
            "ihd,jhd->hij", query_block, key_block, preferred_element_type=jnp.float32
        )
        masked = jnp.where(allowed[None], scores, NEG_FILL)
        soft_probs = jnp.exp(masked - logsum[:, offset : offset + BLOCK, None])
        probs_low = soft_probs.astype(jnp.bfloat16)
        grad_probs = jnp.einsum(
            "ihd,jhd->hij", grad_block, value_block, preferred_element_type=jnp.float32
        )
        inner_sums = jnp.sum(soft_probs * grad_probs, axis=2)
        grad_scores = (soft_probs * (grad_probs - inner_sums[:, :, None])).astype(jnp.bfloat16)
        grad_queries.append(
            jnp.einsum("hij,jhd->ihd", grad_scores, key_block, preferred_element_type=jnp.float32)
        )
        key_terms = jnp.einsum(
            "hij,ihd->jhd", grad_scores, query_block, preferred_element_type=jnp.float32
        )
        value_terms = jnp.einsum(
            "hij,ihd->jhd", probs_low, grad_block, preferred_element_type=jnp.float32
        )
        grad_keys = grad_keys.at[offset : offset + WINDOW + BLOCK].add(key_terms)
        grad_values = grad_values.at[offset : offset + WINDOW + BLOCK].add(value_terms)
    return (jnp.concatenate(grad_queries, axis=0), grad_keys[WINDOW:], grad_values[WINDOW:])


def silu_slope(hidden_pre):
    sigmoid_pre = jax.nn.sigmoid(hidden_pre)
    return sigmoid_pre * (1.0 + hidden_pre * (1.0 - sigmoid_pre))


def general_device(
    tokens,
    lengths,
    qkv_weight,
    out_weight,
    up_weight,
    up_bias,
    down_weight,
    down_bias,
    attn_gain,
    mlp_gain,
    query_scale,
    cotangent,
):
    head_count = qkv_weight.shape[2] // HEAD_DIM
    seq_count = lengths.shape[0]
    row_count = seq_count * LEN

    def by_sequence(values):
        return values.reshape((seq_count, LEN) + values.shape[1:])

    qkv_full, out_full, up_full, down_full = (
        lax.all_gather(qkv_weight, "wide", axis=1, tiled=True),
        lax.all_gather(out_weight, "wide", axis=1, tiled=True),
        lax.all_gather(up_weight, "wide", axis=0, tiled=True),
        lax.all_gather(down_weight, "wide", axis=1, tiled=True),
    )
    segments = jax.vmap(segment_ids)(lengths)
    inputs = tokens.astype(jnp.float32)
    inverse_one, normed_one, normal_one = norm_share(inputs, attn_gain)
    rows_one = group_rows(normal_one)
    projected = jnp.einsum("td,cdn->ctn", rows_one, qkv_full, preferred_element_type=jnp.float32)
    scale_dim = LOG_TWO_E / math.sqrt(HEAD_DIM) * jax.nn.softplus(query_scale)
    query_heads = projected[0].reshape(row_count, head_count, HEAD_DIM)
    query_low = (query_heads * scale_dim).astype(jnp.bfloat16)
    key_low = projected[1].astype(jnp.bfloat16).reshape(row_count, head_count, HEAD_DIM)
    value_low = projected[2].astype(jnp.bfloat16).reshape(row_count, head_count, HEAD_DIM)
    attended, logsum = jax.vmap(attend_forward)(
        by_sequence(query_low), by_sequence(key_low), by_sequence(value_low), segments
    )
    attended_rows = attended.reshape(row_count, head_count * HEAD_DIM)
    middle = inputs + group_parts(
        jnp.dot(attended_rows, out_full, preferred_element_type=jnp.float32)
    )
    inverse_two, normed_two, normal_two = norm_share(middle, mlp_gain)
    grad_down_bias = jnp.sum(cotangent.astype(jnp.float32), axis=0)
    rows_two = group_rows(normal_two)
    hidden_pre = jnp.dot(rows_two, up_full, preferred_element_type=jnp.float32) + up_bias
    hidden_low = jax.nn.silu(hidden_pre).astype(jnp.bfloat16)
    branch_two = (
        group_parts(jnp.dot(hidden_low, down_full, preferred_element_type=jnp.float32)) + down_bias
    )
    result = middle + branch_two
    grad_rows = group_rows(cotangent)
    grad_hidden = contract_last(grad_rows, down_full)
    grad_pre = (grad_hidden * silu_slope(hidden_pre)).astype(jnp.bfloat16)
    grad_up = contract_first(rows_two, grad_pre)
    grad_down = contract_first(hidden_low, grad_rows)
    grad_up_bias = jnp.sum(grad_pre.astype(jnp.float32), axis=0)
    grad_normal_two = group_parts(contract_last(grad_pre, up_full))
    grad_middle_norm, grad_mlp_gain = norm_back(grad_normal_two, mlp_gain, inverse_two, normed_two)
    grad_middle = cotangent.astype(jnp.float32) + grad_middle_norm
    grad_branch = group_rows(grad_middle.astype(jnp.bfloat16))
    grad_attended = contract_last(grad_branch, out_full).astype(jnp.bfloat16)
    grad_out = contract_first(attended_rows, grad_branch)
    grad_scaled, grad_key, grad_value = jax.vmap(attend_backward)(
        by_sequence(query_low),
        by_sequence(key_low),
        by_sequence(value_low),
        segments,
        logsum,
        by_sequence(grad_attended.reshape(row_count, head_count, HEAD_DIM)),
    )
    grad_scaled = grad_scaled.reshape(row_count, head_count, HEAD_DIM)
    grad_scale_part = (
        jnp.sum(grad_scaled * query_heads, axis=(0, 1))
        * (LOG_TWO_E / math.sqrt(HEAD_DIM))
        * jax.nn.sigmoid(query_scale)
    )
    grad_projected = jnp.stack(
        [
            (grad_scaled * scale_dim).reshape(row_count, head_count * HEAD_DIM),
            grad_key.reshape(row_count, head_count * HEAD_DIM),
            grad_value.reshape(row_count, head_count * HEAD_DIM),
        ]
    ).astype(jnp.bfloat16)
    grad_qkv = jnp.einsum(
        "td,ctn->cdn", rows_one, grad_projected, preferred_element_type=jnp.float32
    )
    grad_normal_one = group_parts(
        jnp.einsum("ctn,cdn->td", grad_projected, qkv_full, preferred_element_type=jnp.float32)
    )
    grad_input_norm, grad_attn_gain = norm_back(grad_normal_one, attn_gain, inverse_one, normed_one)
    grad_tokens = grad_middle + grad_input_norm
    grad_qkv, grad_out, grad_up, grad_down = (
        lax.psum_scatter(grad_qkv, "wide", scatter_dimension=1, tiled=True),
        lax.psum_scatter(grad_out, "wide", scatter_dimension=1, tiled=True),
        lax.psum_scatter(grad_up, "wide", scatter_dimension=0, tiled=True),
        lax.psum_scatter(grad_down, "wide", scatter_dimension=1, tiled=True),
    )
    grad_attn_gain, grad_mlp_gain, grad_down_bias, grad_scale = lax.psum(
        (grad_attn_gain, grad_mlp_gain, grad_down_bias, grad_scale_part), ("wide", "narrow")
    )
    grad_up_bias = lax.psum(grad_up_bias, "wide")
    return (
        result.astype(jnp.bfloat16),
        grad_tokens,
        grad_qkv,
        grad_out,
        grad_up,
        grad_up_bias,
        grad_down,
        grad_down_bias,
        grad_attn_gain,
        grad_mlp_gain,
        grad_scale,
    )


def product(left, right, left_dim=1, right_dim=0):
    return lax.dot_general(
        left, right, (((left_dim,), (right_dim,)), ((), ())), preferred_element_type=F32
    )


def flip(value, mask):
    bit = 1
    while bit <= mask:
        if mask & bit:
            value = value + bit * (1 - 2 * lax.rem(lax.div(value, bit), 2))
        bit *= 2
    return value


def part(start, size):
    return pl.ds(pl.multiple_of(start * size, size), size)


def chunks(total, size, body):
    def step(index, carry):
        body(part(index, size))
        return carry

    lax.fori_loop(0, total // size, step, 0)


def add_rows(target, source, size):
    def body(span):
        target[span, :] = (target[span, :].astype(F32) + source[span, :].astype(F32)).astype(LOW)

    chunks(source.shape[0], size, body)


class Place:
    def __init__(self, group):
        self.wide = lax.axis_index("wide")
        self.narrow = lax.axis_index("narrow")
        self.core = lax.rem(self.wide, 2)
        self.y = lax.div(self.wide, 2)
        self.quarter = lax.rem(self.narrow, group)
        self.half = lax.div(self.narrow, group)
        self.x = lax.rem(self.narrow, 2)
        self.z = lax.div(self.quarter, 2)
        self.column = lax.div(self.narrow, 2)
        self.collector = self.core == self.z

    def along_wide(self, mask):
        return (flip(self.wide, mask), self.narrow)

    def along_narrow(self, mask):
        return (self.wide, flip(self.narrow, mask))

    def at(self, core, narrow):
        return (self.y * 2 + core, narrow)


def greet(place, group):
    barrier = pltpu.get_barrier_semaphore()
    peers = [place.along_narrow(m) for m in range(1, 2 * group)]
    peers += [place.along_wide(m) for m in (1, 2, 3)]
    peers += [(flip(place.wide, 1), flip(place.narrow, m)) for m in range(1, group + 1)]
    for peer in peers:
        pl.semaphore_signal(barrier, inc=1, device_id=peer, device_id_type=MESH)
    pl.semaphore_wait(barrier, len(peers))


class Wires:
    def __init__(self, send_sem, recv_sem):
        self.send_sem, self.recv_sem = send_sem, recv_sem
        self.next_id = 0
        self.sent = []

    def ids(self, count):
        first = self.next_id
        self.next_id += count
        assert self.next_id <= self.send_sem.shape[0]
        return first

    def copy(self, source, target, device, index, arrival=None):
        return pltpu.make_async_remote_copy(
            src_ref=source,
            dst_ref=target,
            send_sem=self.send_sem.at[index],
            recv_sem=self.recv_sem.at[index if arrival is None else arrival],
            device_id=device,
            device_id_type=MESH,
        )

    def exchange(self, source, target, incoming, device):
        index = self.ids(1)
        out = self.copy(source, target, device, index)
        out.start()
        self.sent.append((None, lambda: out))
        return self.copy(incoming, incoming, device, index)

    def trade(self, make):
        index = self.ids(1)

        def out():
            source, target, device = make()
            return self.copy(source, target, device, index)

        out().start()
        self.sent.append((None, out))

        def arrive():
            _, target, device = make()
            self.copy(target, target, device, index).wait_recv()

        return arrive

    def start_if(self, condition, make):
        pl.when(condition)(lambda: make().start())
        self.sent.append((condition, make))

    def finish(self, conditional=(True, False)):
        for condition, make in self.sent:
            if (condition is not None) not in conditional:
                continue
            if condition is None:
                make().wait_send()
            else:
                pl.when(condition)(lambda make=make: make().wait_send())
        self.sent = [one for one in self.sent if (one[0] is not None) not in conditional]


def wait_if(condition, make):
    pl.when(condition)(lambda: make().wait_recv())


def ends_row(lengths, row):
    lane = lax.broadcasted_iota(jnp.int32, (8, 128), 1)
    result, total = jnp.zeros((8, 128), jnp.int32), 0
    for index in range(NDOC):
        total = total + lengths[row, index]
        result = jnp.where(lane == index, total, result)
    return result.astype(F32)


def document_ends(row):
    return [
        jnp.broadcast_to(row[0:1, k : k + 1], (1, TILE)).astype(jnp.int32) for k in range(NDOC)
    ]


def first_key(ends, offset):
    position = offset + lax.broadcasted_iota(jnp.int32, (1, TILE), 1)
    start = jnp.zeros_like(position)
    for end in ends:
        start = jnp.where(position >= end, end, start)
    start = jnp.maximum(start, position - (WINDOW - 1))
    return jnp.where(position >= ends[-1], position, start), position


def allowed_scores(scores, key_start, offset, first, position):
    key = key_start + lax.broadcasted_iota(jnp.int32, scores.shape, 0)
    allowed = key >= first
    if key_start + scores.shape[0] > offset:
        allowed = allowed & (key <= position)
    return jnp.where(allowed, scores, NEG_FILL)


def tile_keys(tile):
    offset = tile * TILE
    return offset, range(max(0, offset - WINDOW), offset + TILE, TILE)


def pipelined(tiles, first_half, second_half):
    waiting = None
    for tile in tiles:
        current = (tile, first_half(tile))
        if waiting is not None:
            second_half(*waiting)
        waiting = current
    second_half(*waiting)


def attend_head(head, ends, queries, keys, values_t, attended, logsum):
    def first_half(tile):
        offset, starts = tile_keys(tile)
        first, position = first_key(ends, offset)
        query = queries[head, :, offset : offset + TILE]
        blocks, maxima = [], None
        for start in starts:
            scores = product(keys[head, start : start + TILE, :], query)
            scores = allowed_scores(scores, start, offset, first, position)
            top = jnp.max(scores, axis=0, keepdims=True)
            maxima = top if maxima is None else jnp.maximum(maxima, top)
            blocks.append(scores)
        return blocks, maxima

    def second_half(tile, held):
        blocks, maxima = held
        offset, starts = tile_keys(tile)
        total, output = None, None
        for scores, start in zip(blocks, starts):
            exponent = jnp.exp(scores - maxima)
            share = jnp.sum(exponent, axis=0, keepdims=True)
            term = product(values_t[head, :, start : start + TILE], exponent.astype(LOW))
            total, output = (
                (share, term) if total is None else (total + share, output + term)
            )
        attended[head, :, offset : offset + TILE] = (output * (1.0 / total)).astype(LOW)
        logsum[head, :, offset : offset + TILE] = maxima + jnp.log(total)

    pipelined(range(LEN // TILE), first_half, second_half)


def norm_rows(inputs):
    return lax.rsqrt(jnp.mean(inputs * inputs, axis=1, keepdims=True) + EPSILON)


def scale_column(query_scale):
    values = query_scale[...].reshape(1, -1)
    softplus = jnp.maximum(values, 0.0) + jnp.log(1.0 + jnp.exp(-jnp.abs(values)))
    row = LOG_TWO_E / math.sqrt(HEAD_DIM) * softplus
    return jnp.broadcast_to(row, (128, HEAD_DIM)).T[:, :1]


GATHER_ORDERS = ("zfy", "fzy", "fyz", "fzxy", "fyxz", "fzyx")


def forward_kernel(
    group,
    lengths,
    tokens_in,
    qkv_weight,
    out_weight,
    up_weight,
    up_bias_in,
    down_weight,
    down_bias_in,
    attn_gain,
    mlp_gain,
    query_scale,
    cotangent_in,
    x_out,
    normal_out,
    qf_out,
    q_out,
    kt_out,
    kn_out,
    vn_out,
    wq_out,
    lse_out,
    result_out,
    middle_out,
    att_out,
    wo_out,
    acts_out,
    sums,
    ends_out,
    tokens,
    cotangent,
    x_all,
    normal,
    shards,
    w_qkv,
    w_mlp,
    w_pair,
    w_half,
    bias_all,
    bias_row,
    ends_own,
    ends_other,
    query_full,
    query_t,
    key_t,
    value_t,
    key_n,
    value_n,
    logsum,
    attended,
    att_all,
    grad_att,
    grad_middle,
    send_sem,
    recv_sem,
    local_sem,
):
    place = Place(group)
    core, y, quarter, narrow = place.core, place.y, place.quarter, place.narrow
    collector = place.collector
    other_core = jnp.logical_not(collector)
    rows = tokens.shape[0]
    mid = rows // 2
    slab2 = shards.shape[1]
    slab = slab2 // 2
    pair_cols = 2 * shards.shape[2]
    cols_y = part(y, pair_cols)
    cols_other = part(1 - y, pair_cols)
    x_dev, z_dev, far_dev = (
        place.along_narrow(1),
        place.along_narrow(2),
        place.along_narrow(group),
    )
    core_dev, y_dev = place.along_wide(1), place.along_wide(2)
    wires = Wires(send_sem, recv_sem)
    exchange = wires.exchange
    gain_one, gain_two = attn_gain[...].reshape(1, -1), mlp_gain[...].reshape(1, -1)
    down_bias = down_bias_in[...].astype(F32).reshape(1, -1)

    early = [
        pltpu.make_async_copy(source, target, local_sem.at[16 + k])
        for k, (source, target) in enumerate(((tokens_in, tokens), (cotangent_in, cotangent)))
    ]
    for one in early:
        one.start()
    greet(place, group)

    halves = (slice(0, mid), slice(mid, rows))

    def x_part(mask, which):
        return x_all.at[flip(quarter, mask), halves[which]]

    x_first, z_first, on_first, core_first = (
        wires.ids(2),
        wires.ids(2),
        wires.ids(2),
        wires.ids(5),
    )

    def x_own(which):
        return wires.copy(tokens_in.at[halves[which]], x_part(0, which), x_dev, x_first + which)

    def x_in(which):
        return wires.copy(x_part(1, which), x_part(1, which), x_dev, x_first + which)

    def z_own(which):
        return wires.copy(tokens_in.at[halves[which]], x_part(0, which), z_dev, z_first + which)

    def z_in(which):
        return wires.copy(x_part(2, which), x_part(2, which), z_dev, z_first + which)

    def on_out(which):
        return wires.copy(x_part(2, which), x_part(2, which), x_dev, on_first + which)

    def on_in(which):
        return wires.copy(x_part(3, which), x_part(3, which), x_dev, on_first + which)

    def core_copy(index, mask, which=None):
        there = x_all.at[flip(quarter, mask)] if which is None else x_part(mask, which)
        source = tokens_in if mask == 0 else there
        return wires.copy(source, there, core_dev, core_first + index)

    for which in range(2):
        wires.start_if(collector, lambda which=which: x_own(which))
        wires.start_if(other_core, lambda which=which: z_own(which))
    for m in range(3):
        shards[m] = qkv_weight[m]
    shards[3] = out_weight[...]
    shards[4] = up_weight[...]
    shards[5] = down_weight[...]
    w_arrived = exchange(shards.at[:, part(1 - core, slab), :], w_half, w_half, core_dev)
    ends_own[...] = ends_row(lengths, place.half)
    ends_from = exchange(ends_own, ends_other, ends_other, core_dev)
    wires.start_if(collector, lambda: core_copy(0, 0))
    bias_all[narrow] = jnp.broadcast_to(
        up_bias_in[...].astype(F32).reshape(1, -1), bias_all.shape[1:]
    )
    bias_from = [
        exchange(
            bias_all.at[narrow],
            bias_all.at[narrow],
            bias_all.at[flip(narrow, mask)],
            place.along_narrow(mask),
        )
        for mask in range(1, 2 * group)
    ]

    for one in early:
        one.wait()

    @pl.when(collector)
    def _():
        x_all[quarter] = tokens[...]

    w_arrived.wait_recv()
    own = shards[:, part(core, slab), :]
    other = w_half[...]
    w_pair[:, :, : pair_cols // 2] = jnp.where(core == 0, own, other)
    w_pair[:, :, pair_cols // 2 :] = jnp.where(core == 0, other, own)
    for m in range(3):
        w_qkv[m, place.column, :, cols_y] = w_pair[m]
        w_mlp[m, core, part(narrow, slab), cols_y] = w_pair[3 + m]

    masks = {"x": 1, "z": 2, "f": group}
    devices = {"x": x_dev, "z": z_dev, "f": far_dev, "y": y_dev}

    def block(m, mask, columns):
        where = flip(narrow, mask)
        columns = {"own": cols_y, "other": cols_other, "both": slice(None)}[columns]
        if m < 3:
            return w_qkv.at[m, lax.div(where, 2), :, columns]
        return w_mlp.at[m - 3, core, part(where, slab), columns]

    def whole(m, columns):
        if m < 3:
            return w_qkv.at[m, :, :, columns]
        return w_mlp.at[m - 3, core, :, columns]

    held = [{0: "own"} for _ in range(6)]
    gathered = [[] for _ in range(6)]
    turned = {"own": "other", "other": "own", "both": "both"}

    def arrive(m):
        for one in gathered[m]:
            one.wait_recv()
        gathered[m] = []

    def gather(m, stage):
        arrive(m)
        order = GATHER_ORDERS[m]
        if stage == len(order):
            gathered[m] = [
                exchange(
                    w_mlp.at[m - 3, core],
                    w_mlp.at[m - 3, core],
                    w_mlp.at[m - 3, 1 - core],
                    core_dev,
                )
            ]
            return
        way = order[stage]
        device = devices[way]
        if way == "y" and stage == len(order) - 1:
            mine = whole(m, cols_y)
            gathered[m] = [exchange(mine, mine, whole(m, cols_other), device)]
            return
        more = {}
        for mask, columns in held[m].items():
            mine = block(m, mask, columns)
            if way == "y":
                incoming = block(m, mask, turned[columns])
                more[mask] = "both"
            else:
                incoming = block(m, mask ^ masks[way], columns)
                more[mask ^ masks[way]] = columns
            gathered[m].append(exchange(mine, mine, incoming, device))
        held[m].update(more)

    scale = jnp.tile(scale_column(query_scale), (query_t.shape[0], 1))

    def project(mask):
        where = flip(quarter, mask)
        span = part(where, rows)
        inputs = x_all[where].astype(F32)
        normal[where] = (inputs * norm_rows(inputs) * gain_one).astype(LOW)
        weight = w_qkv[...].reshape(-1, inputs.shape[1])
        out = product(weight, normal[where], 1, 1)
        size = out.shape[0] // 3
        heads = size // HEAD_DIM
        query_full[:, span] = out[:size]
        query_t[:, :, span] = (out[:size] * scale).astype(LOW).reshape(heads, HEAD_DIM, rows)
        key = out[size : 2 * size].astype(LOW).reshape(heads, HEAD_DIM, rows)
        value = out[2 * size :].astype(LOW).reshape(heads, HEAD_DIM, rows)
        key_t[:, :, span] = key
        value_t[:, :, span] = value
        for head in range(heads):
            key_n[head, span, :] = key[head].T
            value_n[head, span, :] = value[head].T

    stores = []

    def store(source, target):
        one = pltpu.make_async_copy(source, target, local_sem.at[len(stores)])
        one.start()
        stores.append(one)

    heads = query_t.shape[0]
    att_first = wires.ids(4 * heads)

    def att_send(head, mask):
        peer = flip(quarter, mask)
        return wires.copy(
            attended.at[head, :, part(peer, rows)],
            att_all.at[core, head, place.x],
            place.at(place.z, flip(narrow, mask)),
            att_first + mask * heads + head,
            att_first + (core * 2 + place.x) * heads + head,
        )

    def att_in(head, from_core, from_x):
        there = att_all.at[from_core, head, from_x]
        return wires.copy(there, there, core_dev, att_first + (from_core * 2 + from_x) * heads + head)

    def one_head(head, carry):
        attend_head(head, ends, query_t, key_n, value_t, attended, logsum)
        for mask in (3, 1, 2):
            att_send(head, mask).start()

        @pl.when(collector)
        def _():
            att_all[core, head, place.x] = attended[head, :, part(quarter, rows)]

        pl.when(other_core)(lambda: att_send(head, 0).start())
        return carry

    def pass_on(which):
        wait_if(collector, lambda: z_in(which))
        wires.start_if(collector, lambda: on_out(which))
        wires.start_if(collector, lambda: core_copy(2 + which, 2, which))

    gather(0, 0)
    gather(1, 0)
    gather(2, 0)
    gather(1, 1)
    pass_on(0)
    gather(4, 0)
    gather(4, 1)
    for which in range(2):
        wait_if(collector, lambda which=which: x_in(which))
    wires.start_if(collector, lambda: core_copy(1, 1))
    gather(0, 1)
    pass_on(1)
    gather(2, 1)
    gather(5, 0)
    gather(3, 0)
    gather(1, 2)
    gather(4, 2)
    gather(0, 2)
    gather(5, 1)
    gather(3, 1)
    gather(3, 2)
    gather(5, 2)
    gather(2, 2)
    gather(4, 3)
    ends_from.wait_recv()
    ends_out[...] = jnp.where(collector, ends_own[...], ends_other[...])
    ends = document_ends(ends_out)
    for m in range(3):
        arrive(m)
    gather(3, 3)
    for which in range(2):
        wait_if(collector, lambda which=which: on_in(which))
    wires.start_if(collector, lambda: core_copy(4, 3))
    gather(5, 3)
    wait_if(other_core, lambda: core_copy(0, 0))
    project(0)
    wait_if(other_core, lambda: core_copy(1, 1))
    project(1)
    for which in range(2):
        wait_if(other_core, lambda which=which: core_copy(2 + which, 2, which))
    project(2)
    wait_if(other_core, lambda: core_copy(4, 3))
    project(3)
    store(x_all, x_out)
    store(normal, normal_out)
    store(query_full, qf_out)
    store(query_t, q_out)
    store(key_t, kt_out)
    store(key_n, kn_out)
    store(value_n, vn_out)
    store(w_qkv, wq_out)
    lax.fori_loop(0, 2, one_head, 0)
    gather(3, 4)
    lax.fori_loop(2, 3, one_head, 0)
    gather(4, 4)
    lax.fori_loop(3, heads, one_head, 0)
    store(logsum, lse_out)

    sums[...] = jnp.zeros_like(sums)
    sums[1:2, :] = jnp.sum(cotangent[...].astype(F32), axis=0, keepdims=True)
    for one in bias_from:
        one.wait_recv()
    for c in range(2):
        for n in range(2 * group):
            start = (c * 2 * group + n) * slab
            bias_row[0:1, start : start + slab] = bias_all[n, 0:1, c * slab : (c + 1) * slab]

    def finish_head(head, carry):
        for from_core in range(2):
            for from_x in range(2):
                local = collector & (core == from_core) & (place.x == from_x)
                wait_if(
                    jnp.logical_not(local),
                    lambda from_core=from_core, from_x=from_x: att_in(head, from_core, from_x),
                )
        return carry

    lax.fori_loop(0, heads, finish_head, 0)
    arrive(3)

    size = 2 * w_mlp.shape[2]
    grad_shape = w_mlp.shape[1:]

    def weight(m):
        return w_mlp[m].reshape(size, -1)

    gather(5, 4)
    wires.finish((True,))
    stores[0].wait()
    result, grad_pre, normal_two, hidden = (x_all.at[slot] for slot in range(4))
    att = att_all[...].reshape(size, rows)
    middle = grad_middle
    middle[...] = tokens[...].astype(F32) + product(att, weight(0), 0, 0)
    inverse = norm_rows(middle[...])
    normal_two[...] = (middle[...] * inverse * gain_two).astype(LOW)
    arrive(4)
    pre = product(normal_two[...], weight(1), 1, 1) + bias_row[...]
    gate = 1.0 / (1.0 + jnp.exp(-pre))
    hidden[...] = (pre * gate).astype(LOW)
    slope = gate * (1.0 + pre * (1.0 - gate))
    arrive(5)
    grad_pre[...] = (product(cotangent[...], weight(2), 1, 1) * slope).astype(LOW)
    for slot in range(3):
        store(x_all.at[1 + slot], acts_out.at[slot])
    result[...] = (middle[...] + (product(hidden[...], weight(2)) + down_bias)).astype(LOW)
    store(result, result_out)
    grad_normal = product(grad_pre[...], weight(1))
    normed = middle[...] * inverse
    sums[0:1, :] = jnp.sum(grad_normal * normed, axis=0, keepdims=True)
    scaled = grad_normal * gain_two
    inner = jnp.mean(scaled * normed, axis=1, keepdims=True)
    grad_middle[...] = cotangent[...].astype(F32) + inverse * (scaled - normed * inner)
    store(grad_middle, middle_out)
    branch = grad_middle[...].astype(LOW)
    grad_att[...] = product(weight(0), branch, 1, 1).astype(LOW).reshape(grad_att.shape)
    store(grad_att, att_out)

    def finish_send(head, carry):
        for mask in (1, 2, 3):
            att_send(head, mask).wait_send()
        pl.when(other_core)(lambda: att_send(head, 0).wait_send())
        return carry

    lax.fori_loop(0, heads, finish_send, 0)
    wires.finish()
    w_mlp[0] = product(att, branch).astype(LOW).reshape(grad_shape)
    store(w_mlp.at[0], wo_out)
    sums[2:3, :] = jnp.sum(grad_pre[...].astype(F32), axis=0, keepdims=True)
    for one in stores[1:]:
        one.wait()


def backward_head(
    head,
    ends,
    queries,
    query_full,
    keys,
    keys_t,
    values,
    grad_out,
    logsum,
    scale,
    grads_t,
    sum_keys,
    sum_values,
    sum_scale,
    halfway,
):
    sum_keys[...] = jnp.zeros_like(sum_keys)
    sum_values[...] = jnp.zeros_like(sum_values)

    def first_half(tile):
        offset, starts = tile_keys(tile)
        first, position = first_key(ends, offset)
        span = slice(offset, offset + TILE)
        query, grad, log_row = queries[head, :, span], grad_out[head, :, span], logsum[head, :, span]
        blocks, inner = [], None
        for start in starts:
            scores = product(keys[head, start : start + TILE, :], query)
            scores = allowed_scores(scores, start, offset, first, position)
            probs = jnp.exp(scores - log_row)
            grad_probs = product(values[head, start : start + TILE, :], grad)
            share = jnp.sum(probs * grad_probs, axis=0, keepdims=True)
            inner = share if inner is None else inner + share
            blocks.append((probs, grad_probs))
        return blocks, inner, query, grad

    def second_half(tile, held):
        blocks, inner, query, grad = held
        offset, starts = tile_keys(tile)
        span = slice(offset, offset + TILE)
        grad_scaled = None
        for (probs, grad_probs), start in zip(blocks, starts):
            there = slice(start, start + TILE)
            grad_scores = (probs * (grad_probs - inner)).astype(LOW)
            term = product(keys_t[head, :, there], grad_scores)
            grad_scaled = term if grad_scaled is None else grad_scaled + term
            sum_keys[:, there] += product(query, grad_scores, 1, 1)
            sum_values[:, there] += product(grad, probs.astype(LOW), 1, 1)
        grads_t[0, head, :, span] = (grad_scaled * scale).astype(LOW)
        terms = grad_scaled * query_full[part(head, HEAD_DIM), span]
        sum_scale[...] += terms[:, : TILE // 2] + terms[:, TILE // 2 :]

    count = LEN // TILE
    pipelined(range(count // 2), first_half, second_half)
    halfway()
    pipelined(range(count // 2, count), first_half, second_half)
    grads_t[1, head] = sum_keys[...].astype(LOW)
    grads_t[2, head] = sum_values[...].astype(LOW)


SCATTER_ORDERS = ("yxzf", "zyxf", "xyzf")


def backward_kernel(
    group,
    ends_in,
    query_scale,
    sums,
    grad_own,
    out_grads,
    acts,
    cotangent,
    x_in,
    normal_in,
    query_full_in,
    query_t_in,
    key_t_in,
    key_n_in,
    value_n_in,
    w_qkv_in,
    logsum_in,
    dx_last,
    mlp_out,
    qkv_out,
    sums_out,
    normal,
    query_full,
    query_t,
    key_t,
    key_n,
    value_n,
    logsum,
    grad_att,
    grads_t,
    sum_keys,
    sum_values,
    sum_scale,
    w_own,
    w_core,
    w_y,
    w_eight,
    w_four,
    w_two,
    w_last,
    dx_own,
    dx_core,
    dx_x,
    w_qkv,
    dw,
    dw_y,
    dw_z_in,
    dw_far,
    dw_last,
    all_sums,
    got_sums,
    send_sem,
    recv_sem,
    local_sem,
):
    place = Place(group)
    core, y, quarter, narrow = place.core, place.y, place.quarter, place.narrow
    collector = place.collector
    other_core = jnp.logical_not(collector)
    mid = dx_last.shape[1]
    rows = 2 * mid
    slab = qkv_out.shape[2]
    cols = qkv_out.shape[3]
    pair_cols = 2 * cols
    cols_y = part(y, pair_cols)
    cols_other = part(1 - y, pair_cols)
    x_dev, z_dev, far_dev = (
        place.along_narrow(1),
        place.along_narrow(2),
        place.along_narrow(group),
    )
    core_dev, y_dev = place.along_wide(1), place.along_wide(2)
    wires = Wires(send_sem, recv_sem)
    scale = scale_column(query_scale)
    dxs = w_core

    trade = wires.trade

    act_loads = [
        pltpu.make_async_copy(source, normal.at[slot], local_sem.at[12 + slot])
        for slot, source in enumerate((acts.at[0], acts.at[1], acts.at[2], cotangent))
    ]
    head_loads = [
        pltpu.make_async_copy(source, target, local_sem.at[16 + k])
        for k, (source, target) in enumerate(
            (
                (query_t_in, query_t),
                (key_n_in, key_n),
                (value_n_in, value_n),
                (key_t_in, key_t),
                (logsum_in, logsum),
                (query_full_in, query_full),
            )
        )
    ]
    for one in act_loads + head_loads:
        one.start()
    greet(place, group)

    heads = query_t.shape[0]
    att_first = wires.ids(4 * heads)

    def att_out(head, to_core, to_x):
        target = place.half * group + core * 2 + to_x
        return wires.copy(
            grad_own.at[to_core, head, to_x],
            grad_att.at[head, :, part(quarter, rows)],
            place.at(to_core, target),
            att_first + (to_core * 2 + to_x) * heads + head,
            att_first + quarter * heads + head,
        )

    def att_local(to_core, to_x):
        return collector & (core == to_core) & (place.x == to_x)

    def att_in(head, mask):
        peer = flip(quarter, mask)
        there = grad_att.at[head, :, part(peer, rows)]
        return wires.copy(there, there, core_dev, att_first + peer * heads + head)

    def block_at(index, row):
        low = 1 - lax.div(index, 2)
        high = lax.rem(index + 1, 2) * lax.div(index, 2) + lax.rem(index, 2) * low
        row = jnp.where(low == 1, flip(row, 1), row)
        return jnp.where(high == 1, flip(row, 2), row)

    def head_at(index):
        return block_at(jnp.int32(index), place.column)

    for index in range(heads):
        head = block_at(jnp.int32(index), place.half * 2 + core)
        for to_core in range(2):
            for to_x in range(2):
                pl.when(jnp.logical_not(att_local(to_core, to_x)))(
                    lambda head=head, to_core=to_core, to_x=to_x: att_out(
                        head, to_core, to_x
                    ).start()
                )

    def own_head(head):
        return pltpu.make_async_copy(
            grad_own.at[core, head, place.x],
            grad_att.at[head, :, part(quarter, rows)],
            local_sem.at[22 + head],
        )

    for head in range(heads):
        pl.when(collector)(lambda head=head: own_head(head).start())

    span_m = w_own.shape[1]

    def core_rows(m):
        return slice(m * span_m, (m + 1) * span_m)

    arrived = [None] * 3
    arrived[0] = [trade(lambda: (out_grads.at[1 - core], w_core.at[core_rows(0)], core_dev))]

    def load_own():
        return pltpu.make_async_copy(out_grads.at[core], w_own.at[0], local_sem.at[0])

    def load_normal():
        return pltpu.make_async_copy(normal_in, normal, local_sem.at[3])

    def load_qkv():
        return pltpu.make_async_copy(w_qkv_in, w_qkv, local_sem.at[4])

    load_own().start()

    def give_half(m, left, right, place_for):
        def half(which):
            return product(left[:, part(which, span_m)], right, 0, 0).astype(LOW)

        place_for[0:2] = half(1 - core).reshape((2,) + place_for.shape[1:])
        count = place_for.shape[1]
        arrived[m] = [
            trade(
                lambda k=k: (
                    place_for.at[k // count, k % count],
                    w_core.at[m * span_m + k * slab : m * span_m + (k + 1) * slab],
                    core_dev,
                )
            )
            for k in range(2 * count)
        ]
        w_own[m] = half(core)

    for one in act_loads:
        one.wait()
    first_given = len(wires.sent)
    give_half(1, normal.at[0], normal[1], dw)
    give_half(2, normal.at[2], normal[3], w_qkv)
    given = wires.sent[first_given:]
    del wires.sent[first_given:]
    load_normal().start()

    def given_gone():
        for _, out in given:
            out().wait_send()
        load_qkv().start()
        load_normal().wait()

    masks = {"x": 1, "z": 2, "f": group}
    devices = {"x": x_dev, "z": z_dev, "f": far_dev, "y": y_dev}
    every = tuple(o for o in range(2 * group))
    kept = [every] * 3
    landing = [None] * 3

    def block(m, mask, columns):
        return w_own.at[m, part(flip(narrow, mask), slab), columns]

    def add_to(target, source):
        target[...] = (target[...].astype(F32) + source[...].astype(F32)).astype(LOW)

    def y_rows(m, k):
        start = span_m + (m - 1) * span_m // 2 + k * slab
        return w_y.at[start : start + slab]

    def scatter(m, stage):
        for one in arrived[m]:
            one()
        if stage == 0:
            if m == 0:
                load_own().wait()
            add_rows(w_own.at[m], w_core.at[core_rows(m)], 128)
        elif SCATTER_ORDERS[m][stage - 1] == "y":
            columns = cols_y
            if stage == 1:
                add_rows(w_own.at[m, :, cols_y], w_y.at[:span_m], 128)
            else:
                for k, mask in enumerate(kept[m]):
                    add_to(block(m, mask, cols_y), y_rows(m, k))
        else:
            width = "y" in SCATTER_ORDERS[m][: stage - 1]
            for k, mask in enumerate(kept[m]):
                columns = cols_y if width else slice(None)
                add_to(block(m, mask, columns), landing[m](k))
        if stage == 4:
            total = w_own[m, part(narrow, slab), cols_y].astype(F32)
            arrived[m] = [last_step(total, mlp_out, m, w_last)]
            return
        way = SCATTER_ORDERS[m][stage]
        if way == "y":
            if stage == 0:
                arrived[m] = [
                    trade(lambda: (w_own.at[m, :, cols_other], w_y.at[:span_m], y_dev))
                ]
            else:
                arrived[m] = [
                    trade(
                        lambda k=k, mask=mask: (
                            block(m, mask, cols_other),
                            y_rows(m, k),
                            y_dev,
                        )
                    )
                    for k, mask in enumerate(kept[m])
                ]
            return
        bit = masks[way]
        width = "y" in SCATTER_ORDERS[m][:stage]
        columns = cols_y if width else slice(None)
        mine = tuple(o for o in kept[m] if not o & bit)
        buffers = {8: w_eight, 4: w_four, 2: w_two}
        buffer = buffers[len(kept[m])]

        def land(k, buffer=buffer, width=width):
            if width and buffer is w_eight:
                return buffer.at[m, k, :, : 2 * cols]
            return buffer.at[m, k]

        arrived[m] = [
            trade(lambda k=k, o=o: (block(m, o | bit, columns), land(k), devices[way]))
            for k, o in enumerate(mine)
        ]
        kept[m] = mine
        landing[m] = land

    def last_step(total, out_ref, m, buffer):
        mine = jnp.where(core == 0, total[:, :cols], total[:, cols:])
        theirs = jnp.where(core == 0, total[:, cols:], total[:, :cols])
        out_ref[m, core] = mine
        buffer[m] = theirs
        return trade(lambda: (buffer.at[m], out_ref.at[m, core], core_dev))

    def column_at(mask):
        return lax.div(flip(narrow, mask), 2)

    def dw_add(where, source):
        there = dw.at[:, where, :, cols_y]
        there[...] = (there[...].astype(F32) + source[...].astype(F32)).astype(LOW)

    def weight_grads(head):
        dw[:, head] = (
            product(
                grads_t[:, head].reshape(3 * HEAD_DIM, LEN), normal[...].reshape(LEN, -1)
            )
            .astype(LOW)
            .reshape(3, HEAD_DIM, -1)
        )

    def dw_y_copy(head, slot):
        return wires.copy(
            dw.at[:, head, :, cols_other], dw_y.at[:, head], y_dev, dw_first + slot
        )

    dw_first = wires.ids(heads)

    def dw_z_step():
        return [
            trade(
                lambda k=k, o=o: (dw.at[:, column_at(o), :, cols_y], dw_z_in.at[:, k], z_dev)
            )
            for k, o in enumerate((2, group + 2))
        ]

    def dw_far_step(came):
        came[1]()
        dw_add(column_at(group), dw_z_in.at[:, 1])
        return trade(lambda: (dw.at[:, column_at(group), :, cols_y], dw_far, far_dev))

    def dw_last_step(came, far):
        came[0]()
        dw_add(column_at(0), dw_z_in.at[:, 0])
        far()
        last = []
        for m in range(3):
            total = dw[m, place.column, :, cols_y].astype(F32) + dw_far[m].astype(F32)
            last.append(last_step(total, qkv_out, m, dw_last))
        return last

    ends = document_ends(ends_in)
    sum_scale[...] = jnp.zeros_like(sum_scale)

    steps = {}

    def at_step(step, action):
        steps.setdefault(step, []).append(action)

    came = {}

    def rows_in(slot):
        dw_y_copy(head_at(slot), slot).wait_recv()
        dw_add(head_at(slot), dw_y.at[:, head_at(slot)])

    def rows_on():
        came["dw_z"] = dw_z_step()

    at_step((0, 1), given_gone)
    at_step((0, 0), lambda: scatter(0, 0))
    at_step((1, 0), lambda: scatter(2, 0))
    at_step((1, 0), lambda: scatter(1, 0))
    at_step((3, 0), lambda: scatter(0, 1))
    at_step((3, 0), lambda: rows_in(0))
    at_step((3, 0), lambda: rows_in(1))
    at_step((3, 0), rows_on)

    def between(index, point):
        for (wanted, where), actions in steps.items():
            if where == point:

                @pl.when(index == wanted)
                def _():
                    for action in actions:
                        action()

    def one_head(index, carry):
        head = head_at(index)
        between(index, 0)
        wait_if(other_core, lambda: att_in(head, 0))
        pl.when(collector)(lambda: own_head(head).wait())
        for mask in range(1, group):
            att_in(head, mask).wait_recv()
        backward_head(
            head,
            ends,
            query_t,
            query_full,
            key_n,
            key_t,
            value_n,
            grad_att,
            logsum,
            scale,
            grads_t,
            sum_keys,
            sum_values,
            sum_scale,
            lambda: between(index, 1),
        )

        @pl.when(index < heads - 1)
        def _():
            weight_grads(head)
            dw_y_copy(head, index).start()

        return carry

    for one in head_loads:
        one.wait()
    lax.fori_loop(0, heads, one_head, 0)

    size = 3 * heads * HEAD_DIM
    load_qkv().wait()

    def kept_rows(mask):
        if mask == 0:
            return dx_own
        start = (group + mask - 1) * mid
        return dxs.at[start : start + mid]

    def grad_inputs(mask):
        first = flip(quarter, mask) * 2
        weight = w_qkv[...].reshape(size, -1)

        def half_rows(which):
            span = part(first + which, mid)
            return product(grads_t[:, :, :, span].reshape(size, mid), weight, 0, 0).astype(LOW)

        there = slice(mask * mid, (mask + 1) * mid)
        dxs[there] = half_rows(1 - core)
        out = trade(lambda: (dxs.at[there], dx_core.at[mask], core_dev))
        kept_rows(mask)[...] = half_rows(core)
        return out

    def add_core(mask, came):
        came()
        add_rows(kept_rows(mask), dx_core.at[mask], 128)

    from_core = {}
    last_first = wires.ids(2)

    def last_out():
        return wires.copy(
            kept_rows(2),
            dx_last.at[core],
            place.at(place.z, flip(narrow, 2)),
            last_first,
            last_first + core,
        )

    def last_core():
        return wires.copy(kept_rows(0), dx_last.at[core], core_dev, last_first + 1, last_first + core)

    def last_in(which):
        return wires.copy(dx_last.at[which], dx_last.at[which], core_dev, last_first + which)

    sum_devices = [core_dev, place.along_wide(3)] + [
        (flip(place.wide, 1), flip(narrow, mask)) for mask in (1, 2, group)
    ]

    def sum_step(stage):
        return trade(lambda: (all_sums.at[stage], got_sums.at[stage], sum_devices[stage]))

    def sum_add(stage, came):
        came()
        all_sums[stage + 1] = all_sums[stage] + got_sums[stage]

    from_core[3] = grad_inputs(3)
    scatter(2, 1)
    scatter(0, 2)
    add_core(3, from_core[3])
    from_x3 = trade(lambda: (kept_rows(3), dx_x.at[1], x_dev))
    rows_in(2)
    from_core[2] = grad_inputs(2)
    dw_f = dw_far_step(came["dw_z"])
    from_core[1] = grad_inputs(1)
    from_core[0] = grad_inputs(0)
    add_core(1, from_core[1])
    from_x1 = trade(lambda: (kept_rows(1), dx_x.at[0], x_dev))
    scatter(0, 3)
    scatter(2, 2)
    scatter(1, 1)
    add_core(2, from_core[2])
    add_core(0, from_core[0])
    raw = [
        pltpu.make_async_copy(
            x_in.at[flip(quarter, mask), part(core, mid)], dx_core.at[mask], local_sem.at[6 + mask]
        )
        for mask in range(group)
    ]
    for one in raw:
        one.start()
    weight_grads(head_at(heads - 1))
    dw_y_copy(head_at(heads - 1), heads - 1).start()
    for one in raw:
        one.wait()
    all_sums[0] = sums[...]
    all_sums[0, 3:4, :HEAD_DIM] = jnp.sum(sum_scale[...].T, axis=0, keepdims=True)
    for mask in range(group):

        def gain_rows(span, mask=mask):
            inputs = dx_core[mask, span, :].astype(F32)
            normed = inputs * norm_rows(inputs)
            terms = kept_rows(mask)[span, :].astype(F32) * normed
            all_sums[0, 4:5, :] += jnp.sum(terms, axis=0, keepdims=True)

        chunks(mid, 128, gain_rows)

    from_x3()
    add_rows(kept_rows(2), dx_x.at[1], 128)
    last_out().start()
    wires.sent.append((None, last_out))
    rows_in(3)
    scatter(1, 2)
    sums_now = sum_step(0)
    scatter(2, 3)
    sum_add(0, sums_now)
    sums_now = sum_step(1)
    scatter(0, 4)
    from_x1()
    add_rows(kept_rows(0), dx_x.at[0], 128)
    wires.start_if(other_core, last_core)

    @pl.when(collector)
    def _():
        dx_last[core] = dx_own[...]

    scatter(1, 3)
    sum_add(1, sums_now)
    sums_now = sum_step(2)
    sum_add(2, sums_now)
    sums_now = sum_step(3)
    scatter(2, 4)
    last = dw_last_step(came["dw_z"], dw_f)
    sum_add(3, sums_now)
    sums_now = sum_step(4)
    scatter(1, 4)
    for which in range(2):
        wait_if(
            jnp.logical_not(collector & (core == which)), lambda which=which: last_in(which)
        )

    sum_add(4, sums_now)
    sums_out[...] = all_sums[5]

    for one in last + arrived[0] + arrived[1] + arrived[2]:
        one()
    for slot in range(heads):
        dw_y_copy(head_at(slot), slot).wait_send()

    def finish_send(head, carry):
        for to_core in range(2):
            for to_x in range(2):
                pl.when(jnp.logical_not(att_local(to_core, to_x)))(
                    lambda to_core=to_core, to_x=to_x: att_out(head, to_core, to_x).wait_send()
                )
        return carry

    lax.fori_loop(0, heads, finish_send, 0)
    wires.finish()


def final_kernel(
    tokens, gain, grad_rows, grad_middle, result, mlp_raw, qkv_raw, sums, query_scale,
    tokens_out, result_out, qkv_out, out_out, up_out, down_out,
    up_bias_out, bias_out, attn_out, mlp_out, scale_out,
):
    inputs = tokens[...].astype(F32)
    inverse = norm_rows(inputs)
    normed = inputs * inverse
    scaled = grad_rows[...].astype(F32) * gain[...].reshape(1, -1)
    inner = jnp.mean(scaled * normed, axis=1, keepdims=True)
    tokens_out[...] = grad_middle[...] + inverse * (scaled - normed * inner)
    result_out[...] = result[...]

    @pl.when(pl.program_id(0) == 0)
    def _():
        qkv_out[...] = qkv_raw[...]
        out_out[...] = mlp_raw[0]
        up_out[...] = mlp_raw[1]
        down_out[...] = mlp_raw[2]
        count, slab = sums.shape[1], up_bias_out.shape[0] // 2
        shift = lax.rem(count - slab * lax.axis_index("narrow"), count)
        here = pltpu.roll(sums[...], shift, 1)[2:3]
        both = [here[:, :slab], here[:, count // 2 : count // 2 + slab]]
        up_bias_out[...] = jnp.concatenate(both, axis=1)[0, :]
        mlp_out[...] = sums[0, :]
        bias_out[...] = sums[1, :]
        attn_out[...] = sums[4, :]
        slope = 1.0 / (1.0 + jnp.exp(-query_scale[...].reshape(1, -1)))
        terms = sums[3:4, :HEAD_DIM] * (LOG_TWO_E / math.sqrt(HEAD_DIM)) * slope
        scale_out[...] = terms[0, :]


def struct(shape, dtype):
    return jax.ShapeDtypeStruct(shape, dtype)


def kernel_call(kernel, outputs, in_specs, out_spaces, scratch, collective_id=None):
    extra = {} if collective_id is None else {"collective_id": collective_id, "has_side_effects": True}
    return pl.pallas_call(
        kernel,
        out_shape=tuple(outputs),
        in_specs=[pl.BlockSpec(memory_space=space) for space in in_specs],
        out_specs=tuple(pl.BlockSpec(memory_space=space) for space in out_spaces),
        scratch_shapes=scratch,
        compiler_params=pltpu.CompilerParams(vmem_limit_bytes=VMEM_LIMIT, **extra),
    )


def fused_device(
    group,
    tokens,
    lengths,
    qkv_weight,
    out_weight,
    up_weight,
    up_bias,
    down_weight,
    down_bias,
    attn_gain,
    mlp_gain,
    query_scale,
    cotangent,
):
    rows, dim = tokens.shape
    slab2, cols = out_weight.shape
    slab = slab2 // 2
    halves = lengths.shape[0]
    heads = halves * slab2 // HEAD_DIM
    local = heads * HEAD_DIM
    narrow_count = group * halves
    hidden = slab2 * narrow_count
    vmem, smem, anywhere = pltpu.VMEM, pltpu.SMEM, pl.ANY

    att_shape = (2, heads, 2, HEAD_DIM, rows)
    wq_shape = (3, heads, slab, dim)
    wm_shape = (3, 2, narrow_count * slab, dim)
    dma = pltpu.SemaphoreType.DMA

    forward_outputs = [
        struct((group, rows, dim), LOW),
        struct((group, rows, dim), LOW),
        struct((local, LEN), F32),
        struct((heads, HEAD_DIM, LEN), LOW),
        struct((heads, HEAD_DIM, LEN), LOW),
        struct((heads, LEN, HEAD_DIM), LOW),
        struct((heads, LEN, HEAD_DIM), LOW),
        struct(wq_shape, LOW),
        struct((heads, 1, LEN), F32),
        struct((rows, dim), LOW),
        struct((rows, dim), F32),
        struct(att_shape, LOW),
        struct(wm_shape[1:], LOW),
        struct((3, rows, dim), LOW),
        struct((8, dim), F32),
        struct((8, 128), F32),
    ]
    (
        x_all,
        normal,
        query_full,
        query_t,
        key_t,
        key_n,
        value_n,
        w_qkv,
        logsum,
        result,
        grad_middle,
        grad_att,
        out_grads,
        acts,
        sums,
        ends,
    ) = kernel_call(
        functools.partial(forward_kernel, group),
        forward_outputs,
        [smem, anywhere] + [vmem] * 9 + [anywhere],
        [anywhere] * (len(forward_outputs) - 2) + [vmem] * 2,
        [
            vmem((rows, dim), LOW),
            vmem((rows, dim), LOW),
            vmem((group, rows, dim), LOW),
            vmem((group, rows, dim), LOW),
            vmem((6, slab2, cols), LOW),
            vmem(wq_shape, LOW),
            vmem(wm_shape, LOW),
            vmem((6, slab, 2 * cols), LOW),
            vmem((6, slab, cols), LOW),
            vmem((narrow_count, 8, slab2), F32),
            vmem((1, hidden), F32),
            vmem((8, 128), F32),
            vmem((8, 128), F32),
            vmem((local, LEN), F32),
            vmem((heads, HEAD_DIM, LEN), LOW),
            vmem((heads, HEAD_DIM, LEN), LOW),
            vmem((heads, HEAD_DIM, LEN), LOW),
            vmem((heads, LEN, HEAD_DIM), LOW),
            vmem((heads, LEN, HEAD_DIM), LOW),
            vmem((heads, 1, LEN), F32),
            vmem((heads, HEAD_DIM, LEN), LOW),
            vmem(att_shape, LOW),
            vmem(att_shape, LOW),
            vmem((rows, dim), F32),
            dma((110,)),
            dma((110,)),
            dma((18,)),
        ],
        collective_id=0,
    )(
        lengths,
        tokens,
        jnp.swapaxes(qkv_weight, 1, 2),
        out_weight,
        up_weight.T,
        up_bias,
        down_weight,
        down_bias,
        attn_gain,
        mlp_gain,
        query_scale,
        cotangent,
    )

    last_shape = (3, 2, slab, cols)
    grad_rows, mlp_grads, qkv_grads, totals = kernel_call(
        functools.partial(backward_kernel, group),
        [
            struct((2, rows // 2, dim), LOW),
            struct(last_shape, F32),
            struct(last_shape, F32),
            struct((8, dim), F32),
        ],
        [vmem] * 3 + [anywhere] * 13,
        [vmem] * 4,
        [
            vmem((group, rows, dim), LOW),
            vmem((local, LEN), F32),
            vmem((heads, HEAD_DIM, LEN), LOW),
            vmem((heads, HEAD_DIM, LEN), LOW),
            vmem((heads, LEN, HEAD_DIM), LOW),
            vmem((heads, LEN, HEAD_DIM), LOW),
            vmem((heads, 1, LEN), F32),
            vmem((heads, HEAD_DIM, LEN), LOW),
            vmem((3, heads, HEAD_DIM, LEN), LOW),
            vmem((HEAD_DIM, LEN), F32),
            vmem((HEAD_DIM, LEN), F32),
            vmem((HEAD_DIM, TILE // 2), F32),
            vmem((3, narrow_count * slab, dim), LOW),
            vmem((3 * narrow_count * slab, dim), LOW),
            vmem((2 * narrow_count * slab, 2 * cols), LOW),
            vmem((3, 4, slab, dim), LOW),
            vmem((3, 2, slab, 2 * cols), LOW),
            vmem((3, 1, slab, 2 * cols), LOW),
            vmem((3, slab, cols), F32),
            vmem((rows // 2, dim), LOW),
            vmem((group, rows // 2, dim), LOW),
            vmem((2, rows // 2, dim), LOW),
            vmem(wq_shape, LOW),
            vmem(wq_shape, LOW),
            vmem((3, heads, slab, 2 * cols), LOW),
            vmem((3, 2, slab, 2 * cols), LOW),
            vmem((3, slab, 2 * cols), LOW),
            vmem((3, slab, cols), F32),
            vmem((6, 8, dim), F32),
            vmem((5, 8, dim), F32),
            dma((100,)),
            dma((100,)),
            dma((26,)),
        ],
        collective_id=1,
    )(
        ends,
        query_scale,
        sums,
        grad_att,
        out_grads,
        acts,
        cotangent,
        x_all,
        normal,
        query_full,
        query_t,
        key_t,
        key_n,
        value_n,
        w_qkv,
        logsum,
    )


    def block(*shape):
        return pl.BlockSpec(shape, lambda step: (0,) * len(shape))

    row_block = pl.BlockSpec((rows // 2, dim), lambda step: (step, 0))
    outputs = [
        (row_block, struct((rows, dim), F32)),
        (row_block, struct((rows, dim), LOW)),
        (block(3, slab2, cols), struct((3, slab2, cols), F32)),
    ]
    outputs += [(block(slab2, cols), struct((slab2, cols), F32))] * 3
    outputs += [
        (block(size), struct((size,), F32)) for size in (slab2, dim, dim, dim, HEAD_DIM)
    ]
    (
        grad_tokens,
        result,
        grad_qkv,
        grad_out,
        grad_up,
        grad_down,
        grad_up_bias,
        grad_down_bias,
        grad_attn_gain,
        grad_mlp_gain,
        grad_scale,
    ) = pl.pallas_call(
        final_kernel,
        grid=(2,),
        out_shape=tuple(shape for _, shape in outputs),
        in_specs=[
            row_block,
            block(dim),
            row_block,
            row_block,
            row_block,
            block(3, slab2, cols),
            block(3, slab2, cols),
            block(8, dim),
            block(HEAD_DIM),
        ],
        out_specs=tuple(spec for spec, _ in outputs),
    )(
        tokens,
        attn_gain,
        grad_rows.reshape(rows, dim),
        grad_middle,
        result,
        mlp_grads.reshape(3, slab2, cols),
        qkv_grads.reshape(3, slab2, cols),
        totals,
        query_scale,
    )
    return (
        result,
        grad_tokens,
        jnp.swapaxes(grad_qkv, 1, 2),
        grad_out,
        grad_up.T,
        grad_up_bias,
        grad_down,
        grad_down_bias,
        grad_attn_gain,
        grad_mlp_gain,
        grad_scale,
    )


def solution(mesh):
    wide_count, narrow_count = mesh.shape["wide"], mesh.shape["narrow"]

    def per_device(*args):
        tokens, lengths, out_weight = args[0], args[1], args[3]
        group = LEN // tokens.shape[0]
        fits = (
            wide_count == 4
            and group == 4
            and narrow_count == group * lengths.shape[0] == 8
            and out_weight.shape[0] == 2 * HEAD_DIM
            and 2 * out_weight.shape[1] % 128 == 0
        )
        if fits:
            return fused_device(group, *args)
        return general_device(*args)

    return jax.shard_map(
        per_device,
        mesh=mesh,
        in_specs=(
            P(("wide", "narrow"), None),
            P("wide", None),
            P(None, "wide", "narrow"),
            P("narrow", "wide"),
            P("wide", "narrow"),
            P("narrow"),
            P("narrow", "wide"),
            P(),
            P(),
            P(),
            P(),
            P(("wide", "narrow"), None),
        ),
        out_specs=(
            P(("wide", "narrow"), None),
            P(("wide", "narrow"), None),
            P(None, "wide", "narrow"),
            P("narrow", "wide"),
            P("wide", "narrow"),
            P("narrow"),
            P("narrow", "wide"),
            P(),
            P(),
            P(),
            P(),
        ),
        check_vma=False,
    )
```
